32 devices in a mesh: dp: 4 (over z), expert: 8 (over y, x, core).
Axes of the slice: x: 2, y: 2, z: 4, core: 2. Of those that a mesh axis runs over, the one named last changes fastest.
Arguments:
- tokens: bfloat16 [4096, 2048], P(('dp', 'expert')), may hold values from -6 to 6
- expert_ids: int32 [4096, 4], P(('dp', 'expert')), may hold values from 0 to 7, all different within a row; in each aligned block of 128 rows (0 to 127, 128 to 255, ...) at most 128 rows name the same one
- gates: bfloat16 [4096, 4], P(('dp', 'expert')), may hold values from 0.099609375 to 1
- w_gate: bfloat16 [8, 2048, 384], P('expert'), may hold values from -0.125 to 0.125
- w_up: bfloat16 [8, 2048, 384], P('expert'), may hold values from -0.125 to 0.125
- w_down: bfloat16 [8, 384, 2048], P('expert'), may hold values from -0.3125 to 0.3125
- cotangent: bfloat16 [4096, 2048], P(('dp', 'expert')), may hold values from -6 to 6
Outputs:
- mixed: bfloat16 [4096, 2048], P(('dp', 'expert'))
- grad_tokens: bfloat16 [4096, 2048], P(('dp', 'expert'))
- grad_gate: float32 [8, 2048, 384], P('expert', 'dp')
- grad_up: float32 [8, 2048, 384], P('expert', 'dp')
- grad_down: float32 [8, 384, 2048], P('expert', 'dp')
The draws below stay inside these ranges and needn't reach their ends.
Inputs may be any that keep to these rules, and one draw needn't show every extreme that they name: `expert_ids`: each row names 4 different experts. In each aligned block of 128 rows (the rows of one device) no expert is named by more than 128 rows, a bound that some block reaches.
All inputs are finite; a program needn't handle non-finite values.
Results may differ from the reference program's by a relative error of at most 0.024.
Values may be sent and summed in bfloat16 or wider, within the bound.
No kernel may reach another device: no remote copies, remote signals or barrier semaphores. Data moves between devices by JAX's collectives and lax.ppermute only.
A program may use at most 128 MiB of HBM per device.

```python
import math
import jax
import jax.numpy as jnp
import numpy as np
from jax import lax

D = 2048
HID = 384
TOPK = 4
TOK_DEV = 128
MOST = 128
EXPERTS = 8
TOKENS = 4096
N_DP = 4
N_EXPERT = 8


def with_spikes(entries, key, source, target, shards_of, factor):
    def block_of(axis_at):
        return (jnp.arange(entries.shape[axis_at]) // (entries.shape[axis_at] // shards_of)).reshape((-1,) + (1,) * (entries.ndim - 1 - axis_at))

    one_side = jax.random.permutation(key, shards_of)[block_of(target)]
    second = (block_of(target) + shards_of // 2) % shards_of
    return jnp.where((block_of(source) == one_side) | (block_of(source) == second), factor * entries, entries)


def level_of(key, dims, split, least, top_value):
    def one(position, parts):
        draws = jax.random.uniform(jax.random.fold_in(jax.random.fold_in(key, 6), position), (parts,), jnp.float32, least / len(split), top_value / len(split))
        return jnp.repeat(jnp.exp(draws), dims[position] // parts).reshape((-1,) + (1,) * (len(dims) - position - 1))

    gain = one(*split[0])
    for cut in split[1:]:
        gain = gain * one(*cut)
    return gain


def shared_out(rng, own, number, rows, amount, top, bound, slope):
    sequence = jax.random.permutation(rng, amount)
    heavy_load, common = shares(amount, rows * top, bound, slope, True), shares(amount, rows * top, bound, slope, False)
    places = jnp.arange(amount)

    def named(sizes, turn):
        used = int((sizes > 0).sum())
        fixed = max(1, used // 4)
        passed = fixed + (places - fixed + turn * (used - fixed)) % max(1, amount - fixed)
        return jnp.zeros((amount,), jnp.int32).at[sequence[jnp.where(places < fixed, places, passed)]].set(jnp.asarray(sizes, jnp.int32))

    sizes = jnp.where(number % 4 == 0, named(heavy_load, number // 4), named(common, number - number // 4 - 1))
    mixed = jax.random.permutation(jax.random.fold_in(own, 3), amount)
    donor, taker = mixed[0:amount // 2 * 2:2], mixed[1:amount // 2 * 2:2]
    margin = jnp.minimum(sizes[donor] - 1, bound - sizes[taker]) // 2
    margin = jnp.where((donor == sequence[0]) | (taker == sequence[0]) | (sizes[taker] == 0), 0, jnp.maximum(margin, 0))
    passed = jax.random.randint(jax.random.fold_in(own, 4), (amount // 2,), 0, 1 << 20) % (margin + 1)
    sizes = sizes.at[donor].add(-passed).at[taker].add(passed)
    members = jnp.searchsorted(jnp.cumsum(sizes), jnp.arange(rows * top), side="right").astype(jnp.int32)
    table = members.reshape(top, rows).T
    table = table[jax.random.permutation(jax.random.fold_in(own, 1), rows)]
    turn = jax.random.randint(jax.random.fold_in(own, 2), (rows, 1), 0, top)
    return jnp.take_along_axis(table, (jnp.arange(top)[None, :] + turn) % top, axis=1)


def shares(count, total, limit, slope, full):
    loads = [(1 << 20) // math.isqrt(standing ** slope) + 1 for standing in range(1, count + 1)]
    largest = limit if full else min(limit, max(-(-total // count), total * loads[0] // sum(loads)))
    least = 1 if total - largest >= count - 1 else 0
    counts, rest = [largest] + [least] * (count - 1), total - largest - least * (count - 1)
    while rest > 0:
        free = [i for i in range(1, count) if counts[i] < largest] or [i for i in range(1, count) if counts[i] < limit]
        pool, left = sum([loads[i] for i in free]), rest
        for i in free:
            more = min(limit - counts[i], max(1, left * loads[i] // pool), rest)
            counts[i] = counts[i] + more
            rest = rest - more
    return np.array(counts)


def bell_draw(stream_key, dims, scale, reach, pieces=(), kind=jnp.bfloat16):
    entries = jax.random.normal(stream_key, dims, jnp.float32) * scale
    if len(pieces) > 0:
        entries = level_of(stream_key, dims, pieces, -0.22, 0.18) * entries
    return jnp.clip(entries, min=-reach, max=reach).astype(kind)


def heavy_noise(key, shape, deviation, most, shards, heavy, held_as=jnp.bfloat16):
    values = deviation * jax.random.normal(key, shape, jnp.float32)
    if shards:
        values = values * level_of(key, shape, shards, -0.22, 0.18)
    return jnp.clip(with_spikes(values, jax.random.fold_in(key, 3), *heavy), -most, most).astype(held_as)


def setup_inputs(seed: int = 0) -> dict:
    key_of = jax.random.split(jax.random.key(seed), 8)
    tokens = heavy_noise(key_of[0], (TOKENS, D), 1.0, 6.0, ((0, 32),), (0, 1, 32, 2.75))
    expert_ids_keys = jax.random.split(jax.random.fold_in(key_of[1], 1), TOKENS // TOK_DEV)
    expert_ids_turns = jax.random.permutation(jax.random.fold_in(key_of[1], 3), TOKENS // TOK_DEV)
    expert_ids = jax.vmap(lambda own, number: shared_out(jax.random.fold_in(key_of[1], 2), own, number, TOK_DEV, EXPERTS, TOPK, MOST, 2))(expert_ids_keys, expert_ids_turns).reshape((TOKENS, TOPK))
    gates = jnp.clip(0.099609375 + 0.9003906 * jax.random.uniform(key_of[2], (TOKENS, TOPK), jnp.float32) ** level_of(key_of[2], (TOKENS, TOPK), ((0, 32),), -0.2, 0.2), 0.099609375, 1.0).astype(jnp.bfloat16)
    w_gate = bell_draw(key_of[3], (EXPERTS, D, HID), D ** -0.5, 0.125, ((0, 8),))
    w_up = bell_draw(key_of[4], (EXPERTS, D, HID), D ** -0.5, 0.125, ((0, 8),))
    w_down = bell_draw(key_of[5], (EXPERTS, HID, D), HID ** -0.5, 0.3125, ((0, 8),))
    cotangent = bell_draw(key_of[6], (TOKENS, D), 1.0, 6.0, ((0, 32),))
    return {"tokens": tokens, "expert_ids": expert_ids, "gates": gates, "w_gate": w_gate, "w_up": w_up, "w_down": w_down, "cotangent": cotangent}


def expert_rows(inputs, out_grads, gate_col, gate_panel, up_panel, down_panel):
    pre_gate = jnp.dot(inputs, gate_panel, preferred_element_type=jnp.float32)
    pre_up = jnp.dot(inputs, up_panel, preferred_element_type=jnp.float32)
    gate_sigmoid = jax.nn.sigmoid(pre_gate)
    activated = (pre_gate * gate_sigmoid * pre_up).astype(jnp.bfloat16)
    expert_out = jnp.dot(activated, down_panel, preferred_element_type=jnp.float32)
    contrib = (gate_col.astype(jnp.float32)[:, None] * expert_out).astype(jnp.bfloat16)
    act_grad = lax.dot_general(out_grads, down_panel, (((1,), (1,)), ((), ())), preferred_element_type=jnp.float32)
    up_grad = (act_grad * pre_gate * gate_sigmoid).astype(jnp.bfloat16)
    pre_grad = (act_grad * pre_up * gate_sigmoid * (1.0 + pre_gate * (1.0 - gate_sigmoid))).astype(jnp.bfloat16)
    grad_rows = lax.dot_general(pre_grad, gate_panel, (((1,), (1,)), ((), ())), preferred_element_type=jnp.float32)
    grad_rows = grad_rows + lax.dot_general(up_grad, up_panel, (((1,), (1,)), ((), ())), preferred_element_type=jnp.float32)
    grad_rows = grad_rows.astype(jnp.bfloat16)
    wgrad_gate = lax.dot_general(inputs, pre_grad, (((0,), (0,)), ((), ())), preferred_element_type=jnp.float32)
    wgrad_up = lax.dot_general(inputs, up_grad, (((0,), (0,)), ((), ())), preferred_element_type=jnp.float32)
    wgrad_down = lax.dot_general(activated, out_grads, (((0,), (0,)), ((), ())), preferred_element_type=jnp.float32)
    return contrib, grad_rows, wgrad_gate, wgrad_up, wgrad_down


def reference(tokens, expert_ids, gates, w_gate, w_up, w_down, cotangent):
    pair_total = TOKENS * TOPK
    room_rows = N_DP * N_EXPERT * MOST
    span_rows = math.gcd(1024, room_rows)
    flat_ids = expert_ids.reshape(pair_total)
    flat_gates = gates.reshape(pair_total)
    pair_index = jnp.arange(pair_total, dtype=jnp.int32)

    def per_expert(state_now, expert_num):
        matches = (flat_ids == expert_num).astype(jnp.int32)
        rank_of = jnp.cumsum(matches) - matches
        target = jnp.where(matches == 1, rank_of, room_rows).astype(jnp.int32)
        chosen = jnp.zeros((room_rows,), jnp.int32).at[target].set(pair_index, mode="drop")
        live_count = jnp.sum(matches).astype(jnp.int32)
        gate_panel = w_gate[expert_num]
        up_panel = w_up[expert_num]
        down_panel = w_down[expert_num]

        def block_step(block_index, inner_state):
            mixed_acc, grad_acc, acc_gate, acc_up, acc_down = inner_state
            start_row = (block_index * span_rows).astype(jnp.int32)
            positions = start_row + jnp.arange(span_rows, dtype=jnp.int32)
            pair_ids = lax.dynamic_slice_in_dim(chosen, start_row, span_rows)
            keep_mask = positions < live_count
            row_index = jnp.where(keep_mask, pair_ids // TOPK, 0).astype(jnp.int32)
            keep_b = keep_mask.astype(jnp.bfloat16)
            inputs = tokens[row_index] * keep_b[:, None]
            gate_col = flat_gates[pair_ids] * keep_b
            out_grads = (gate_col.astype(jnp.float32)[:, None] * cotangent[row_index].astype(jnp.float32)).astype(jnp.bfloat16)
            contrib, grad_rows, wgrad_gate, wgrad_up, wgrad_down = expert_rows(inputs, out_grads, gate_col, gate_panel, up_panel, down_panel)
            dest = jnp.where(keep_mask, row_index, TOKENS).astype(jnp.int32)
            mixed_acc = mixed_acc.at[dest].add(contrib.astype(jnp.float32), mode="drop")
            grad_acc = grad_acc.at[dest].add(grad_rows.astype(jnp.float32), mode="drop")
            return mixed_acc, grad_acc, acc_gate + wgrad_gate, acc_up + wgrad_up, acc_down + wgrad_down

        block_total = (live_count + span_rows - 1) // span_rows
        init = (state_now[0], state_now[1], jnp.zeros((D, HID), jnp.float32), jnp.zeros((D, HID), jnp.float32), jnp.zeros((HID, D), jnp.float32))
        mixed_acc, grad_acc, acc_gate, acc_up, acc_down = lax.fori_loop(0, block_total, block_step, init)
        return (mixed_acc, grad_acc), (acc_gate, acc_up, acc_down)

    start = (jnp.zeros((TOKENS, D), jnp.float32), jnp.zeros((TOKENS, D), jnp.float32))
    (mixed_acc, grad_acc), (grad_gate, grad_up, grad_down) = lax.scan(per_expert, start, jnp.arange(EXPERTS, dtype=jnp.int32))
    return mixed_acc.astype(jnp.bfloat16), grad_acc.astype(jnp.bfloat16), grad_gate, grad_up, grad_down
```

```python
import functools

import jax
import jax.numpy as jnp
from jax import lax
from jax.experimental import pallas as pl
from jax.experimental.pallas import tpu as pltpu
from jax.sharding import PartitionSpec as P

F32 = jnp.float32
BF16 = jnp.bfloat16
LANES = 128
CORE, NEAR, FAR = 1, 2, 4
VMEM_BYTES = 48 * 1024 * 1024


def matmul_cost(flops, arrays):
    size = sum(a.size * a.dtype.itemsize for a in arrays)
    return pl.CostEstimate(flops=flops, bytes_accessed=size, transcendentals=0)


def own_gate(gate_rows, expert_num):
    lane = lax.broadcasted_iota(jnp.int32, gate_rows.shape, 1)
    kept = jnp.where(lane == expert_num, gate_rows.astype(F32), 0.0)
    return jnp.sum(kept, axis=1, keepdims=True)


def hidden_kernel(me_ref, tok_a, tok_b, cot_a, cot_b, wg_ref, wu_ref, wd_ref, act_ref, hid_ref, og_ref):
    width = cot_a.shape[1]
    hid = wg_ref.shape[1]
    rows = jnp.concatenate([tok_a[:, :width], tok_b[:, :width]], axis=0)
    gate_col = own_gate(jnp.concatenate([tok_a[:, width:], tok_b[:, width:]], axis=0), me_ref[0])
    cot = jnp.concatenate([cot_a[...], cot_b[...]], axis=0)
    out_grad = (gate_col * cot.astype(F32)).astype(BF16)
    og_ref[...] = out_grad
    pre_gate = jnp.dot(rows, wg_ref[...], preferred_element_type=F32)
    pre_up = jnp.dot(rows, wu_ref[...], preferred_element_type=F32)
    act_grad = lax.dot_general(out_grad, wd_ref[...], (((1,), (1,)), ((), ())), preferred_element_type=F32)
    s = 1.0 / (1.0 + jnp.exp(-pre_gate))
    act_ref[...] = (pre_gate * s * pre_up).astype(BF16)
    hid_ref[:, :hid] = (act_grad * pre_up * s * (1.0 + pre_gate * (1.0 - s))).astype(BF16)
    hid_ref[:, hid:] = (act_grad * pre_gate * s).astype(BF16)


def hidden(me, tok_a, tok_b, cot_a, cot_b, wg, wu, wd):
    rows = 2 * tok_a.shape[0]
    width, hid = wg.shape
    outs = (
        jax.ShapeDtypeStruct((rows, hid), BF16),
        jax.ShapeDtypeStruct((rows, 2 * hid), BF16),
        jax.ShapeDtypeStruct((rows, width), BF16),
    )
    vmem = pl.BlockSpec(memory_space=pltpu.VMEM)
    return pl.pallas_call(
        hidden_kernel,
        out_shape=outs,
        in_specs=[pl.BlockSpec(memory_space=pltpu.SMEM)] + [vmem] * 7,
        out_specs=(vmem,) * 3,
        compiler_params=pltpu.CompilerParams(vmem_limit_bytes=VMEM_BYTES),
        cost_estimate=matmul_cost(6 * rows * width * hid, (tok_a, tok_b, cot_a, cot_b, wg, wu, wd) + outs),
    )(me, tok_a, tok_b, cot_a, cot_b, wg, wu, wd)


def rows_kernel(me_ref, gate_a, gate_b, act_ref, hid_ref, wg_ref, wu_ref, wd_ref, out_a, out_b, grad_a, grad_b):
    half = out_a.shape[0]
    hid = wg_ref.shape[1]
    gate_col = own_gate(jnp.concatenate([gate_a[...], gate_b[...]], axis=0), me_ref[0])
    expert_out = jnp.dot(act_ref[...], wd_ref[...], preferred_element_type=F32)
    contrib = (gate_col * expert_out).astype(BF16)
    out_a[...] = contrib[:half]
    out_b[...] = contrib[half:]
    nt = (((1,), (1,)), ((), ()))
    grad = lax.dot_general(hid_ref[:, :hid], wg_ref[...], nt, preferred_element_type=F32)
    grad = grad + lax.dot_general(hid_ref[:, hid:], wu_ref[...], nt, preferred_element_type=F32)
    grad = grad.astype(BF16)
    grad_a[...] = grad[:half]
    grad_b[...] = grad[half:]


def rows_out(me, tok_a, tok_b, act, hid, wg, wu, wd):
    half = tok_a.shape[0]
    width, hidden_size = wg.shape
    out = jax.ShapeDtypeStruct((half, width), BF16)
    vmem = pl.BlockSpec(memory_space=pltpu.VMEM)
    gate_spec = pl.BlockSpec((half, LANES), lambda i: (0, width // LANES))
    whole = lambda a: pl.BlockSpec(a.shape, lambda i: (0, 0))
    return pl.pallas_call(
        rows_kernel,
        out_shape=(out,) * 4,
        grid=(1,),
        in_specs=[pl.BlockSpec(memory_space=pltpu.SMEM), gate_spec, gate_spec]
        + [whole(a) for a in (act, hid, wg, wu, wd)],
        out_specs=(pl.BlockSpec((half, width), lambda i: (0, 0)),) * 4,
        compiler_params=pltpu.CompilerParams(vmem_limit_bytes=VMEM_BYTES),
        cost_estimate=matmul_cost(12 * half * width * hidden_size, (act, hid, wg, wu, wd) + (out,) * 4),
    )(me, tok_a, tok_b, act, hid, wg, wu, wd)


TN = (((0,), (0,)), ((), ()))


def wide_grad_kernel(blocks, z_ref, *refs):
    toks, hids, out_ref = refs[: 2 * blocks], refs[2 * blocks : 3 * blocks], refs[-1]
    rows = jnp.concatenate([t[...] for t in toks], axis=0)
    hids = jnp.concatenate([h[...] for h in hids], axis=0)
    out_ref[0] = lax.dot_general(rows, hids, TN, preferred_element_type=F32).astype(BF16)


def wide_grads(z, toks, hids, width, shards, picks):
    blocks = len(hids)
    tile = min(512, width // shards)
    parts = width // shards // tile
    both = hids[0].shape[1]
    first, stride = picks[0], (picks[1] - picks[0]) if len(picks) > 1 else 0
    tok_map = lambda i, j, z: (0, lax.rem(z[0] + first + i * stride, shards) * parts + j)
    return pl.pallas_call(
        functools.partial(wide_grad_kernel, blocks),
        out_shape=jax.ShapeDtypeStruct((len(picks), width // shards, both), BF16),
        grid_spec=pltpu.PrefetchScalarGridSpec(
            num_scalar_prefetch=1,
            grid=(len(picks), parts),
            in_specs=[pl.BlockSpec((t.shape[0], tile), tok_map) for t in toks]
            + [pl.BlockSpec(h.shape, lambda i, j, z: (0, 0)) for h in hids],
            out_specs=pl.BlockSpec((1, tile, both), lambda i, j, z: (i, j, 0)),
        ),
        compiler_params=pltpu.CompilerParams(vmem_limit_bytes=VMEM_BYTES),
        cost_estimate=pl.CostEstimate(
            flops=2 * len(picks) * blocks * hids[0].shape[0] * both * width // shards,
            bytes_accessed=8 * 1024 * 1024 // 2,
            transcendentals=0,
        ),
    )(z, *toks, *hids)


def down_grad_kernel(blocks, shards, z_ref, *refs):
    acts, ogs = refs[:blocks], refs[blocks : 2 * blocks]
    out_ref, full = refs[-2], refs[-1]
    act = jnp.concatenate([a[...] for a in acts], axis=0)
    og = jnp.concatenate([o[...] for o in ogs], axis=0)
    full[...] = lax.dot_general(act, og, TN, preferred_element_type=F32)
    size = full.shape[0] // shards
    for k in range(shards):
        at = pl.multiple_of(lax.rem(z_ref[0] + k, shards) * size, size)
        out_ref[k] = full[pl.ds(at, size), :].astype(BF16)


def down_grads(z, acts, ogs, shards):
    blocks = len(acts)
    rows, hid = acts[0].shape
    width = ogs[0].shape[1]
    tile = 512
    return pl.pallas_call(
        functools.partial(down_grad_kernel, blocks, shards),
        out_shape=jax.ShapeDtypeStruct((shards, hid // shards, width), BF16),
        grid_spec=pltpu.PrefetchScalarGridSpec(
            num_scalar_prefetch=1,
            grid=(width // tile,),
            in_specs=[pl.BlockSpec((rows, hid), lambda i, z: (0, 0)) for _ in acts]
            + [pl.BlockSpec((rows, tile), lambda i, z: (0, i)) for _ in ogs],
            out_specs=pl.BlockSpec((shards, hid // shards, tile), lambda i, z: (0, 0, i)),
            scratch_shapes=[pltpu.VMEM((hid, tile), F32)],
        ),
        compiler_params=pltpu.CompilerParams(vmem_limit_bytes=VMEM_BYTES),
        cost_estimate=matmul_cost(2 * blocks * rows * hid * width, tuple(acts) + tuple(ogs)),
    )(z, *acts, *ogs)


def line_sum(parts, axis, size):
    add = lambda a, b: a if b is None else (a.astype(F32) + b.astype(F32)).astype(BF16)
    right, left = None, None
    for step in range(1, size):
        up = [(i, i + 1) for i in range(step)]
        down = [(size - 1 - i, size - 2 - i) for i in range(step)]
        right = lax.ppermute(add(parts[size - step], right), axis, up)
        left = lax.ppermute(add(parts[step], left), axis, down)
    total = parts[0].astype(F32)
    for other in (right, left):
        if other is not None:
            total = total + other.astype(F32)
    return total


def add_rows(a, b):
    return (a.astype(F32) + b.astype(F32)).astype(BF16)


def per_device(tokens, expert_ids, gates, w_gate, w_up, w_down, cotangent):
    width = tokens.shape[1]
    group = lax.axis_size("expert")
    shards = lax.axis_size("dp")
    assert group == 8
    me = lax.axis_index("expert").astype(jnp.int32).reshape(1)
    z = lax.axis_index("dp").astype(jnp.int32).reshape(1)
    wg, wu, wd = w_gate[0], w_up[0], w_down[0]

    def flip(array, bit):
        return lax.ppermute(array, "expert", [(i, i ^ bit) for i in range(group)])

    lanes = jnp.arange(LANES, dtype=jnp.int32)[None, None, :]
    spread = jnp.where(expert_ids[:, :, None] == lanes, gates.astype(F32)[:, :, None], 0.0)
    tok0 = jnp.concatenate([tokens, jnp.sum(spread, axis=1).astype(BF16)], axis=1)
    cot0 = cotangent

    cot_y = flip(cot0, FAR)
    tok_x = flip(tok0, NEAR)
    cot_x = flip(cot0, NEAR)
    tok_y = flip(tok0, FAR)
    tok_d = flip(tok_x, FAR)
    cot_d = flip(cot_y, NEAR)
    toks, hids, acts, ogs, outs, grads = [], [], [], [], [], []
    for tok, cot in ((tok0, cot0), (tok_x, cot_x), (tok_y, cot_y), (tok_d, cot_d)):
        tok_s, cot_s = flip(tok, CORE), flip(cot, CORE)
        act, hid, og = hidden(me, tok, tok_s, cot, cot_s, wg, wu, wd)
        toks += [tok, tok_s]
        hids.append(hid)
        acts.append(act)
        ogs.append(og)

    chain = shards <= 4
    if chain:
        pieces = shards
        wide_far = wide_grads(z, toks, hids, width, pieces, (3, 1)) if shards == 4 else None
    if chain and shards == 4:
        down = down_grads(z, acts, ogs, 4)
        wide_near = wide_grads(z, toks, hids, width, 4, (2, 0))
        grad_wide = line_sum([wide_near[1], wide_far[1], wide_near[0], wide_far[0]], "dp", 4)
        grad_down = line_sum([down[k] for k in range(4)], "dp", 4)
    else:
        zero = jnp.zeros_like(z)
        wide = wide_grads(zero, toks, hids, width, 1, (0,))[0]
        down = down_grads(zero, acts, ogs, 1)[0]
        grad_wide = lax.psum_scatter(wide, "dp", scatter_dimension=0, tiled=True).astype(F32)
        grad_down = lax.psum_scatter(down, "dp", scatter_dimension=0, tiled=True).astype(F32)

    for i in range(4):
        out_m, out_s, grad_m, grad_s = rows_out(me, toks[2 * i], toks[2 * i + 1], acts[i], hids[i], wg, wu, wd)
        outs.append(add_rows(out_m, flip(out_s, CORE)))
        grads.append(add_rows(grad_m, flip(grad_s, CORE)))
    out_0, out_x, out_y, out_d = outs
    grad_0, grad_x, grad_y, grad_d = grads
    out_y = add_rows(out_y, flip(out_d, NEAR))
    grad_x = add_rows(grad_x, flip(grad_d, FAR))
    mixed = out_0.astype(F32) + flip(out_x, NEAR).astype(F32) + flip(out_y, FAR).astype(F32)
    grad_tokens = grad_0.astype(F32) + flip(grad_y, FAR).astype(F32) + flip(grad_x, NEAR).astype(F32)
    hid_size = wg.shape[1]
    return (
        mixed.astype(BF16),
        grad_tokens.astype(BF16),
        grad_wide[None, :, :hid_size],
        grad_wide[None, :, hid_size:],
        grad_down[None],
    )


def solution(mesh):
    return jax.shard_map(
        per_device,
        mesh=mesh,
        in_specs=(
            P(("dp", "expert"), None),
            P(("dp", "expert"), None),
            P(("dp", "expert"), None),
            P("expert", None, None),
            P("expert", None, None),
            P("expert", None, None),
            P(("dp", "expert"), None),
        ),
        out_specs=(
            P(("dp", "expert"), None),
            P(("dp", "expert"), None),
            P("expert", "dp", None),
            P("expert", "dp", None),
            P("expert", "dp", None),
        ),
        check_vma=False,
    )
```

```python
import functools

import jax
import jax.numpy as jnp
from jax import lax
from jax.experimental import pallas as pl
from jax.experimental.pallas import tpu as pltpu
from jax.sharding import PartitionSpec as P

F32 = jnp.float32
BF16 = jnp.bfloat16
LANES = 128
CORE, NEAR, FAR = 1, 2, 4
PARAMS = pltpu.CompilerParams(vmem_limit_bytes=60 * 1024 * 1024)
ANY = pl.BlockSpec(memory_space=pl.ANY)
SMEM = pl.BlockSpec(memory_space=pltpu.SMEM)
NT = (((1,), (1,)), ((), ()))


def cost(flops, arrays):
    size = sum(a.size * a.dtype.itemsize for a in arrays)
    return pl.CostEstimate(flops=flops // 64, bytes_accessed=size // 64, transcendentals=0)


def own_gate(gate_rows, expert_num):
    lane = lax.broadcasted_iota(jnp.int32, gate_rows.shape, 1)
    kept = jnp.where(lane == expert_num, gate_rows.astype(F32), 0.0)
    return jnp.sum(kept, axis=1, keepdims=True)


def hidden_kernel(blocks, *refs):
    me_ref = refs[0]
    toks, cots = refs[1 : 1 + blocks], refs[1 + blocks : 1 + 2 * blocks]
    wg_hbm, wu_hbm, wd_hbm = refs[1 + 2 * blocks : 4 + 2 * blocks]
    act_ref, hid_ref, act_t_ref, hid_t_ref, og_hbm = refs[4 + 2 * blocks : 9 + 2 * blocks]
    rows, gates, cot, wide, down, og, sems = refs[9 + 2 * blocks :]
    each, width = cots[0].shape
    hid = wg_hbm.shape[1]

    def copy(source, target, number):
        made = pltpu.make_async_copy(source, target, sems.at[number])
        made.start()
        return made

    first = [copy(wg_hbm, wide.at[:, :hid], 0), copy(wu_hbm, wide.at[:, hid:], 1)]
    for i in range(blocks):
        at = pl.ds(i * each, each)
        first.append(copy(toks[i].at[:, :width], rows.at[at, :], 3 + 3 * i))
    second = []
    for i in range(blocks):
        at = pl.ds(i * each, each)
        second.append(copy(toks[i].at[:, width:], gates.at[at, :], 4 + 3 * i))
        second.append(copy(cots[i], cot.at[at, :], 5 + 3 * i))
    second.append(copy(wd_hbm, down, 2))
    for made in first:
        made.wait()
    pre = jnp.dot(rows[...], wide[...], preferred_element_type=F32)
    for made in second:
        made.wait()
    og[...] = (own_gate(gates[...], me_ref[0]) * cot[...].astype(F32)).astype(BF16)
    out = pltpu.make_async_copy(og, og_hbm, sems.at[0])
    out.start()
    act_grad = lax.dot_general(og[...], down[...], NT, preferred_element_type=F32)
    pre_gate, pre_up = pre[:, :hid], pre[:, hid:]
    s = 1.0 / (1.0 + jnp.exp(-pre_gate))
    act = (pre_gate * s * pre_up).astype(BF16)
    pre_grad = (act_grad * pre_up * s * (1.0 + pre_gate * (1.0 - s))).astype(BF16)
    up_grad = (act_grad * pre_gate * s).astype(BF16)
    act_ref[...] = act
    act_t_ref[...] = act.T
    hid_ref[:, :hid] = pre_grad
    hid_ref[:, hid:] = up_grad
    hid_t_ref[:hid, :] = pre_grad.T
    hid_t_ref[hid:, :] = up_grad.T
    out.wait()


def hidden(me, toks, cots, wg, wu, wd):
    blocks = len(toks)
    each = cots[0].shape[0]
    rows = blocks * each
    width, hid = wg.shape
    shapes = [(rows, hid), (rows, 2 * hid), (hid, rows), (2 * hid, rows)]
    outs = tuple(jax.ShapeDtypeStruct(s, BF16) for s in shapes + [(rows, width)])
    specs = tuple(pl.BlockSpec(s, lambda i: (0, 0)) for s in shapes) + (ANY,)
    return pl.pallas_call(
        functools.partial(hidden_kernel, blocks),
        out_shape=outs,
        grid=(1,),
        in_specs=[SMEM] + [ANY] * (2 * blocks + 3),
        out_specs=specs,
        scratch_shapes=[
            pltpu.VMEM((rows, width), BF16),
            pltpu.VMEM((rows, LANES), BF16),
            pltpu.VMEM((rows, width), BF16),
            pltpu.VMEM((width, 2 * hid), BF16),
            pltpu.VMEM((hid, width), BF16),
            pltpu.VMEM((rows, width), BF16),
            pltpu.SemaphoreType.DMA((3 + 3 * blocks,)),
        ],
        compiler_params=PARAMS,
        cost_estimate=cost(6 * rows * width * hid, (*toks, *cots, wg, wu, wd) + outs),
    )(me, *toks, *cots, wg, wu, wd)


def rows_kernel(blocks, more, *refs):
    me_ref, gates, refs = refs[0], refs[1 : 1 + blocks], refs[1 + blocks :]
    act_ref, hid_ref, wg_hbm, wu_hbm, wd_hbm = refs[:5]
    added = refs[5 : 5 + more]
    outs, (wide, down, sems) = refs[5 + more : -3], refs[-3:]
    hid = wg_hbm.shape[1]
    copies = [
        pltpu.make_async_copy(wd_hbm, down, sems.at[0]),
        pltpu.make_async_copy(wg_hbm, wide.at[:, :hid], sems.at[1]),
        pltpu.make_async_copy(wu_hbm, wide.at[:, hid:], sems.at[2]),
    ]
    for made in copies:
        made.start()
    gate_col = own_gate(jnp.concatenate([g[...] for g in gates], axis=0), me_ref[0])
    half = len(outs) // 2

    def put(values, number):
        if more:
            values = values.astype(F32) + added[number][...].astype(F32)
        values = values.astype(BF16)
        each = values.shape[0] // half
        for i in range(half):
            outs[number * half + i][...] = values[i * each : (i + 1) * each]

    copies[0].wait()
    expert_out = jnp.dot(act_ref[...], down[...], preferred_element_type=F32)
    put((gate_col * expert_out).astype(BF16), 0)
    copies[1].wait()
    copies[2].wait()
    grad = lax.dot_general(hid_ref[...], wide[...], NT, preferred_element_type=F32)
    put(grad.astype(BF16), 1)


def rows_out(me, gate_arrays, act, hid, part, parts, wg, wu, wd, added, split):
    blocks = len(gate_arrays)
    each = gate_arrays[0].shape[0]
    rows = blocks * each
    assert rows * parts == act.shape[0]
    width, hidden_size = wg.shape
    out = jax.ShapeDtypeStruct((rows // split, width), BF16)
    gate_spec = pl.BlockSpec((each, LANES), lambda i: (0, width // LANES))
    return pl.pallas_call(
        functools.partial(rows_kernel, blocks, len(added)),
        out_shape=(out,) * (2 * split),
        grid=(1,),
        in_specs=[SMEM]
        + [gate_spec] * blocks
        + [pl.BlockSpec((rows, a.shape[1]), lambda i: (part, 0)) for a in (act, hid)]
        + [ANY] * 3
        + [pl.BlockSpec(a.shape, lambda i: (0, 0)) for a in added],
        out_specs=(pl.BlockSpec(out.shape, lambda i: (0, 0)),) * (2 * split),
        scratch_shapes=[
            pltpu.VMEM((width, 2 * hidden_size), BF16),
            pltpu.VMEM((hidden_size, width), BF16),
            pltpu.SemaphoreType.DMA((3,)),
        ],
        compiler_params=PARAMS,
        cost_estimate=cost(6 * rows * width * hidden_size, (wg, wu, wd) + tuple(added) + (out,) * (2 * split)),
    )(me, *gate_arrays, act, hid, wg, wu, wd, *added)


def wide_grad_kernel(groups, first, count, order_ref, *refs):
    blocks = sum(groups)
    toks, hids, outs = refs[:blocks], refs[blocks : blocks + len(groups)], refs[blocks + len(groups) :]
    total, at = None, 0
    for hid_ref, size in zip(hids, groups):
        rows = jnp.concatenate([t[...] for t in toks[at : at + size]], axis=0)
        part = jnp.dot(hid_ref[...], rows, preferred_element_type=F32)
        total = part if total is None else total + part
        at += size
    total = total.astype(BF16)
    for k in range(count):

        @pl.when(pl.program_id(0) == k)
        def _():
            outs[k][...] = total


def wide_grads(order, toks, hids, width, first, count):
    blocks = len(toks)
    each = toks[0].shape[0]
    groups = tuple(h.shape[1] // each for h in hids)
    both, tile = hids[0].shape[0], width // 4
    out = jax.ShapeDtypeStruct((both, tile), BF16)
    return pl.pallas_call(
        functools.partial(wide_grad_kernel, groups, first, count),
        out_shape=(out,) * count,
        grid_spec=pltpu.PrefetchScalarGridSpec(
            num_scalar_prefetch=1,
            grid=(count,),
            in_specs=[pl.BlockSpec((each, tile), lambda i, order: (0, order[first + i]))] * blocks
            + [pl.BlockSpec(h.shape, lambda i, order: (0, 0)) for h in hids],
            out_specs=(pl.BlockSpec(out.shape, lambda i, order: (0, 0)),) * count,
        ),
        compiler_params=PARAMS,
        cost_estimate=cost(2 * count * blocks * each * both * tile, tuple(hids) + (out,) * count),
    )(order, *toks, *hids)


def down_grad_kernel(groups, order_ref, *refs):
    acts, ogs, outs, full = refs[:groups], refs[groups : 2 * groups], refs[2 * groups : -1], refs[-1]
    total = None
    for act, og in zip(acts, ogs):
        part = jnp.dot(act[...], og[...], preferred_element_type=F32)
        total = part if total is None else total + part
    full[...] = total
    size = full.shape[0] // 4
    for k in range(4):
        at = pl.multiple_of(order_ref[k] * size, size)
        outs[k][...] = full[pl.ds(at, size), :].astype(BF16)


def down_grads(order, acts, ogs):
    hid = acts[0].shape[0]
    rows = sum(a.shape[1] for a in acts)
    width = ogs[0].shape[1]
    tile = width // 4
    out = jax.ShapeDtypeStruct((hid // 4, width), BF16)
    return pl.pallas_call(
        functools.partial(down_grad_kernel, len(acts)),
        out_shape=(out,) * 4,
        grid_spec=pltpu.PrefetchScalarGridSpec(
            num_scalar_prefetch=1,
            grid=(width // tile,),
            in_specs=[pl.BlockSpec(a.shape, lambda i, order: (0, 0)) for a in acts]
            + [pl.BlockSpec((o.shape[0], tile), lambda i, order: (0, i)) for o in ogs],
            out_specs=(pl.BlockSpec((hid // 4, tile), lambda i, order: (0, i)),) * 4,
            scratch_shapes=[pltpu.VMEM((hid, tile), F32)],
        ),
        compiler_params=PARAMS,
        cost_estimate=cost(2 * rows * hid * width, tuple(acts) + tuple(ogs)),
    )(order, *acts, *ogs)


def turn_kernel(mid_ref, own, a1, a2, a3, a4, gate_ref, up_ref):
    ends = a1[...].astype(F32) + a2[...].astype(F32)
    total = own[...].astype(F32) + (a3[...].astype(F32) + a4[...].astype(F32))
    total = (total + jnp.where(mid_ref[0] == 1, 0.0, ends)).T
    hid = gate_ref.shape[1]
    gate_ref[...] = total[:, :hid]
    up_ref[...] = total[:, hid:]


def turn(mid, terms):
    both, tile = terms[0].shape
    out = jax.ShapeDtypeStruct((tile, both // 2), F32)
    return pl.pallas_call(
        turn_kernel,
        out_shape=(out, out),
        grid=(tile // LANES,),
        in_specs=[SMEM] + [pl.BlockSpec((both, LANES), lambda i: (0, i))] * 5,
        out_specs=(pl.BlockSpec((LANES, both // 2), lambda i: (i, 0)),) * 2,
        compiler_params=PARAMS,
        cost_estimate=cost(5 * both * tile, terms + (out, out)),
    )(mid, *terms)


def after(values, earlier):
    return lax.optimization_barrier((values, earlier))[0]


def add(a, b):
    return (a.astype(F32) + b.astype(F32)).astype(BF16)


def line_terms(parts, mid):
    move = lambda a, pairs: lax.ppermute(a, "dp", pairs)
    one = move(parts[0], [(0, 1), (1, 0), (2, 3), (3, 2)])
    two = move(add(parts[1], jnp.where(mid, one, jnp.zeros_like(one))), [(0, 1), (1, 3), (3, 2), (2, 0)])
    three = move(parts[2], [(0, 1), (3, 2)])
    four = move(add(parts[2], two), [(1, 2), (2, 1)])
    return (parts[3], one, two, three, four)


LINE_ORDER = ((3, 2, 1, 0), (0, 3, 2, 1), (3, 0, 1, 2), (0, 1, 2, 3))


def per_device(tokens, expert_ids, gates, w_gate, w_up, w_down, cotangent):
    width = tokens.shape[1]
    group = lax.axis_size("expert")
    shards = lax.axis_size("dp")
    assert group == 8
    me = lax.axis_index("expert").astype(jnp.int32).reshape(1)
    z = lax.axis_index("dp")
    wg, wu, wd = w_gate[0], w_up[0], w_down[0]

    def flip(array, bit):
        return lax.ppermute(array, "expert", [(i, i ^ bit) for i in range(group)])

    cot_0 = cotangent
    cot_y = flip(cot_0, FAR)
    cot_x = flip(cot_0, NEAR)
    lanes = jnp.arange(LANES, dtype=jnp.int32)[None, None, :]
    spread = jnp.where(expert_ids[:, :, None] == lanes, gates.astype(F32)[:, :, None], 0.0)
    tok_0 = jnp.concatenate([tokens, jnp.sum(spread, axis=1).astype(BF16)], axis=1)
    tok_x = flip(tok_0, NEAR)
    tok_y = flip(tok_0, FAR)
    cot_d = flip(cot_y, NEAR)
    tok_d = flip(tok_x, FAR)

    toks_a, cots_a = [tok_0, tok_x, tok_y], [cot_0, cot_x, cot_y]
    toks_a += [flip(t, CORE) for t in toks_a]
    cots_a += [flip(c, CORE) for c in cots_a]
    toks_b, cots_b = [tok_d, flip(tok_d, CORE)], [cot_d, flip(cot_d, CORE)]
    act_a, hid_a, act_t_a, hid_t_a, og_a = hidden(me, toks_a, cots_a, wg, wu, wd)
    act_b, hid_b, act_t_b, hid_t_b, og_b = hidden(me, toks_b, cots_b, wg, wu, wd)

    line = shards == 4
    table = jnp.asarray(LINE_ORDER if line else ((0, 1, 2, 3),), jnp.int32)
    order = table[z if line else 0]
    toks = toks_a + toks_b
    wide = wide_grads(order, toks, (hid_t_a, hid_t_b), width, 0, 1)
    act_t_a, act_b = after((act_t_a, act_b), wide[0])
    down = down_grads(order, (act_t_a, act_t_b), (og_a, og_b))
    act_b, hid_t_a = after((act_b, hid_t_a), down[0])
    out_s, grad_s = rows_out(me, toks_b[1:], act_b, hid_b, 1, 2, wg, wu, wd, (), 1)
    hid_t_a = after(hid_t_a, out_s)
    wide = wide + wide_grads(order, toks, (hid_t_a, hid_t_b), width, 1, 3)
    added = after((flip(out_s, CORE), flip(grad_s, CORE)), wide[1])
    out_d, grad_d = rows_out(me, toks_b[:1], act_b, hid_b, 0, 2, wg, wu, wd, added, 1)
    act_a = after(act_a, out_d)
    hid_size = wg.shape[1]
    if line:
        mid = (z == 1) | (z == 2)
        wide_terms = line_terms(wide, mid)
        down_terms = line_terms(down, mid)
        grad_gate, grad_up = turn(mid.astype(jnp.int32).reshape(1), wide_terms)
        own, one, two, three, four = (t.astype(F32) for t in down_terms)
        grad_down = own + (three + four) + jnp.where(mid, 0.0, one + two)
    else:
        wide_all = jnp.concatenate(wide, axis=1).T
        grad_wide = lax.psum_scatter(wide_all, "dp", scatter_dimension=0, tiled=True).astype(F32)
        grad_gate, grad_up = grad_wide[:, :hid_size], grad_wide[:, hid_size:]
        grad_down = lax.psum_scatter(jnp.concatenate(down, axis=0), "dp", scatter_dimension=0, tiled=True).astype(F32)

    out_s, grad_s = rows_out(me, toks_a[3:], act_a, hid_a, 1, 2, wg, wu, wd, (), 1)
    out_0, out_x, out_y, grad_0, grad_x, grad_y = rows_out(
        me, toks_a[:3], act_a, hid_a, 0, 2, wg, wu, wd, (flip(out_s, CORE), flip(grad_s, CORE)), 3
    )
    out_y = add(out_y, flip(out_d, NEAR))
    grad_x = add(grad_x, flip(grad_d, FAR))
    mixed = out_0.astype(F32) + flip(out_x, NEAR).astype(F32) + flip(out_y, FAR).astype(F32)
    grad_tokens = grad_0.astype(F32) + flip(grad_y, FAR).astype(F32) + flip(grad_x, NEAR).astype(F32)
    return (mixed.astype(BF16), grad_tokens.astype(BF16), grad_gate[None], grad_up[None], grad_down[None])


def solution(mesh):
    return jax.shard_map(
        per_device,
        mesh=mesh,
        in_specs=(
            P(("dp", "expert"), None),
            P(("dp", "expert"), None),
            P(("dp", "expert"), None),
            P("expert", None, None),
            P("expert", None, None),
            P("expert", None, None),
            P(("dp", "expert"), None),
        ),
        out_specs=(
            P(("dp", "expert"), None),
            P(("dp", "expert"), None),
            P("expert", "dp", None),
            P("expert", "dp", None),
            P("expert", "dp", None),
        ),
        check_vma=False,
    )
```

```python
import functools

import jax
import jax.numpy as jnp
from jax import lax
from jax.experimental import pallas as pl
from jax.experimental.pallas import tpu as pltpu
from jax.sharding import PartitionSpec as P

F32 = jnp.float32
BF16 = jnp.bfloat16
LANES = 128
CORE, NEAR, FAR = 1, 2, 4
PARAMS = pltpu.CompilerParams(vmem_limit_bytes=60 * 1024 * 1024)
ANY = pl.BlockSpec(memory_space=pl.ANY)
SMEM = pl.BlockSpec(memory_space=pltpu.SMEM)
NT = (((1,), (1,)), ((), ()))


def cost(flops, arrays):
    size = sum(a.size * a.dtype.itemsize for a in arrays)
    return pl.CostEstimate(flops=flops // 64, bytes_accessed=size // 64, transcendentals=0)


def own_gate(gate_rows, expert_num):
    lane = lax.broadcasted_iota(jnp.int32, gate_rows.shape, 1)
    kept = jnp.where(lane == expert_num, gate_rows.astype(F32), 0.0)
    return jnp.sum(kept, axis=1, keepdims=True)


def transpose_kernel(wg_ref, wu_ref, out_ref):
    hid = wg_ref.shape[1]
    out_ref[:hid, :] = wg_ref[...].T
    out_ref[hid:, :] = wu_ref[...].T


def transposed(wg, wu):
    width, hid = wg.shape
    tile = width // 4
    return pl.pallas_call(
        transpose_kernel,
        out_shape=jax.ShapeDtypeStruct((2 * hid, width), BF16),
        grid=(4,),
        in_specs=[pl.BlockSpec((tile, hid), lambda i: (i, 0))] * 2,
        out_specs=pl.BlockSpec((2 * hid, tile), lambda i: (0, i)),
        compiler_params=PARAMS,
        cost_estimate=cost(width, (wg,)),
    )(wg, wu)


def hidden_kernel(blocks, *refs):
    me_ref, gates_ref = refs[:2]
    toks, cots = refs[2 : 2 + blocks], refs[2 + blocks : 2 + 2 * blocks]
    wt_hbm, wd_hbm = refs[2 + 2 * blocks : 4 + 2 * blocks]
    act_ref, hid_ref, act_t_ref, hid_t_ref, og_hbm = refs[4 + 2 * blocks : 9 + 2 * blocks]
    rows, cot, wide, down, og, sems = refs[9 + 2 * blocks :]
    each = cots[0].shape[0]
    hid = wd_hbm.shape[0]

    def copy(source, target, number):
        made = pltpu.make_async_copy(source, target, sems.at[number])
        made.start()
        return made

    first = [copy(wt_hbm, wide, 0)]
    for i in range(blocks):
        first.append(copy(toks[i], rows.at[pl.ds(i * each, each), :], 2 + 2 * i))
    second = []
    for i in range(blocks):
        second.append(copy(cots[i], cot.at[pl.ds(i * each, each), :], 3 + 2 * i))
    second.append(copy(wd_hbm, down, 1))
    for made in first:
        made.wait()
    pre = lax.dot_general(wide[...], rows[...], NT, preferred_element_type=F32)
    for made in second:
        made.wait()
    og[...] = (own_gate(gates_ref[...], me_ref[0]) * cot[...].astype(F32)).astype(BF16)
    out = pltpu.make_async_copy(og, og_hbm, sems.at[0])
    out.start()
    act_grad = lax.dot_general(down[...], og[...], NT, preferred_element_type=F32)
    pre_gate, pre_up = pre[:hid], pre[hid:]
    s = 1.0 / (1.0 + jnp.exp(-pre_gate))
    act = (pre_gate * s * pre_up).astype(BF16)
    pre_grad = (act_grad * pre_up * s * (1.0 + pre_gate * (1.0 - s))).astype(BF16)
    up_grad = (act_grad * pre_gate * s).astype(BF16)
    act_t_ref[...] = act
    act_ref[...] = act.T
    hid_t_ref[:hid, :] = pre_grad
    hid_t_ref[hid:, :] = up_grad
    hid_ref[:, :hid] = pre_grad.T
    hid_ref[:, hid:] = up_grad.T
    out.wait()


def hidden(me, gates, toks, cots, wt, wd):
    blocks = len(toks)
    each = cots[0].shape[0]
    rows = blocks * each
    hid, width = wd.shape
    shapes = [(rows, hid), (rows, 2 * hid), (hid, rows), (2 * hid, rows)]
    outs = tuple(jax.ShapeDtypeStruct(s, BF16) for s in shapes + [(rows, width)])
    specs = tuple(pl.BlockSpec(s, lambda i: (0, 0)) for s in shapes) + (ANY,)
    return pl.pallas_call(
        functools.partial(hidden_kernel, blocks),
        out_shape=outs,
        grid=(1,),
        in_specs=[SMEM, pl.BlockSpec(gates.shape, lambda i: (0, 0))] + [ANY] * (2 * blocks + 2),
        out_specs=specs,
        scratch_shapes=[
            pltpu.VMEM((rows, width), BF16),
            pltpu.VMEM((rows, width), BF16),
            pltpu.VMEM((2 * hid, width), BF16),
            pltpu.VMEM((hid, width), BF16),
            pltpu.VMEM((rows, width), BF16),
            pltpu.SemaphoreType.DMA((2 + 2 * blocks,)),
        ],
        compiler_params=PARAMS,
        cost_estimate=cost(6 * rows * width * hid, (*toks, *cots, wt, wd) + outs),
    )(me, gates, *toks, *cots, wt, wd)


def rows_kernel(more, *refs):
    me_ref, gates_ref, act_ref, hid_ref, wt_hbm, wd_hbm = refs[:6]
    added = refs[6 : 6 + more]
    outs, (wide, down, sems) = refs[6 + more : -3], refs[-3:]
    copies = [pltpu.make_async_copy(wd_hbm, down, sems.at[0]), pltpu.make_async_copy(wt_hbm, wide, sems.at[1])]
    for made in copies:
        made.start()
    gate_col = own_gate(gates_ref[...], me_ref[0])
    half = len(outs) // 2

    def put(values, number):
        if more:
            values = values.astype(F32) + added[number][...].astype(F32)
        values = values.astype(BF16)
        each = values.shape[0] // half
        for i in range(half):
            outs[number * half + i][...] = values[i * each : (i + 1) * each]

    copies[0].wait()
    expert_out = jnp.dot(act_ref[...], down[...], preferred_element_type=F32)
    put((gate_col * expert_out).astype(BF16), 0)
    copies[1].wait()
    grad = jnp.dot(hid_ref[...], wide[...], preferred_element_type=F32)
    put(grad.astype(BF16), 1)


def rows_out(me, gates, act, hid, part, parts, wt, wd, added, split):
    rows = act.shape[0] // parts
    hidden_size, width = wd.shape
    out = jax.ShapeDtypeStruct((rows // split, width), BF16)
    return pl.pallas_call(
        functools.partial(rows_kernel, len(added)),
        out_shape=(out,) * (2 * split),
        grid=(1,),
        in_specs=[SMEM]
        + [pl.BlockSpec((rows, a.shape[1]), lambda i: (part, 0)) for a in (gates, act, hid)]
        + [ANY] * 2
        + [pl.BlockSpec(a.shape, lambda i: (0, 0)) for a in added],
        out_specs=(pl.BlockSpec(out.shape, lambda i: (0, 0)),) * (2 * split),
        scratch_shapes=[
            pltpu.VMEM((2 * hidden_size, width), BF16),
            pltpu.VMEM((hidden_size, width), BF16),
            pltpu.SemaphoreType.DMA((2,)),
        ],
        compiler_params=PARAMS,
        cost_estimate=cost(6 * rows * width * hidden_size, (wt, wd) + tuple(added) + (out,) * (2 * split)),
    )(me, gates, act, hid, wt, wd, *added)


def wide_grad_kernel(groups, first, count, order_ref, *refs):
    blocks = sum(groups)
    toks, hids, outs = refs[:blocks], refs[blocks : blocks + len(groups)], refs[blocks + len(groups) :]
    total, at = None, 0
    for hid_ref, size in zip(hids, groups):
        rows = jnp.concatenate([t[...] for t in toks[at : at + size]], axis=0)
        part = jnp.dot(hid_ref[...], rows, preferred_element_type=F32)
        total = part if total is None else total + part
        at += size
    total = total.astype(BF16)
    for k in range(count):

        @pl.when(pl.program_id(0) == k)
        def _():
            outs[k][...] = total


def wide_grads(order, toks, hids, width, first, count):
    blocks = len(toks)
    each = toks[0].shape[0]
    groups = tuple(h.shape[1] // each for h in hids)
    both, tile = hids[0].shape[0], width // 4
    out = jax.ShapeDtypeStruct((both, tile), BF16)
    return pl.pallas_call(
        functools.partial(wide_grad_kernel, groups, first, count),
        out_shape=(out,) * count,
        grid_spec=pltpu.PrefetchScalarGridSpec(
            num_scalar_prefetch=1,
            grid=(count,),
            in_specs=[pl.BlockSpec((each, tile), lambda i, order: (0, order[first + i]))] * blocks
            + [pl.BlockSpec(h.shape, lambda i, order: (0, 0)) for h in hids],
            out_specs=(pl.BlockSpec(out.shape, lambda i, order: (0, 0)),) * count,
        ),
        compiler_params=PARAMS,
        cost_estimate=cost(2 * count * blocks * each * both * tile, tuple(hids) + (out,) * count),
    )(order, *toks, *hids)


def down_grad_kernel(groups, order_ref, *refs):
    acts, ogs, outs, full = refs[:groups], refs[groups : 2 * groups], refs[2 * groups : -1], refs[-1]
    total = None
    for act, og in zip(acts, ogs):
        part = jnp.dot(act[...], og[...], preferred_element_type=F32)
        total = part if total is None else total + part
    full[...] = total
    size = full.shape[0] // 4
    for k in range(4):
        at = pl.multiple_of(order_ref[k] * size, size)
        outs[k][...] = full[pl.ds(at, size), :].astype(BF16)


def down_grads(order, acts, ogs):
    hid = acts[0].shape[0]
    rows = sum(a.shape[1] for a in acts)
    width = ogs[0].shape[1]
    tile = width // 4
    out = jax.ShapeDtypeStruct((hid // 4, width), BF16)
    return pl.pallas_call(
        functools.partial(down_grad_kernel, len(acts)),
        out_shape=(out,) * 4,
        grid_spec=pltpu.PrefetchScalarGridSpec(
            num_scalar_prefetch=1,
            grid=(width // tile,),
            in_specs=[pl.BlockSpec(a.shape, lambda i, order: (0, 0)) for a in acts]
            + [pl.BlockSpec((o.shape[0], tile), lambda i, order: (0, i)) for o in ogs],
            out_specs=(pl.BlockSpec((hid // 4, tile), lambda i, order: (0, i)),) * 4,
            scratch_shapes=[pltpu.VMEM((hid, tile), F32)],
        ),
        compiler_params=PARAMS,
        cost_estimate=cost(2 * rows * hid * width, tuple(acts) + tuple(ogs)),
    )(order, *acts, *ogs)


def turn_kernel(mid_ref, own, a1, a2, a3, a4, gate_ref, up_ref):
    ends = a1[...].astype(F32) + a2[...].astype(F32)
    total = own[...].astype(F32) + (a3[...].astype(F32) + a4[...].astype(F32))
    total = (total + jnp.where(mid_ref[0] == 1, 0.0, ends)).T
    hid = gate_ref.shape[1]
    gate_ref[...] = total[:, :hid]
    up_ref[...] = total[:, hid:]


def turn(mid, terms):
    both, tile = terms[0].shape
    out = jax.ShapeDtypeStruct((tile, both // 2), F32)
    return pl.pallas_call(
        turn_kernel,
        out_shape=(out, out),
        grid=(tile // LANES,),
        in_specs=[SMEM] + [pl.BlockSpec((both, LANES), lambda i: (0, i))] * 5,
        out_specs=(pl.BlockSpec((LANES, both // 2), lambda i: (i, 0)),) * 2,
        compiler_params=PARAMS,
        cost_estimate=cost(5 * both * tile, terms + (out, out)),
    )(mid, *terms)


def after(values, earlier):
    return lax.optimization_barrier((values, earlier))[0]


def add(a, b):
    return (a.astype(F32) + b.astype(F32)).astype(BF16)


LINE_ORDER = ((3, 2, 1, 0), (0, 3, 2, 1), (3, 0, 1, 2), (0, 1, 2, 3))


def per_device(tokens, expert_ids, gates, w_gate, w_up, w_down, cotangent):
    width = tokens.shape[1]
    group = lax.axis_size("expert")
    shards = lax.axis_size("dp")
    assert group == 8
    me = lax.axis_index("expert").astype(jnp.int32).reshape(1)
    z = lax.axis_index("dp")
    wg, wu, wd = w_gate[0], w_up[0], w_down[0]

    def flip(array, bit):
        return lax.ppermute(array, "expert", [(i, i ^ bit) for i in range(group)])

    tok_0, cot_0 = tokens, cotangent
    cot_y = flip(cot_0, FAR)
    tok_x = flip(tok_0, NEAR)
    cot_x = flip(cot_0, NEAR)
    tok_y = flip(tok_0, FAR)
    cot_d = flip(cot_y, NEAR)
    tok_d = flip(tok_x, FAR)
    lanes = jnp.arange(LANES, dtype=jnp.int32)[None, None, :]
    spread = jnp.where(expert_ids[:, :, None] == lanes, gates.astype(F32)[:, :, None], 0.0)
    gate_0 = jnp.sum(spread, axis=1).astype(BF16)
    gate_x, gate_y = flip(gate_0, NEAR), flip(gate_0, FAR)
    gate_m = jnp.concatenate([gate_0, gate_x, gate_y, flip(gate_x, FAR)], axis=0)
    gate_s = flip(gate_m, CORE)
    most = 3 * tokens.shape[0]
    gates_a = jnp.concatenate([gate_m[:most], gate_s[:most]], axis=0)
    gates_b = jnp.concatenate([gate_m[most:], gate_s[most:]], axis=0)
    wt = transposed(wg, wu)

    toks_a, cots_a = [tok_0, tok_x, tok_y], [cot_0, cot_x, cot_y]
    toks_a += [flip(t, CORE) for t in toks_a]
    cots_a += [flip(c, CORE) for c in cots_a]
    act_a, hid_a, act_t_a, hid_t_a, og_a = hidden(me, gates_a, toks_a, cots_a, wt, wd)
    tok_d, cot_d = after((tok_d, cot_d), act_a)
    toks_b, cots_b = [tok_d, flip(tok_d, CORE)], [cot_d, flip(cot_d, CORE)]
    act_b, hid_b, act_t_b, hid_t_b, og_b = hidden(me, gates_b, toks_b, cots_b, wt, wd)

    line = shards == 4
    table = jnp.asarray(LINE_ORDER if line else ((0, 1, 2, 3),), jnp.int32)
    order = table[z if line else 0]
    mid = (z == 1) | (z == 2)

    def move(array, pairs):
        return lax.ppermute(array, "dp", pairs) if line else array

    def if_mid(array):
        return jnp.where(mid, array, jnp.zeros_like(array))

    one_pairs = [(0, 1), (1, 0), (2, 3), (3, 2)]
    two_pairs = [(0, 1), (1, 3), (3, 2), (2, 0)]
    up_pairs, down_pairs = [(0, 1), (1, 2)], [(3, 2), (2, 1)]
    toks = toks_a + toks_b
    hid_t = (hid_t_a, hid_t_b)
    wide_0 = wide_grads(order, toks, hid_t, width, 0, 1)
    wide_one = move(wide_0[0], one_pairs)
    act_t_a = after(act_t_a, wide_0)
    down = down_grads(order, (act_t_a, act_t_b), (og_a, og_b))
    down_one = move(down[0], one_pairs)
    act_b = after(act_b, down)
    out_s, grad_s = rows_out(me, gates_b, act_b, hid_b, 1, 2, wt, wd, (), 1)
    out_s, grad_s = flip(out_s, CORE), flip(grad_s, CORE)
    hid_t_a = after(hid_t_a, (out_s, grad_s))
    wide = wide_0 + wide_grads(order, toks, (hid_t_a, hid_t_b), width, 1, 3)
    if line:
        wide_send = add(wide[1], if_mid(wide_one))
        wide_two = move(wide_send, two_pairs)
        act_b = after(act_b, wide_send)
    out_d, grad_d = rows_out(me, gates_b, act_b, hid_b, 0, 2, wt, wd, (out_s, grad_s), 1)
    out_d, grad_d, act_a = after((out_d, grad_d, act_a), out_d)
    out_dx, grad_dy = flip(out_d, NEAR), flip(grad_d, FAR)
    out_s, grad_s = rows_out(me, gates_a, act_a, hid_a, 1, 2, wt, wd, (), 1)
    out_s, grad_s = flip(out_s, CORE), flip(grad_s, CORE)
    if line:
        down_send = add(down[1], if_mid(down_one))
        down_two = move(down_send, two_pairs)
        act_a = after(act_a, down_send)
    out_0, out_x, out_y, grad_0, grad_x, grad_y = rows_out(
        me, gates_a, act_a, hid_a, 0, 2, wt, wd, (out_s, grad_s), 3
    )
    out_xx, grad_yy = flip(out_x, NEAR), flip(grad_y, FAR)
    out_yy = flip(add(out_y, out_dx), FAR)
    grad_xx = flip(add(grad_x, grad_dy), NEAR)
    hid_size = wd.shape[0]
    if line:
        wide_send = add(wide[2], if_mid(wide_two))
        wide_up, wide_down = move(wide_send, up_pairs), move(wide_send, down_pairs)
        down_send = add(down[2], if_mid(down_two))
        down_up, down_down = move(down_send, up_pairs), move(down_send, down_pairs)
    mixed = out_0.astype(F32) + out_xx.astype(F32) + out_yy.astype(F32)
    grad_tokens = grad_0.astype(F32) + grad_yy.astype(F32) + grad_xx.astype(F32)
    if line:
        grad_gate, grad_up = turn(
            mid.astype(jnp.int32).reshape(1), (wide[3], wide_one, wide_two, wide_up, wide_down)
        )
        own, one, two, up, low = (t.astype(F32) for t in (down[3], down_one, down_two, down_up, down_down))
        grad_down = own + (up + low) + jnp.where(mid, 0.0, one + two)
    else:
        wide_all = jnp.concatenate(wide, axis=1).T
        grad_wide = lax.psum_scatter(wide_all, "dp", scatter_dimension=0, tiled=True).astype(F32)
        grad_gate, grad_up = grad_wide[:, :hid_size], grad_wide[:, hid_size:]
        grad_down = lax.psum_scatter(jnp.concatenate(down, axis=0), "dp", scatter_dimension=0, tiled=True).astype(F32)

    return (mixed.astype(BF16), grad_tokens.astype(BF16), grad_gate[None], grad_up[None], grad_down[None])


def solution(mesh):
    return jax.shard_map(
        per_device,
        mesh=mesh,
        in_specs=(
            P(("dp", "expert"), None),
            P(("dp", "expert"), None),
            P(("dp", "expert"), None),
            P("expert", None, None),
            P("expert", None, None),
            P("expert", None, None),
            P(("dp", "expert"), None),
        ),
        out_specs=(
            P(("dp", "expert"), None),
            P(("dp", "expert"), None),
            P("expert", "dp", None),
            P("expert", "dp", None),
            P("expert", "dp", None),
        ),
        check_vma=False,
    )
```

```python
import functools

import jax
import jax.numpy as jnp
from jax import lax
from jax.experimental import pallas as pl
from jax.experimental.pallas import tpu as pltpu
from jax.sharding import PartitionSpec as P

F32 = jnp.float32
BF16 = jnp.bfloat16
LANES = 128
CHUNKS = 4
CORE, NEAR, FAR = 1, 2, 4
PARAMS = pltpu.CompilerParams(vmem_limit_bytes=60 * 1024 * 1024)
ANY = pl.BlockSpec(memory_space=pl.ANY)
SMEM = pl.BlockSpec(memory_space=pltpu.SMEM)
NT = (((1,), (1,)), ((), ()))


def cost(flops, arrays):
    size = sum(a.size * a.dtype.itemsize for a in arrays)
    return pl.CostEstimate(flops=flops // 64, bytes_accessed=size // 64, transcendentals=0)


def own_gate(gate_rows, expert_num):
    lane = lax.broadcasted_iota(jnp.int32, gate_rows.shape, 1)
    kept = jnp.where(lane == expert_num, gate_rows.astype(F32), 0.0)
    return jnp.sum(kept, axis=1, keepdims=True)


def pack_kernel(tok_ref, ids_ref, gates_ref, out_ref):
    rows, width = tok_ref.shape
    out_ref[:, :width] = tok_ref[...]
    lane = lax.broadcasted_iota(jnp.int32, (rows, LANES), 1)
    ids, gates = ids_ref[...], gates_ref[...].astype(F32)
    total = jnp.zeros((rows, LANES), F32)
    for k in range(ids.shape[1]):
        total = total + jnp.where(ids[:, k : k + 1] == lane, gates[:, k : k + 1], 0.0)
    out_ref[:, width:] = total.astype(BF16)


def packed(tokens, ids, gates):
    rows, width = tokens.shape
    return pl.pallas_call(
        pack_kernel,
        out_shape=jax.ShapeDtypeStruct((rows, width + LANES), BF16),
        compiler_params=PARAMS,
    )(tokens, ids, gates)


def hidden_kernel(blocks, *refs):
    me_ref = refs[0]
    toks, cots = refs[1 : 1 + blocks], refs[1 + blocks : 1 + 2 * blocks]
    wg_hbm, wu_hbm, wd_hbm = refs[1 + 2 * blocks : 4 + 2 * blocks]
    act_ref, hid_ref, act_t_ref, hid_t_ref, og_hbm = refs[4 + 2 * blocks : 9 + 2 * blocks]
    rows, gates, cot, wide, down, og, sems = refs[9 + 2 * blocks :]
    each, width = cots[0].shape
    hid = wg_hbm.shape[1]

    def copy(source, target, number):
        made = pltpu.make_async_copy(source, target, sems.at[number])
        made.start()
        return made

    def at(i):
        return pl.ds(i * each, each)

    step = width // CHUNKS
    tok_copies = [copy(toks[i].at[:, :width], rows.at[at(i), :], 3 * i) for i in range(blocks)]
    wide_copies = []
    for j in range(CHUNKS):
        part = pl.ds(j * step, step)
        number = 3 * blocks + 1 + 2 * j
        wide_copies.append(copy(wg_hbm.at[part, :], wide.at[part, :hid], number))
        wide_copies.append(copy(wu_hbm.at[part, :], wide.at[part, hid:], number + 1))
    second = []
    for i in range(blocks):
        second.append(copy(toks[i].at[:, width:], gates.at[at(i), :], 3 * i + 1))
        second.append(copy(cots[i], cot.at[at(i), :], 3 * i + 2))
    second.append(copy(wd_hbm, down, 3 * blocks))
    for made in tok_copies:
        made.wait()
    pre = None
    for j in range(CHUNKS):
        wide_copies[2 * j].wait()
        wide_copies[2 * j + 1].wait()
        part = slice(j * step, (j + 1) * step)
        more = jnp.dot(rows[:, part], wide[part, :], preferred_element_type=F32)
        pre = more if pre is None else pre + more
    for made in second:
        made.wait()
    og[...] = (own_gate(gates[...], me_ref[0]) * cot[...].astype(F32)).astype(BF16)
    out = pltpu.make_async_copy(og, og_hbm, sems.at[0])
    out.start()
    act_grad = lax.dot_general(og[...], down[...], NT, preferred_element_type=F32)
    pre_gate, pre_up = pre[:, :hid], pre[:, hid:]
    s = 1.0 / (1.0 + jnp.exp(-pre_gate))
    act = (pre_gate * s * pre_up).astype(BF16)
    pre_grad = (act_grad * pre_up * s * (1.0 + pre_gate * (1.0 - s))).astype(BF16)
    up_grad = (act_grad * pre_gate * s).astype(BF16)
    act_ref[...] = act
    act_t_ref[...] = act.T
    hid_ref[:, :hid] = pre_grad
    hid_ref[:, hid:] = up_grad
    hid_t_ref[:hid, :] = pre_grad.T
    hid_t_ref[hid:, :] = up_grad.T
    out.wait()


def hidden(me, toks, cots, wg, wu, wd):
    blocks = len(toks)
    each = cots[0].shape[0]
    rows = blocks * each
    width, hid = wg.shape
    shapes = [(rows, hid), (rows, 2 * hid), (hid, rows), (2 * hid, rows)]
    outs = tuple(jax.ShapeDtypeStruct(s, BF16) for s in shapes + [(rows, width)])
    specs = tuple(pl.BlockSpec(s, lambda i: (0, 0)) for s in shapes) + (ANY,)
    return pl.pallas_call(
        functools.partial(hidden_kernel, blocks),
        out_shape=outs,
        grid=(1,),
        in_specs=[SMEM] + [ANY] * (2 * blocks + 3),
        out_specs=specs,
        scratch_shapes=[
            pltpu.VMEM((rows, width), BF16),
            pltpu.VMEM((rows, LANES), BF16),
            pltpu.VMEM((rows, width), BF16),
            pltpu.VMEM((width, 2 * hid), BF16),
            pltpu.VMEM((hid, width), BF16),
            pltpu.VMEM((rows, width), BF16),
            pltpu.SemaphoreType.DMA((3 * blocks + 1 + 2 * CHUNKS,)),
        ],
        compiler_params=PARAMS,
        cost_estimate=cost(6 * rows * width * hid, (*toks, *cots, wg, wu, wd) + outs),
    )(me, *toks, *cots, wg, wu, wd)


def rows_kernel(blocks, groups, more, *refs):
    me_ref, gates, refs = refs[0], refs[1 : 1 + blocks], refs[1 + blocks :]
    acts, hids, refs = refs[:groups], refs[groups : 2 * groups], refs[2 * groups :]
    wg_hbm, wu_hbm, wd_hbm = refs[:3]
    added, outs, (wide, down, sems) = refs[3 : 3 + more], refs[3 + more : -3], refs[-3:]
    hid = wg_hbm.shape[1]
    copies = [
        pltpu.make_async_copy(wd_hbm, down, sems.at[0]),
        pltpu.make_async_copy(wg_hbm, wide.at[:, :hid], sems.at[1]),
        pltpu.make_async_copy(wu_hbm, wide.at[:, hid:], sems.at[2]),
    ]
    for made in copies:
        made.start()
    gate_col = own_gate(jnp.concatenate([g[...] for g in gates], axis=0), me_ref[0])
    each = gates[0].shape[0]

    def put(values, number):
        for i in range(blocks):
            piece = values[i * each : (i + 1) * each]
            if more:
                piece = (piece.astype(F32) + added[number * blocks + i][...].astype(F32)).astype(BF16)
            outs[number * blocks + i][...] = piece

    copies[0].wait()
    act = jnp.concatenate([a[...] for a in acts], axis=0)
    expert_out = jnp.dot(act, down[...], preferred_element_type=F32)
    put((gate_col * expert_out).astype(BF16), 0)
    copies[1].wait()
    copies[2].wait()
    hidden_grads = jnp.concatenate([h[...] for h in hids], axis=0)
    grad = lax.dot_general(hidden_grads, wide[...], NT, preferred_element_type=F32)
    put(grad.astype(BF16), 1)


def rows_out(me, gate_arrays, acts, hids, part, wg, wu, wd, added):
    blocks, groups = len(gate_arrays), len(acts)
    each = gate_arrays[0].shape[0]
    width, hid = wg.shape
    outs = (jax.ShapeDtypeStruct((each, width), BF16),) * (2 * blocks)
    block = pl.BlockSpec((each, width), lambda i: (0, 0))
    gate_spec = pl.BlockSpec((each, LANES), lambda i: (0, width // LANES))
    return pl.pallas_call(
        functools.partial(rows_kernel, blocks, groups, len(added)),
        out_shape=outs,
        grid=(1,),
        in_specs=[SMEM]
        + [gate_spec] * blocks
        + [pl.BlockSpec((a.shape[0] // 2, a.shape[1]), lambda i: (part, 0)) for a in (*acts, *hids)]
        + [ANY] * 3
        + [block] * len(added),
        out_specs=(block,) * (2 * blocks),
        scratch_shapes=[
            pltpu.VMEM((width, 2 * hid), BF16),
            pltpu.VMEM((hid, width), BF16),
            pltpu.SemaphoreType.DMA((3,)),
        ],
        compiler_params=PARAMS,
        cost_estimate=cost(6 * blocks * each * width * hid, (wg, wu, wd) + outs),
    )(me, *gate_arrays, *acts, *hids, wg, wu, wd, *added)


def wide_grad_kernel(groups, first, count, order_ref, *refs):
    blocks = sum(groups)
    toks, hids, outs = refs[:blocks], refs[blocks : blocks + len(groups)], refs[blocks + len(groups) :]
    total, at = None, 0
    for hid_ref, size in zip(hids, groups):
        rows = jnp.concatenate([t[...] for t in toks[at : at + size]], axis=0)
        part = jnp.dot(hid_ref[...], rows, preferred_element_type=F32)
        total = part if total is None else total + part
        at += size
    total = total.astype(BF16)
    for k in range(count):

        @pl.when(pl.program_id(0) == k)
        def _():
            outs[k][...] = total


def wide_grads(order, toks, hids, width, first, count):
    blocks = len(toks)
    each = toks[0].shape[0]
    groups = tuple(h.shape[1] // each for h in hids)
    both, tile = hids[0].shape[0], width // 4
    out = jax.ShapeDtypeStruct((both, tile), BF16)
    return pl.pallas_call(
        functools.partial(wide_grad_kernel, groups, first, count),
        out_shape=(out,) * count,
        grid_spec=pltpu.PrefetchScalarGridSpec(
            num_scalar_prefetch=1,
            grid=(count,),
            in_specs=[pl.BlockSpec((each, tile), lambda i, order: (0, order[first + i]))] * blocks
            + [pl.BlockSpec(h.shape, lambda i, order: (0, 0)) for h in hids],
            out_specs=(pl.BlockSpec(out.shape, lambda i, order: (0, 0)),) * count,
        ),
        compiler_params=PARAMS,
        cost_estimate=cost(2 * count * blocks * each * both * tile, tuple(hids) + (out,) * count),
    )(order, *toks, *hids)


def down_grad_kernel(groups, order_ref, *refs):
    acts, ogs, outs, full = refs[:groups], refs[groups : 2 * groups], refs[2 * groups : -1], refs[-1]
    total = None
    for act, og in zip(acts, ogs):
        part = jnp.dot(act[...], og[...], preferred_element_type=F32)
        total = part if total is None else total + part
    full[...] = total
    size = full.shape[0] // 4
    for k in range(4):
        at = pl.multiple_of(order_ref[k] * size, size)
        outs[k][...] = full[pl.ds(at, size), :].astype(BF16)


def down_grads(order, acts, ogs):
    hid = acts[0].shape[0]
    rows = sum(a.shape[1] for a in acts)
    width = ogs[0].shape[1]
    tile = width // 4
    out = jax.ShapeDtypeStruct((hid // 4, width), BF16)
    return pl.pallas_call(
        functools.partial(down_grad_kernel, len(acts)),
        out_shape=(out,) * 4,
        grid_spec=pltpu.PrefetchScalarGridSpec(
            num_scalar_prefetch=1,
            grid=(width // tile,),
            in_specs=[pl.BlockSpec(a.shape, lambda i, order: (0, 0)) for a in acts]
            + [pl.BlockSpec((o.shape[0], tile), lambda i, order: (0, i)) for o in ogs],
            out_specs=(pl.BlockSpec((hid // 4, tile), lambda i, order: (0, i)),) * 4,
            scratch_shapes=[pltpu.VMEM((hid, tile), F32)],
        ),
        compiler_params=PARAMS,
        cost_estimate=cost(2 * rows * hid * width, tuple(acts) + tuple(ogs)),
    )(order, *acts, *ogs)


def turn_kernel(mid_ref, own, a1, a2, a3, a4, gate_ref, up_ref):
    ends = a1[...].astype(F32) + a2[...].astype(F32)
    total = own[...].astype(F32) + (a3[...].astype(F32) + a4[...].astype(F32))
    total = (total + jnp.where(mid_ref[0] == 1, 0.0, ends)).T
    hid = gate_ref.shape[1]
    gate_ref[...] = total[:, :hid]
    up_ref[...] = total[:, hid:]


def turn(mid, terms):
    both, tile = terms[0].shape
    out = jax.ShapeDtypeStruct((tile, both // 2), F32)
    return pl.pallas_call(
        turn_kernel,
        out_shape=(out, out),
        grid=(tile // LANES,),
        in_specs=[SMEM] + [pl.BlockSpec((both, LANES), lambda i: (0, i))] * 5,
        out_specs=(pl.BlockSpec((LANES, both // 2), lambda i: (i, 0)),) * 2,
        compiler_params=PARAMS,
        cost_estimate=cost(5 * both * tile, terms + (out, out)),
    )(mid, *terms)


def after(values, earlier):
    return lax.optimization_barrier((values, earlier))[0]


def add(a, b):
    return (a.astype(F32) + b.astype(F32)).astype(BF16)


LINE_ORDER = ((3, 2, 1, 0), (0, 3, 2, 1), (3, 0, 1, 2), (0, 1, 2, 3))


def per_device(tokens, expert_ids, gates, w_gate, w_up, w_down, cotangent):
    width = tokens.shape[1]
    group = lax.axis_size("expert")
    shards = lax.axis_size("dp")
    assert group == 8
    me = lax.axis_index("expert").astype(jnp.int32).reshape(1)
    z = lax.axis_index("dp")
    wg, wu, wd = w_gate[0], w_up[0], w_down[0]

    def flip(array, bit):
        return lax.ppermute(array, "expert", [(i, i ^ bit) for i in range(group)])

    cot_0 = cotangent
    tok_0 = packed(tokens, expert_ids, gates)
    tok_x, cot_y = flip(tok_0, NEAR), flip(cot_0, FAR)
    cot_x, tok_y = flip(cot_0, NEAR), flip(tok_0, FAR)
    cot_d, tok_d = flip(cot_y, NEAR), flip(tok_x, FAR)

    toks_a, cots_a = [tok_0, tok_x, tok_y], [cot_0, cot_x, cot_y]
    toks_a += [flip(t, CORE) for t in toks_a]
    cots_a += [flip(c, CORE) for c in cots_a]
    act_a, hid_a, act_t_a, hid_t_a, og_a = hidden(me, toks_a, cots_a, wg, wu, wd)
    tok_d, cot_d = after((tok_d, cot_d), act_a)
    toks_b, cots_b = [tok_d, flip(tok_d, CORE)], [cot_d, flip(cot_d, CORE)]
    act_b, hid_b, act_t_b, hid_t_b, og_b = hidden(me, toks_b, cots_b, wg, wu, wd)

    line = shards == 4
    table = jnp.asarray(LINE_ORDER if line else ((0, 1, 2, 3),), jnp.int32)
    order = table[z if line else 0]
    mid = (z == 1) | (z == 2)

    def move(array, pairs):
        return lax.ppermute(array, "dp", pairs) if line else array

    def if_mid(array):
        return jnp.where(mid, array, jnp.zeros_like(array))

    one_pairs = [(0, 1), (1, 0), (2, 3), (3, 2)]
    two_pairs = [(0, 1), (1, 3), (3, 2), (2, 0)]
    up_pairs, down_pairs = [(0, 1), (1, 2)], [(3, 2), (2, 1)]
    toks = toks_a + toks_b
    hid_t = (hid_t_a, hid_t_b)
    wide_0 = wide_grads(order, toks, hid_t, width, 0, 1)
    wide_one = move(wide_0[0], one_pairs)
    act_t_a = after(act_t_a, wide_0)
    down = down_grads(order, (act_t_a, act_t_b), (og_a, og_b))
    down_one = move(down[0], one_pairs)
    hid_t_a = after(hid_t_a, down)
    wide = wide_0 + wide_grads(order, toks, (hid_t_a, hid_t_b), width, 1, 3)
    act_a = after(act_a, wide[1])
    acts, hids = (act_a, act_b), (hid_a, hid_b)
    sent = rows_out(me, toks_a[3:] + toks_b[1:], acts, hids, 1, wg, wu, wd, ())
    if line:
        wide_one = after(wide_one, sent)
        wide_send = add(wide[1], if_mid(wide_one))
        wide_two = move(wide_send, two_pairs)
        down_one = after(down_one, wide_send)
        down_send = add(down[1], if_mid(down_one))
        down_two = move(down_send, two_pairs)
        sent = after(sent, down_send)
    sent = [flip(a, CORE) for a in sent]
    kept = rows_out(me, toks_a[:3] + toks_b[:1], acts, hids, 0, wg, wu, wd, sent)
    out_0, out_x, out_y, out_d, grad_0, grad_x, grad_y, grad_d = kept
    out_dx, grad_dy = flip(out_d, NEAR), flip(grad_d, FAR)
    out_xx, grad_yy = flip(out_x, NEAR), flip(grad_y, FAR)
    hid_size = wd.shape[0]
    if line:
        wide_two = after(wide_two, kept)
        wide_send = add(wide[2], if_mid(wide_two))
        wide_up, wide_down = move(wide_send, up_pairs), move(wide_send, down_pairs)
        down_two = after(down_two, wide_send)
        down_send = add(down[2], if_mid(down_two))
        down_up, down_down = move(down_send, up_pairs), move(down_send, down_pairs)
        out_dx, grad_dy = after((out_dx, grad_dy), down_send)
    out_yy = flip(add(out_y, out_dx), FAR)
    grad_xx = flip(add(grad_x, grad_dy), NEAR)
    mixed = (out_0.astype(F32) + out_xx.astype(F32) + out_yy.astype(F32)).astype(BF16)
    grad_tokens = (grad_0.astype(F32) + grad_yy.astype(F32) + grad_xx.astype(F32)).astype(BF16)
    if line:
        wide_up, wide_down = after((wide_up, wide_down), (mixed, grad_tokens))
        grad_gate, grad_up = turn(
            mid.astype(jnp.int32).reshape(1), (wide[3], wide_one, wide_two, wide_up, wide_down)
        )
        own, one, two, up, low = (t.astype(F32) for t in (down[3], down_one, down_two, down_up, down_down))
        grad_down = own + (up + low) + jnp.where(mid, 0.0, one + two)
    else:
        wide_all = jnp.concatenate(wide, axis=1).T
        grad_wide = lax.psum_scatter(wide_all, "dp", scatter_dimension=0, tiled=True).astype(F32)
        grad_gate, grad_up = grad_wide[:, :hid_size], grad_wide[:, hid_size:]
        grad_down = lax.psum_scatter(jnp.concatenate(down, axis=0), "dp", scatter_dimension=0, tiled=True).astype(F32)

    return (mixed, grad_tokens, grad_gate[None], grad_up[None], grad_down[None])


def solution(mesh):
    return jax.shard_map(
        per_device,
        mesh=mesh,
        in_specs=(
            P(("dp", "expert"), None),
            P(("dp", "expert"), None),
            P(("dp", "expert"), None),
            P("expert", None, None),
            P("expert", None, None),
            P("expert", None, None),
            P(("dp", "expert"), None),
        ),
        out_specs=(
            P(("dp", "expert"), None),
            P(("dp", "expert"), None),
            P("expert", "dp", None),
            P("expert", "dp", None),
            P("expert", "dp", None),
        ),
        check_vma=False,
    )
```

```python
import functools

import jax
import jax.numpy as jnp
from jax import lax
from jax.experimental import pallas as pl
from jax.experimental.pallas import tpu as pltpu
from jax.sharding import PartitionSpec as P

F32 = jnp.float32
BF16 = jnp.bfloat16
LANES = 128
CHUNKS = 4
CORE, NEAR, FAR = 1, 2, 4
PARAMS = pltpu.CompilerParams(vmem_limit_bytes=60 * 1024 * 1024)
ANY = pl.BlockSpec(memory_space=pl.ANY)
SMEM = pl.BlockSpec(memory_space=pltpu.SMEM)
NT = (((1,), (1,)), ((), ()))


def cost(flops, arrays):
    size = sum(a.size * a.dtype.itemsize for a in arrays)
    return pl.CostEstimate(flops=flops // 64, bytes_accessed=size // 64, transcendentals=0)


def own_gate(gate_rows, expert_num):
    lane = lax.broadcasted_iota(jnp.int32, gate_rows.shape, 1)
    kept = jnp.where(lane == expert_num, gate_rows.astype(F32), 0.0)
    return jnp.sum(kept, axis=1, keepdims=True)


def pack_kernel(tok_ref, ids_ref, gates_ref, out_ref):
    rows, width = tok_ref.shape
    out_ref[:, :width] = tok_ref[...]
    lane = lax.broadcasted_iota(jnp.int32, (rows, LANES), 1)
    ids, gates = ids_ref[...], gates_ref[...].astype(F32)
    total = jnp.zeros((rows, LANES), F32)
    for k in range(ids.shape[1]):
        total = total + jnp.where(ids[:, k : k + 1] == lane, gates[:, k : k + 1], 0.0)
    out_ref[:, width:] = total.astype(BF16)


def packed(tokens, ids, gates):
    rows, width = tokens.shape
    return pl.pallas_call(
        pack_kernel,
        out_shape=jax.ShapeDtypeStruct((rows, width + LANES), BF16),
        compiler_params=PARAMS,
    )(tokens, ids, gates)


def hidden_kernel(blocks, *refs):
    me_ref = refs[0]
    toks, cots = refs[1 : 1 + blocks], refs[1 + blocks : 1 + 2 * blocks]
    wg_hbm, wu_hbm, wd_hbm = refs[1 + 2 * blocks : 4 + 2 * blocks]
    act_ref, hid_ref, og_hbm = refs[4 + 2 * blocks : 7 + 2 * blocks]
    rows, gates, cot, wide, down, og, sems = refs[7 + 2 * blocks :]
    each, width = cots[0].shape
    hid = wg_hbm.shape[1]

    def copy(source, target, number):
        made = pltpu.make_async_copy(source, target, sems.at[number])
        made.start()
        return made

    def at(i):
        return pl.ds(i * each, each)

    step = width // CHUNKS
    tok_copies = [copy(toks[i].at[:, :width], rows.at[at(i), :], 3 * i) for i in range(blocks)]
    wide_copies = []
    for j in range(CHUNKS):
        part = pl.ds(j * step, step)
        number = 3 * blocks + 1 + 2 * j
        wide_copies.append(copy(wg_hbm.at[part, :], wide.at[part, :hid], number))
        wide_copies.append(copy(wu_hbm.at[part, :], wide.at[part, hid:], number + 1))
    second = []
    for i in range(blocks):
        second.append(copy(toks[i].at[:, width:], gates.at[at(i), :], 3 * i + 1))
        second.append(copy(cots[i], cot.at[at(i), :], 3 * i + 2))
    second.append(copy(wd_hbm, down, 3 * blocks))
    for made in tok_copies:
        made.wait()
    pre = None
    for j in range(CHUNKS):
        wide_copies[2 * j].wait()
        wide_copies[2 * j + 1].wait()
        part = slice(j * step, (j + 1) * step)
        more = jnp.dot(rows[:, part], wide[part, :], preferred_element_type=F32)
        pre = more if pre is None else pre + more
    for made in second:
        made.wait()
    og[...] = (own_gate(gates[...], me_ref[0]) * cot[...].astype(F32)).astype(BF16)
    out = pltpu.make_async_copy(og, og_hbm, sems.at[0])
    out.start()
    act_grad = lax.dot_general(og[...], down[...], NT, preferred_element_type=F32)
    pre_gate, pre_up = pre[:, :hid], pre[:, hid:]
    s = 1.0 / (1.0 + jnp.exp(-pre_gate))
    act_ref[...] = (pre_gate * s * pre_up).astype(BF16)
    hid_ref[:, :hid] = (act_grad * pre_up * s * (1.0 + pre_gate * (1.0 - s))).astype(BF16)
    hid_ref[:, hid:] = (act_grad * pre_gate * s).astype(BF16)
    out.wait()


def hidden(me, toks, cots, wg, wu, wd):
    blocks = len(toks)
    each = cots[0].shape[0]
    rows = blocks * each
    width, hid = wg.shape
    shapes = [(rows, hid), (rows, 2 * hid)]
    outs = tuple(jax.ShapeDtypeStruct(s, BF16) for s in shapes + [(rows, width)])
    specs = tuple(pl.BlockSpec(s, lambda i: (0, 0)) for s in shapes) + (ANY,)
    return pl.pallas_call(
        functools.partial(hidden_kernel, blocks),
        out_shape=outs,
        grid=(1,),
        in_specs=[SMEM] + [ANY] * (2 * blocks + 3),
        out_specs=specs,
        scratch_shapes=[
            pltpu.VMEM((rows, width), BF16),
            pltpu.VMEM((rows, LANES), BF16),
            pltpu.VMEM((rows, width), BF16),
            pltpu.VMEM((width, 2 * hid), BF16),
            pltpu.VMEM((hid, width), BF16),
            pltpu.VMEM((rows, width), BF16),
            pltpu.SemaphoreType.DMA((3 * blocks + 1 + 2 * CHUNKS,)),
        ],
        compiler_params=PARAMS,
        cost_estimate=cost(6 * rows * width * hid, (*toks, *cots, wg, wu, wd) + outs),
    )(me, *toks, *cots, wg, wu, wd)


def rows_kernel(blocks, groups, places, more, *refs):
    me_ref, gates, refs = refs[0], refs[1 : 1 + blocks], refs[1 + blocks :]
    acts, hids, refs = refs[:groups], refs[groups : 2 * groups], refs[2 * groups :]
    wg_hbm, wu_hbm, wd_hbm = refs[:3]
    added, outs, (wide, down, sems) = refs[3 : 3 + more], refs[3 + more : -3], refs[-3:]
    hid = wg_hbm.shape[1]
    copies = [
        pltpu.make_async_copy(wd_hbm, down, sems.at[0]),
        pltpu.make_async_copy(wg_hbm, wide.at[:, :hid], sems.at[1]),
        pltpu.make_async_copy(wu_hbm, wide.at[:, hid:], sems.at[2]),
    ]
    for made in copies:
        made.start()
    gate_col = own_gate(jnp.concatenate([g[...] for g in gates], axis=0), me_ref[0])
    each = gates[0].shape[0]

    def put(values, number):
        for i in range(blocks):
            piece = values[i * each : (i + 1) * each]
            if more:
                other = added[number][i * each : (i + 1) * each, :]
                piece = (piece.astype(F32) + other.astype(F32)).astype(BF16)
            array, block = places[number][i]
            outs[array][block * each : (block + 1) * each, :] = piece

    copies[0].wait()
    act = jnp.concatenate([a[...] for a in acts], axis=0)
    expert_out = jnp.dot(act, down[...], preferred_element_type=F32)
    put((gate_col * expert_out).astype(BF16), 0)
    copies[1].wait()
    copies[2].wait()
    hidden_grads = jnp.concatenate([h[...] for h in hids], axis=0)
    grad = lax.dot_general(hidden_grads, wide[...], NT, preferred_element_type=F32)
    put(grad.astype(BF16), 1)


def rows_out(me, gate_arrays, acts, hids, part, wg, wu, wd, added, places):
    blocks, groups = len(gate_arrays), len(acts)
    each = gate_arrays[0].shape[0]
    width, hid = wg.shape
    flat = places[0] + places[1]
    sizes = [sum(array == k for array, _ in flat) for k in range(1 + max(array for array, _ in flat))]
    outs = tuple(jax.ShapeDtypeStruct((n * each, width), BF16) for n in sizes)
    gate_spec = pl.BlockSpec((each, LANES), lambda i: (0, width // LANES))
    whole = lambda a: pl.BlockSpec(a.shape, lambda i: (0, 0))
    return pl.pallas_call(
        functools.partial(rows_kernel, blocks, groups, places, len(added)),
        out_shape=outs,
        grid=(1,),
        in_specs=[SMEM]
        + [gate_spec] * blocks
        + [pl.BlockSpec((a.shape[0] // 2, a.shape[1]), lambda i: (part, 0)) for a in (*acts, *hids)]
        + [ANY] * 3
        + [whole(a) for a in added],
        out_specs=tuple(whole(o) for o in outs),
        scratch_shapes=[
            pltpu.VMEM((width, 2 * hid), BF16),
            pltpu.VMEM((hid, width), BF16),
            pltpu.SemaphoreType.DMA((3,)),
        ],
        compiler_params=PARAMS,
        cost_estimate=cost(6 * blocks * each * width * hid, (wg, wu, wd) + outs),
    )(me, *gate_arrays, *acts, *hids, wg, wu, wd, *added)


TN = (((0,), (0,)), ((), ()))


def wide_grad_kernel(blocks, count, order_ref, *refs):
    toks, hids, outs = refs[:blocks], refs[blocks:-count], refs[-count:]
    rows = jnp.concatenate([t[...] for t in toks], axis=0)
    hidden_grads = jnp.concatenate([h[...] for h in hids], axis=0)
    total = lax.dot_general(rows, hidden_grads, TN, preferred_element_type=F32).astype(BF16)
    for k in range(count):

        @pl.when(pl.program_id(0) == k)
        def _():
            outs[k][...] = total


def wide_grads(order, toks, hids, width, first, count):
    blocks = len(toks)
    each = toks[0].shape[0]
    both, tile = hids[0].shape[1], width // 4
    out = jax.ShapeDtypeStruct((tile, both), BF16)
    return pl.pallas_call(
        functools.partial(wide_grad_kernel, blocks, count),
        out_shape=(out,) * count,
        grid_spec=pltpu.PrefetchScalarGridSpec(
            num_scalar_prefetch=1,
            grid=(count,),
            in_specs=[pl.BlockSpec((each, tile), lambda i, order: (0, order[first + i]))] * blocks
            + [pl.BlockSpec(h.shape, lambda i, order: (0, 0)) for h in hids],
            out_specs=(pl.BlockSpec(out.shape, lambda i, order: (0, 0)),) * count,
        ),
        compiler_params=PARAMS,
        cost_estimate=cost(2 * count * blocks * each * both * tile, tuple(hids) + (out,) * count),
    )(order, *toks, *hids)


def down_grad_kernel(groups, order_ref, *refs):
    acts, ogs, outs, full = refs[:groups], refs[groups : 2 * groups], refs[2 * groups : -1], refs[-1]
    act = jnp.concatenate([a[...] for a in acts], axis=0)
    og = jnp.concatenate([o[...] for o in ogs], axis=0)
    full[...] = lax.dot_general(act, og, TN, preferred_element_type=F32)
    size = full.shape[0] // 4
    for k in range(4):
        at = pl.multiple_of(order_ref[k] * size, size)
        outs[k][...] = full[pl.ds(at, size), :].astype(BF16)


def down_grads(order, acts, ogs):
    hid = acts[0].shape[1]
    rows = sum(a.shape[0] for a in acts)
    width = ogs[0].shape[1]
    tile = width // 4
    out = jax.ShapeDtypeStruct((hid // 4, width), BF16)
    return pl.pallas_call(
        functools.partial(down_grad_kernel, len(acts)),
        out_shape=(out,) * 4,
        grid_spec=pltpu.PrefetchScalarGridSpec(
            num_scalar_prefetch=1,
            grid=(width // tile,),
            in_specs=[pl.BlockSpec(a.shape, lambda i, order: (0, 0)) for a in acts]
            + [pl.BlockSpec((o.shape[0], tile), lambda i, order: (0, i)) for o in ogs],
            out_specs=(pl.BlockSpec((hid // 4, tile), lambda i, order: (0, i)),) * 4,
            scratch_shapes=[pltpu.VMEM((hid, tile), F32)],
        ),
        compiler_params=PARAMS,
        cost_estimate=cost(2 * rows * hid * width, tuple(acts) + tuple(ogs)),
    )(order, *acts, *ogs)


PIECE = 256


def pieces(wide_shape, down_shape):
    at = 0
    for number, (rows, columns) in enumerate((wide_shape, down_shape)):
        for j in range(columns // PIECE):
            yield number, slice(at, at + rows), slice(j * PIECE, (j + 1) * PIECE)
            at += rows


def join_kernel(joined, mid_ref, wide_own, down_own, *refs):
    came, out_ref = refs[:-1], refs[-1]
    owns = wide_own, down_own
    for number, rows, part in pieces(wide_own.shape, down_own.shape):
        other = came[0][rows, :] if joined else came[number][:, part]
        other = jnp.where(mid_ref[0] == 1, other.astype(F32), 0.0)
        out_ref[rows, :] = (owns[number][:, part].astype(F32) + other).astype(BF16)


def join(mid, wide_own, down_own, *came):
    out = jax.ShapeDtypeStruct(((wide_own.size + down_own.size) // PIECE, PIECE), BF16)
    return pl.pallas_call(
        functools.partial(join_kernel, len(came) == 1),
        out_shape=out,
        in_specs=[SMEM] + [pl.BlockSpec(memory_space=pltpu.VMEM)] * (2 + len(came)),
        compiler_params=PARAMS,
        cost_estimate=cost(wide_own.size, (out,)),
    )(mid, wide_own, down_own, *came)


def base_kernel(mid_ref, wide_own, down_own, wide_one, down_one, two_ref, wide_out, down_out):
    owns, ones, outs = (wide_own, down_own), (wide_one, down_one), (wide_out, down_out)
    for number, rows, part in pieces(wide_own.shape, down_own.shape):
        came = ones[number][:, part].astype(F32) + two_ref[rows, :].astype(F32)
        came = jnp.where(mid_ref[0] == 1, 0.0, came)
        outs[number][:, part] = owns[number][:, part].astype(F32) + came


def base_terms(mid, wide_own, down_own, wide_one, down_one, two):
    outs = tuple(jax.ShapeDtypeStruct(a.shape, F32) for a in (wide_own, down_own))
    return pl.pallas_call(
        base_kernel,
        out_shape=outs,
        in_specs=[SMEM] + [pl.BlockSpec(memory_space=pltpu.VMEM)] * 5,
        compiler_params=PARAMS,
        cost_estimate=cost(wide_own.size, outs),
    )(mid, wide_own, down_own, wide_one, down_one, two)


def finish_kernel(wide_ref, down_ref, up_ref, low_ref, gate_out, up_out, down_out):
    bases, outs = (wide_ref, down_ref), ((gate_out, up_out), (down_out,))
    for number, rows, part in pieces(wide_ref.shape, down_ref.shape):
        came = up_ref[rows, :].astype(F32) + low_ref[rows, :].astype(F32)
        total = bases[number][:, part] + came
        for k, out in enumerate(outs[number]):
            size = out.shape[1]
            a, b = max(part.start, k * size), min(part.stop, (k + 1) * size)
            if a < b:
                out[:, a - k * size : b - k * size] = total[:, a - part.start : b - part.start]


def finish(wide, down, one, two):
    rows, both = wide.shape
    outs = (jax.ShapeDtypeStruct((rows, both // 2), F32),) * 2 + (jax.ShapeDtypeStruct(down.shape, F32),)
    return pl.pallas_call(
        finish_kernel,
        out_shape=outs,
        compiler_params=PARAMS,
        cost_estimate=cost(wide.size, outs),
    )(wide, down, one, two)


def after(values, earlier):
    return lax.optimization_barrier((values, earlier))[0]


def pair_sums_kernel(count, *refs):
    for k, out_ref in enumerate(refs[-2:]):
        terms = [r[...].astype(F32) for r in refs[k * count : (k + 1) * count]]
        out_ref[...] = sum(terms[1:], terms[0]).astype(BF16)


def pair_sums(each, first, second):
    width = first[0][0].shape[1]
    tile = each // 4
    spec = lambda block: pl.BlockSpec((tile, width), lambda i: (4 * block + i, 0))
    out = jax.ShapeDtypeStruct((each, width), BF16)
    return pl.pallas_call(
        functools.partial(pair_sums_kernel, len(first)),
        out_shape=(out, out),
        grid=(4,),
        in_specs=[spec(block) for _, block in first + second],
        out_specs=(spec(0), spec(0)),
        compiler_params=PARAMS,
        cost_estimate=cost(out.size, (out,)),
    )(*[a for a, _ in first + second])


LINE_ORDER = ((3, 2, 1, 0), (0, 3, 2, 1), (3, 0, 1, 2), (0, 1, 2, 3))


def per_device(tokens, expert_ids, gates, w_gate, w_up, w_down, cotangent):
    width = tokens.shape[1]
    group = lax.axis_size("expert")
    shards = lax.axis_size("dp")
    assert group == 8
    me = lax.axis_index("expert").astype(jnp.int32).reshape(1)
    z = lax.axis_index("dp")
    wg, wu, wd = w_gate[0], w_up[0], w_down[0]

    def flip(array, bit):
        return lax.ppermute(array, "expert", [(i, i ^ bit) for i in range(group)])

    cot_0 = cotangent
    tok_0 = packed(tokens, expert_ids, gates)
    tok_x, cot_y = flip(tok_0, NEAR), flip(cot_0, FAR)
    cot_x, tok_y = flip(cot_0, NEAR), flip(tok_0, FAR)
    cot_d, tok_d = flip(cot_y, NEAR), flip(tok_x, FAR)

    toks_a, cots_a = [tok_0, tok_x, tok_y], [cot_0, cot_x, cot_y]
    toks_a += [flip(t, CORE) for t in toks_a]
    cots_a += [flip(c, CORE) for c in cots_a]
    act_a, hid_a, og_a = hidden(me, toks_a, cots_a, wg, wu, wd)
    tok_d, cot_d = after((tok_d, cot_d), act_a)
    toks_b, cots_b = [tok_d, flip(tok_d, CORE)], [cot_d, flip(cot_d, CORE)]
    act_b, hid_b, og_b = hidden(me, toks_b, cots_b, wg, wu, wd)

    line = shards == 4
    table = jnp.asarray(LINE_ORDER if line else ((0, 1, 2, 3),), jnp.int32)
    order = table[z if line else 0]
    mid = (z == 1) | (z == 2)

    def move(array, pairs):
        return lax.ppermute(array, "dp", pairs) if line else array

    one_pairs = [(0, 1), (1, 0), (2, 3), (3, 2)]
    two_pairs = [(0, 1), (1, 3), (3, 2), (2, 0)]
    up_pairs, down_pairs = [(0, 1), (1, 2)], [(3, 2), (2, 1)]
    toks, hids = toks_a + toks_b, (hid_a, hid_b)
    wide_0 = wide_grads(order, toks, hids, width, 0, 1)
    wide_one = move(wide_0[0], one_pairs)
    act_a = after(act_a, wide_0)
    down = down_grads(order, (act_a, act_b), (og_a, og_b))
    down_one = move(down[0], one_pairs)
    hid_a = after(hid_a, down)
    wide = wide_0 + wide_grads(order, toks, (hid_a, hid_b), width, 1, 3)
    act_a = after(act_a, wide[1])
    acts, hids = (act_a, act_b), (hid_a, hid_b)
    there = tuple((0, i) for i in range(4)), tuple((1, i) for i in range(4))
    sent = rows_out(me, toks_a[3:] + toks_b[1:], acts, hids, 1, wg, wu, wd, (), there)
    if line:
        mid_number = mid.astype(jnp.int32).reshape(1)
        wide_one, down_one = after((wide_one, down_one), sent)
        second = join(mid_number, wide[1], down[1], wide_one, down_one)
        two = move(second, two_pairs)
        sent = after(sent, second)
    sent = [flip(a, CORE) for a in sent]
    here = ((0, 0), (2, 0), (1, 0), (2, 1)), ((3, 0), (4, 0), (5, 0), (5, 1))
    kept = rows_out(me, toks_a[:3] + toks_b[:1], acts, hids, 0, wg, wu, wd, sent, here)
    out_0, out_y, out_near, grad_0, grad_x, grad_far = kept
    out_near, grad_far = flip(out_near, NEAR), flip(grad_far, FAR)
    hid_size = wd.shape[0]
    each = tokens.shape[0]
    if line:
        two = after(two, kept)
        last = join(mid_number, wide[2], down[2], two)
        last_up, last_down = move(last, up_pairs), move(last, down_pairs)
        out_near, grad_far = after((out_near, grad_far), last)
    out_y, grad_x = pair_sums(each, [(out_y, 0), (out_near, 1)], [(grad_x, 0), (grad_far, 1)])
    out_yy, grad_xx = flip(out_y, FAR), flip(grad_x, NEAR)
    if line:
        base = base_terms(mid_number, wide[3], down[3], wide_one, down_one, after(two, (out_y, grad_x)))
    mixed, grad_tokens = pair_sums(
        each, [(out_0, 0), (out_near, 0), (out_yy, 0)], [(grad_0, 0), (grad_far, 0), (grad_xx, 0)]
    )
    if line:
        base, mixed, grad_tokens = lax.optimization_barrier((base, mixed, grad_tokens))
        last_up, last_down = after((last_up, last_down), (mixed, grad_tokens))
        grad_gate, grad_up, grad_down = finish(*base, last_up, last_down)
    else:
        wide_all = jnp.concatenate(wide, axis=0)
        grad_wide = lax.psum_scatter(wide_all, "dp", scatter_dimension=0, tiled=True).astype(F32)
        grad_gate, grad_up = grad_wide[:, :hid_size], grad_wide[:, hid_size:]
        grad_down = lax.psum_scatter(jnp.concatenate(down, axis=0), "dp", scatter_dimension=0, tiled=True).astype(F32)
    return (mixed, grad_tokens, grad_gate[None], grad_up[None], grad_down[None])


def solution(mesh):
    return jax.shard_map(
        per_device,
        mesh=mesh,
        in_specs=(
            P(("dp", "expert"), None),
            P(("dp", "expert"), None),
            P(("dp", "expert"), None),
            P("expert", None, None),
            P("expert", None, None),
            P("expert", None, None),
            P(("dp", "expert"), None),
        ),
        out_specs=(
            P(("dp", "expert"), None),
            P(("dp", "expert"), None),
            P("expert", "dp", None),
            P("expert", "dp", None),
            P("expert", "dp", None),
        ),
        check_vma=False,
    )
```

```python
import functools

import jax
import jax.numpy as jnp
from jax import lax
from jax.experimental import pallas as pl
from jax.experimental.pallas import tpu as pltpu
from jax.sharding import PartitionSpec as P

F32 = jnp.float32
BF16 = jnp.bfloat16
LANES = 128
CHUNKS = 4
CORE, NEAR, FAR = 1, 2, 4
MEDIUM = pltpu.CompilerParams(vmem_limit_bytes=32 * 1024 * 1024)
SMALL = pltpu.CompilerParams(vmem_limit_bytes=16 * 1024 * 1024)
ANY = pl.BlockSpec(memory_space=pl.ANY)
SMEM = pl.BlockSpec(memory_space=pltpu.SMEM)
NT = (((1,), (1,)), ((), ()))


def cost(flops, arrays):
    size = sum(a.size * a.dtype.itemsize for a in arrays)
    return pl.CostEstimate(flops=flops // 64, bytes_accessed=size // 64, transcendentals=0)


def own_gate(gate_rows, expert_num):
    lane = lax.broadcasted_iota(jnp.int32, gate_rows.shape, 1)
    kept = jnp.where(lane == expert_num, gate_rows.astype(F32), 0.0)
    return jnp.sum(kept, axis=1, keepdims=True)


def pack_kernel(tok_ref, ids_ref, gates_ref, out_ref):
    rows, width = tok_ref.shape
    out_ref[:, :width] = tok_ref[...]
    lane = lax.broadcasted_iota(jnp.int32, (rows, LANES), 1)
    ids, gates = ids_ref[...], gates_ref[...].astype(F32)
    total = jnp.zeros((rows, LANES), F32)
    for k in range(ids.shape[1]):
        total = total + jnp.where(ids[:, k : k + 1] == lane, gates[:, k : k + 1], 0.0)
    out_ref[:, width:] = total.astype(BF16)


def packed(tokens, ids, gates):
    rows, width = tokens.shape
    return pl.pallas_call(
        pack_kernel,
        out_shape=jax.ShapeDtypeStruct((rows, width + LANES), BF16),
        compiler_params=SMALL,
    )(tokens, ids, gates)


def hidden_kernel(blocks, *refs):
    me_ref = refs[0]
    toks, cots = refs[1 : 1 + blocks], refs[1 + blocks : 1 + 2 * blocks]
    wg_hbm, wu_hbm, wd_hbm = refs[1 + 2 * blocks : 4 + 2 * blocks]
    act_ref, hid_ref, og_hbm = refs[4 + 2 * blocks : 7 + 2 * blocks]
    rows, gates, cot, wide, down, og, sems = refs[7 + 2 * blocks :]
    each, width = cots[0].shape
    hid = wg_hbm.shape[1]

    def copy(source, target, number):
        made = pltpu.make_async_copy(source, target, sems.at[number])
        made.start()
        return made

    def at(i):
        return pl.ds(i * each, each)

    step = width // CHUNKS
    tok_copies = [copy(toks[i].at[:, :width], rows.at[at(i), :], 3 * i) for i in range(blocks)]
    wide_copies = []
    for j in range(CHUNKS):
        part = pl.ds(j * step, step)
        number = 3 * blocks + 1 + 2 * j
        wide_copies.append(copy(wg_hbm.at[part, :], wide.at[part, :hid], number))
        wide_copies.append(copy(wu_hbm.at[part, :], wide.at[part, hid:], number + 1))
    second = []
    for i in range(blocks):
        second.append(copy(toks[i].at[:, width:], gates.at[at(i), :], 3 * i + 1))
        second.append(copy(cots[i], cot.at[at(i), :], 3 * i + 2))
    second.append(copy(wd_hbm, down, 3 * blocks))
    for made in tok_copies:
        made.wait()
    pre = None
    for j in range(CHUNKS):
        wide_copies[2 * j].wait()
        wide_copies[2 * j + 1].wait()
        part = slice(j * step, (j + 1) * step)
        more = jnp.dot(rows[:, part], wide[part, :], preferred_element_type=F32)
        pre = more if pre is None else pre + more
    for made in second:
        made.wait()
    og[...] = (own_gate(gates[...], me_ref[0]) * cot[...].astype(F32)).astype(BF16)
    out = pltpu.make_async_copy(og, og_hbm, sems.at[0])
    out.start()
    act_grad = lax.dot_general(og[...], down[...], NT, preferred_element_type=F32)
    pre_gate, pre_up = pre[:, :hid], pre[:, hid:]
    s = 1.0 / (1.0 + jnp.exp(-pre_gate))
    act_ref[...] = (pre_gate * s * pre_up).astype(BF16)
    hid_ref[:, :hid] = (act_grad * pre_up * s * (1.0 + pre_gate * (1.0 - s))).astype(BF16)
    hid_ref[:, hid:] = (act_grad * pre_gate * s).astype(BF16)
    out.wait()


def hidden(me, toks, cots, wg, wu, wd):
    blocks = len(toks)
    each = cots[0].shape[0]
    rows = blocks * each
    width, hid = wg.shape
    shapes = [(rows, hid), (rows, 2 * hid)]
    outs = tuple(jax.ShapeDtypeStruct(s, BF16) for s in shapes + [(rows, width)])
    specs = tuple(pl.BlockSpec(s, lambda i: (0, 0)) for s in shapes) + (ANY,)
    return pl.pallas_call(
        functools.partial(hidden_kernel, blocks),
        out_shape=outs,
        grid=(1,),
        in_specs=[SMEM] + [ANY] * (2 * blocks + 3),
        out_specs=specs,
        scratch_shapes=[
            pltpu.VMEM((rows, width), BF16),
            pltpu.VMEM((rows, LANES), BF16),
            pltpu.VMEM((rows, width), BF16),
            pltpu.VMEM((width, 2 * hid), BF16),
            pltpu.VMEM((hid, width), BF16),
            pltpu.VMEM((rows, width), BF16),
            pltpu.SemaphoreType.DMA((3 * blocks + 1 + 2 * CHUNKS,)),
        ],
        compiler_params=MEDIUM,
        cost_estimate=cost(6 * rows * width * hid, (*toks, *cots, wg, wu, wd) + outs),
    )(me, *toks, *cots, wg, wu, wd)


def rows_kernel(blocks, groups, places, more, *refs):
    me_ref, gates, refs = refs[0], refs[1 : 1 + blocks], refs[1 + blocks :]
    acts, hids, refs = refs[:groups], refs[groups : 2 * groups], refs[2 * groups :]
    wg_ref, wu_ref, wd_ref = refs[:3]
    added, outs = refs[3 : 3 + more], refs[3 + more :]
    gate_col = own_gate(jnp.concatenate([g[...] for g in gates], axis=0), me_ref[0])
    each = gates[0].shape[0]
    hid = wg_ref.shape[1]

    def put(values, number):
        for i in range(blocks):
            piece = values[i * each : (i + 1) * each]
            if more:
                other = added[number][i * each : (i + 1) * each, :]
                piece = (piece.astype(F32) + other.astype(F32)).astype(BF16)
            array, block = places[number][i]
            outs[array][block * each : (block + 1) * each, :] = piece

    act = jnp.concatenate([a[...] for a in acts], axis=0)
    expert_out = jnp.dot(act, wd_ref[...], preferred_element_type=F32)
    put((gate_col * expert_out).astype(BF16), 0)
    hidden_grads = jnp.concatenate([h[...] for h in hids], axis=0)
    grad = lax.dot_general(hidden_grads[:, :hid], wg_ref[...], NT, preferred_element_type=F32)
    grad = grad + lax.dot_general(hidden_grads[:, hid:], wu_ref[...], NT, preferred_element_type=F32)
    put(grad.astype(BF16), 1)


def rows_out(me, gate_arrays, acts, hids, part, wg, wu, wd, added, places):
    blocks, groups = len(gate_arrays), len(acts)
    each = gate_arrays[0].shape[0]
    width, hid = wg.shape
    tile = width // 4
    flat = places[0] + places[1]
    sizes = [sum(array == k for array, _ in flat) for k in range(1 + max(array for array, _ in flat))]
    outs = tuple(jax.ShapeDtypeStruct((n * each, width), BF16) for n in sizes)
    gate_spec = pl.BlockSpec((each, LANES), lambda i: (0, width // LANES))
    column = lambda a: pl.BlockSpec((a.shape[0], tile), lambda i: (0, i))
    row = lambda a: pl.BlockSpec((tile, a.shape[1]), lambda i: (i, 0))
    return pl.pallas_call(
        functools.partial(rows_kernel, blocks, groups, places, len(added)),
        out_shape=outs,
        grid=(4,),
        in_specs=[SMEM]
        + [gate_spec] * blocks
        + [pl.BlockSpec((a.shape[0] // 2, a.shape[1]), lambda i: (part, 0)) for a in (*acts, *hids)]
        + [row(wg), row(wu), column(wd)]
        + [column(a) for a in added],
        out_specs=tuple(column(o) for o in outs),
        compiler_params=MEDIUM,
        cost_estimate=cost(6 * blocks * each * width * hid, (wg, wu, wd) + outs),
    )(me, *gate_arrays, *acts, *hids, wg, wu, wd, *added)


TN = (((0,), (0,)), ((), ()))


def wide_grad_kernel(blocks, count, order_ref, *refs):
    toks, hids, outs = refs[:blocks], refs[blocks:-count], refs[-count:]
    rows = jnp.concatenate([t[...] for t in toks], axis=0)
    hidden_grads = jnp.concatenate([h[...] for h in hids], axis=0)
    total = lax.dot_general(rows, hidden_grads, TN, preferred_element_type=F32).astype(BF16)
    for k in range(count):

        @pl.when(pl.program_id(0) == k)
        def _():
            outs[k][...] = total


def wide_grads(order, toks, hids, width, first, count):
    blocks = len(toks)
    each = toks[0].shape[0]
    both, tile = hids[0].shape[1], width // 4
    out = jax.ShapeDtypeStruct((tile, both), BF16)
    return pl.pallas_call(
        functools.partial(wide_grad_kernel, blocks, count),
        out_shape=(out,) * count,
        grid_spec=pltpu.PrefetchScalarGridSpec(
            num_scalar_prefetch=1,
            grid=(count,),
            in_specs=[pl.BlockSpec((each, tile), lambda i, order: (0, order[first + i]))] * blocks
            + [pl.BlockSpec(h.shape, lambda i, order: (0, 0)) for h in hids],
            out_specs=(pl.BlockSpec(out.shape, lambda i, order: (0, 0)),) * count,
        ),
        compiler_params=MEDIUM,
        cost_estimate=cost(2 * count * blocks * each * both * tile, tuple(hids) + (out,) * count),
    )(order, *toks, *hids)


def down_grad_kernel(groups, order_ref, *refs):
    acts, ogs, outs, full = refs[:groups], refs[groups : 2 * groups], refs[2 * groups : -1], refs[-1]
    act = jnp.concatenate([a[...] for a in acts], axis=0)
    og = jnp.concatenate([o[...] for o in ogs], axis=0)
    full[...] = lax.dot_general(act, og, TN, preferred_element_type=F32)
    size = full.shape[0] // 4
    for k in range(4):
        at = pl.multiple_of(order_ref[k] * size, size)
        outs[k][...] = full[pl.ds(at, size), :].astype(BF16)


def down_grads(order, acts, ogs):
    hid = acts[0].shape[1]
    rows = sum(a.shape[0] for a in acts)
    width = ogs[0].shape[1]
    tile = width // 4
    out = jax.ShapeDtypeStruct((hid // 4, width), BF16)
    return pl.pallas_call(
        functools.partial(down_grad_kernel, len(acts)),
        out_shape=(out,) * 4,
        grid_spec=pltpu.PrefetchScalarGridSpec(
            num_scalar_prefetch=1,
            grid=(width // tile,),
            in_specs=[pl.BlockSpec(a.shape, lambda i, order: (0, 0)) for a in acts]
            + [pl.BlockSpec((o.shape[0], tile), lambda i, order: (0, i)) for o in ogs],
            out_specs=(pl.BlockSpec((hid // 4, tile), lambda i, order: (0, i)),) * 4,
            scratch_shapes=[pltpu.VMEM((hid, tile), F32)],
        ),
        compiler_params=MEDIUM,
        cost_estimate=cost(2 * rows * hid * width, tuple(acts) + tuple(ogs)),
    )(order, *acts, *ogs)


PIECE = 256


def pieces(wide_shape, down_shape):
    at = 0
    for number, (rows, columns) in enumerate((wide_shape, down_shape)):
        for j in range(columns // PIECE):
            yield number, slice(at, at + rows), slice(j * PIECE, (j + 1) * PIECE)
            at += rows


def join_kernel(joined, mid_ref, wide_own, down_own, *refs):
    came, out_ref = refs[:-1], refs[-1]
    owns = wide_own, down_own
    for number, rows, part in pieces(wide_own.shape, down_own.shape):
        other = came[0][rows, :] if joined else came[number][:, part]
        other = jnp.where(mid_ref[0] == 1, other.astype(F32), 0.0)
        out_ref[rows, :] = (owns[number][:, part].astype(F32) + other).astype(BF16)


def join(mid, wide_own, down_own, *came):
    out = jax.ShapeDtypeStruct(((wide_own.size + down_own.size) // PIECE, PIECE), BF16)
    return pl.pallas_call(
        functools.partial(join_kernel, len(came) == 1),
        out_shape=out,
        in_specs=[SMEM] + [pl.BlockSpec(memory_space=pltpu.VMEM)] * (2 + len(came)),
        compiler_params=SMALL,
        cost_estimate=cost(wide_own.size, (out,)),
    )(mid, wide_own, down_own, *came)


def base_kernel(mid_ref, wide_own, down_own, wide_one, down_one, two_ref, wide_out, down_out):
    owns, ones, outs = (wide_own, down_own), (wide_one, down_one), (wide_out, down_out)
    for number, rows, part in pieces(wide_own.shape, down_own.shape):
        came = ones[number][:, part].astype(F32) + two_ref[rows, :].astype(F32)
        came = jnp.where(mid_ref[0] == 1, 0.0, came)
        outs[number][:, part] = owns[number][:, part].astype(F32) + came


def base_terms(mid, wide_own, down_own, wide_one, down_one, two):
    outs = tuple(jax.ShapeDtypeStruct(a.shape, F32) for a in (wide_own, down_own))
    return pl.pallas_call(
        base_kernel,
        out_shape=outs,
        in_specs=[SMEM] + [pl.BlockSpec(memory_space=pltpu.VMEM)] * 5,
        compiler_params=SMALL,
        cost_estimate=cost(wide_own.size, outs),
    )(mid, wide_own, down_own, wide_one, down_one, two)


def finish_kernel(wide_ref, down_ref, up_ref, low_ref, gate_out, up_out, down_out):
    bases, outs = (wide_ref, down_ref), ((gate_out, up_out), (down_out,))
    for number, rows, part in pieces(wide_ref.shape, down_ref.shape):
        came = up_ref[rows, :].astype(F32) + low_ref[rows, :].astype(F32)
        total = bases[number][:, part] + came
        for k, out in enumerate(outs[number]):
            size = out.shape[1]
            a, b = max(part.start, k * size), min(part.stop, (k + 1) * size)
            if a < b:
                out[:, a - k * size : b - k * size] = total[:, a - part.start : b - part.start]


def finish(wide, down, one, two):
    rows, both = wide.shape
    outs = (jax.ShapeDtypeStruct((rows, both // 2), F32),) * 2 + (jax.ShapeDtypeStruct(down.shape, F32),)
    return pl.pallas_call(
        finish_kernel,
        out_shape=outs,
        compiler_params=SMALL,
        cost_estimate=cost(wide.size, outs),
    )(wide, down, one, two)


def after(values, earlier):
    return lax.optimization_barrier((values, earlier))[0]


def pair_sums_kernel(count, *refs):
    for k, out_ref in enumerate(refs[-2:]):
        terms = [r[...].astype(F32) for r in refs[k * count : (k + 1) * count]]
        out_ref[...] = sum(terms[1:], terms[0]).astype(BF16)


def pair_sums(each, first, second):
    width = first[0][0].shape[1]
    tile = each // 4
    spec = lambda block: pl.BlockSpec((tile, width), lambda i: (4 * block + i, 0))
    out = jax.ShapeDtypeStruct((each, width), BF16)
    return pl.pallas_call(
        functools.partial(pair_sums_kernel, len(first)),
        out_shape=(out, out),
        grid=(4,),
        in_specs=[spec(block) for _, block in first + second],
        out_specs=(spec(0), spec(0)),
        compiler_params=SMALL,
        cost_estimate=cost(out.size, (out,)),
    )(*[a for a, _ in first + second])


LINE_ORDER = ((3, 2, 1, 0), (0, 3, 2, 1), (3, 0, 1, 2), (0, 1, 2, 3))


def per_device(tokens, expert_ids, gates, w_gate, w_up, w_down, cotangent):
    width = tokens.shape[1]
    group = lax.axis_size("expert")
    shards = lax.axis_size("dp")
    assert group == 8
    me = lax.axis_index("expert").astype(jnp.int32).reshape(1)
    z = lax.axis_index("dp")
    wg, wu, wd = w_gate[0], w_up[0], w_down[0]

    def flip(array, bit):
        return lax.ppermute(array, "expert", [(i, i ^ bit) for i in range(group)])

    cot_0 = cotangent
    tok_0 = packed(tokens, expert_ids, gates)
    tok_x, cot_y = flip(tok_0, NEAR), flip(cot_0, FAR)
    cot_x, tok_y = flip(cot_0, NEAR), flip(tok_0, FAR)
    cot_d, tok_d = flip(cot_y, NEAR), flip(tok_x, FAR)

    toks_a, cots_a = [tok_0, tok_x, tok_y], [cot_0, cot_x, cot_y]
    toks_a += [flip(t, CORE) for t in toks_a]
    cots_a += [flip(c, CORE) for c in cots_a]
    act_a, hid_a, og_a = hidden(me, toks_a, cots_a, wg, wu, wd)
    tok_d, cot_d = after((tok_d, cot_d), act_a)
    toks_b, cots_b = [tok_d, flip(tok_d, CORE)], [cot_d, flip(cot_d, CORE)]
    act_b, hid_b, og_b = hidden(me, toks_b, cots_b, wg, wu, wd)

    line = shards == 4
    table = jnp.asarray(LINE_ORDER if line else ((0, 1, 2, 3),), jnp.int32)
    order = table[z if line else 0]
    mid = (z == 1) | (z == 2)

    def move(array, pairs):
        return lax.ppermute(array, "dp", pairs) if line else array

    one_pairs = [(0, 1), (1, 0), (2, 3), (3, 2)]
    two_pairs = [(0, 1), (1, 3), (3, 2), (2, 0)]
    up_pairs, down_pairs = [(0, 1), (1, 2)], [(3, 2), (2, 1)]
    toks, hids = toks_a + toks_b, (hid_a, hid_b)
    wide_0 = wide_grads(order, toks, hids, width, 0, 1)
    wide_one = move(wide_0[0], one_pairs)
    act_a = after(act_a, wide_0)
    down = down_grads(order, (act_a, act_b), (og_a, og_b))
    down_one = move(down[0], one_pairs)
    hid_a = after(hid_a, down)
    wide = wide_0 + wide_grads(order, toks, (hid_a, hid_b), width, 1, 3)
    act_a = after(act_a, wide[1])
    acts, hids = (act_a, act_b), (hid_a, hid_b)
    there = tuple((0, i) for i in range(4)), tuple((1, i) for i in range(4))
    sent = rows_out(me, toks_a[3:] + toks_b[1:], acts, hids, 1, wg, wu, wd, (), there)
    if line:
        mid_number = mid.astype(jnp.int32).reshape(1)
        wide_one, down_one = after((wide_one, down_one), sent)
        second = join(mid_number, wide[1], down[1], wide_one, down_one)
        two = move(second, two_pairs)
        sent = after(sent, second)
    sent = [flip(a, CORE) for a in sent]
    here = ((0, 0), (2, 0), (1, 0), (2, 1)), ((3, 0), (4, 0), (5, 0), (5, 1))
    kept = rows_out(me, toks_a[:3] + toks_b[:1], acts, hids, 0, wg, wu, wd, sent, here)
    out_0, out_y, out_near, grad_0, grad_x, grad_far = kept
    out_near, grad_far = flip(out_near, NEAR), flip(grad_far, FAR)
    hid_size = wd.shape[0]
    each = tokens.shape[0]
    if line:
        two = after(two, kept)
        last = join(mid_number, wide[2], down[2], two)
        last_up, last_down = move(last, up_pairs), move(last, down_pairs)
        out_near, grad_far = after((out_near, grad_far), last)
    out_y, grad_x = pair_sums(each, [(out_y, 0), (out_near, 1)], [(grad_x, 0), (grad_far, 1)])
    out_yy, grad_xx = flip(out_y, FAR), flip(grad_x, NEAR)
    if line:
        base = base_terms(mid_number, wide[3], down[3], wide_one, down_one, after(two, (out_y, grad_x)))
    mixed, grad_tokens = pair_sums(
        each, [(out_0, 0), (out_near, 0), (out_yy, 0)], [(grad_0, 0), (grad_far, 0), (grad_xx, 0)]
    )
    if line:
        base, mixed, grad_tokens = lax.optimization_barrier((base, mixed, grad_tokens))
        last_up, last_down = after((last_up, last_down), (mixed, grad_tokens))
        grad_gate, grad_up, grad_down = finish(*base, last_up, last_down)
    else:
        wide_all = jnp.concatenate(wide, axis=0)
        grad_wide = lax.psum_scatter(wide_all, "dp", scatter_dimension=0, tiled=True).astype(F32)
        grad_gate, grad_up = grad_wide[:, :hid_size], grad_wide[:, hid_size:]
        grad_down = lax.psum_scatter(jnp.concatenate(down, axis=0), "dp", scatter_dimension=0, tiled=True).astype(F32)
    return (mixed, grad_tokens, grad_gate[None], grad_up[None], grad_down[None])


def solution(mesh):
    return jax.shard_map(
        per_device,
        mesh=mesh,
        in_specs=(
            P(("dp", "expert"), None),
            P(("dp", "expert"), None),
            P(("dp", "expert"), None),
            P("expert", None, None),
            P("expert", None, None),
            P("expert", None, None),
            P(("dp", "expert"), None),
        ),
        out_specs=(
            P(("dp", "expert"), None),
            P(("dp", "expert"), None),
            P("expert", "dp", None),
            P("expert", "dp", None),
            P("expert", "dp", None),
        ),
        check_vma=False,
    )
```

```python
import functools

import jax
import jax.numpy as jnp
from jax import lax
from jax.experimental import pallas as pl
from jax.experimental.pallas import tpu as pltpu
from jax.sharding import PartitionSpec as P

F32 = jnp.float32
BF16 = jnp.bfloat16
LANES = 128
CORE, NEAR, FAR = 1, 2, 4
MEDIUM = pltpu.CompilerParams(vmem_limit_bytes=32 * 1024 * 1024)
SMALL = pltpu.CompilerParams(vmem_limit_bytes=16 * 1024 * 1024)
VMEM = pl.BlockSpec(memory_space=pltpu.VMEM)
SMEM = pl.BlockSpec(memory_space=pltpu.SMEM)
NT = (((1,), (1,)), ((), ()))


def cost(flops, arrays):
    size = sum(a.size * a.dtype.itemsize for a in arrays)
    return pl.CostEstimate(flops=flops // 64, bytes_accessed=size // 64, transcendentals=0)


def own_gate(gate_rows, expert_num):
    lane = lax.broadcasted_iota(jnp.int32, gate_rows.shape, 1)
    kept = jnp.where(lane == expert_num, gate_rows.astype(F32), 0.0)
    return jnp.sum(kept, axis=1, keepdims=True)


def pack_kernel(tok_ref, ids_ref, gates_ref, out_ref):
    rows, width = tok_ref.shape
    out_ref[:, :width] = tok_ref[...]
    lane = lax.broadcasted_iota(jnp.int32, (rows, LANES), 1)
    ids, gates = ids_ref[...], gates_ref[...].astype(F32)
    total = jnp.zeros((rows, LANES), F32)
    for k in range(ids.shape[1]):
        total = total + jnp.where(ids[:, k : k + 1] == lane, gates[:, k : k + 1], 0.0)
    out_ref[:, width:] = total.astype(BF16)


def packed(tokens, ids, gates):
    rows, width = tokens.shape
    return pl.pallas_call(
        pack_kernel,
        out_shape=jax.ShapeDtypeStruct((rows, width + LANES), BF16),
        compiler_params=SMALL,
    )(tokens, ids, gates)


def panels_kernel(wg_ref, wu_ref, wd_ref, wide_ref, down_ref):
    hid = wg_ref.shape[1]
    wide_ref[:, :hid] = wg_ref[...]
    wide_ref[:, hid:] = wu_ref[...]
    down_ref[...] = wd_ref[...]


def panels(wg, wu, wd):
    width, hid = wg.shape
    outs = (jax.ShapeDtypeStruct((width, 2 * hid), BF16), jax.ShapeDtypeStruct(wd.shape, BF16))
    return pl.pallas_call(
        panels_kernel,
        out_shape=outs,
        in_specs=[VMEM] * 3,
        out_specs=(VMEM, VMEM),
        compiler_params=SMALL,
        cost_estimate=cost(width, outs),
    )(wg, wu, wd)


def hidden_kernel(blocks, me_ref, *refs):
    toks, cots = refs[:blocks], refs[blocks : 2 * blocks]
    wide_ref, down_ref, act_ref, hid_ref, og_ref = refs[2 * blocks :]
    each, width = cots[0].shape
    hid = down_ref.shape[0]
    rows = jnp.concatenate([t[:, :width] for t in toks], axis=0)
    pre = jnp.dot(rows, wide_ref[...], preferred_element_type=F32)
    for i in range(blocks):
        gate_col = own_gate(toks[i][:, width:], me_ref[0])
        og_ref[i * each : (i + 1) * each, :] = (gate_col * cots[i][...].astype(F32)).astype(BF16)
    act_grad = lax.dot_general(og_ref[...], down_ref[...], NT, preferred_element_type=F32)
    pre_gate, pre_up = pre[:, :hid], pre[:, hid:]
    s = 1.0 / (1.0 + jnp.exp(-pre_gate))
    act_ref[...] = (pre_gate * s * pre_up).astype(BF16)
    hid_ref[:, :hid] = (act_grad * pre_up * s * (1.0 + pre_gate * (1.0 - s))).astype(BF16)
    hid_ref[:, hid:] = (act_grad * pre_gate * s).astype(BF16)


def hidden(me, toks, cots, wide, down):
    blocks = len(toks)
    rows = blocks * cots[0].shape[0]
    hid, width = down.shape
    outs = tuple(jax.ShapeDtypeStruct((rows, n), BF16) for n in (hid, 2 * hid, width))
    return pl.pallas_call(
        functools.partial(hidden_kernel, blocks),
        out_shape=outs,
        in_specs=[SMEM] + [VMEM] * (2 * blocks + 2),
        out_specs=(VMEM,) * 3,
        compiler_params=MEDIUM,
        cost_estimate=cost(6 * rows * width * hid, (*toks, *cots, wide, down) + outs),
    )(me, *toks, *cots, wide, down)


def rows_kernel(blocks, groups, part, places, more, me_ref, *refs):
    toks, refs = refs[:blocks], refs[blocks:]
    acts, hids, refs = refs[:groups], refs[groups : 2 * groups], refs[2 * groups :]
    wide_ref, down_ref = refs[:2]
    added, outs = refs[2 : 2 + more], refs[2 + more :]
    width = down_ref.shape[1]
    each = toks[0].shape[0]
    gate_col = own_gate(jnp.concatenate([t[:, width:] for t in toks], axis=0), me_ref[0])

    def half(ref):
        size = ref.shape[0] // 2
        return ref[part * size : (part + 1) * size, :]

    def put(values, number, columns):
        for i in range(blocks):
            piece = values[i * each : (i + 1) * each]
            if more:
                other = added[number][i * each : (i + 1) * each, columns]
                piece = (piece.astype(F32) + other.astype(F32)).astype(BF16)
            array, block = places[number][i]
            outs[array][block * each : (block + 1) * each, columns] = piece

    act = jnp.concatenate([half(a) for a in acts], axis=0)
    hidden_grads = jnp.concatenate([half(h) for h in hids], axis=0)
    step = width // 4
    for j in range(4):
        columns = slice(j * step, (j + 1) * step)
        expert_out = jnp.dot(act, down_ref[:, columns], preferred_element_type=F32)
        put((gate_col * expert_out).astype(BF16), 0, columns)
        grad = lax.dot_general(hidden_grads, wide_ref[columns, :], NT, preferred_element_type=F32)
        put(grad.astype(BF16), 1, columns)


def rows_out(me, toks, acts, hids, part, wide, down, added, places):
    blocks, groups = len(toks), len(acts)
    each = toks[0].shape[0]
    hid, width = down.shape
    flat = places[0] + places[1]
    sizes = [sum(array == k for array, _ in flat) for k in range(1 + max(array for array, _ in flat))]
    outs = tuple(jax.ShapeDtypeStruct((n * each, width), BF16) for n in sizes)
    return pl.pallas_call(
        functools.partial(rows_kernel, blocks, groups, part, places, len(added)),
        out_shape=outs,
        in_specs=[SMEM] + [VMEM] * (blocks + 2 * groups + 2 + len(added)),
        out_specs=(VMEM,) * len(outs),
        compiler_params=MEDIUM,
        cost_estimate=cost(6 * blocks * each * width * hid, (wide, down) + outs),
    )(me, *toks, *acts, *hids, wide, down, *added)


TN = (((0,), (0,)), ((), ()))


def wide_grad_kernel(blocks, first, count, order_ref, *refs):
    toks, hids, outs = refs[:blocks], refs[blocks:-count], refs[-count:]
    hidden_grads = jnp.concatenate([h[...] for h in hids], axis=0)
    tile = outs[0].shape[0]
    for k in range(count):
        at = pl.multiple_of(order_ref[first + k] * tile, tile)
        rows = jnp.concatenate([t[:, pl.ds(at, tile)] for t in toks], axis=0)
        outs[k][...] = lax.dot_general(rows, hidden_grads, TN, preferred_element_type=F32).astype(BF16)


def wide_grads(order, toks, hids, width, first, count):
    blocks = len(toks)
    each = toks[0].shape[0]
    both, tile = hids[0].shape[1], width // 4
    out = jax.ShapeDtypeStruct((tile, both), BF16)
    return pl.pallas_call(
        functools.partial(wide_grad_kernel, blocks, first, count),
        out_shape=(out,) * count,
        in_specs=[SMEM] + [VMEM] * (blocks + len(hids)),
        out_specs=(VMEM,) * count,
        compiler_params=MEDIUM,
        cost_estimate=cost(2 * count * blocks * each * both * tile, tuple(hids) + (out,) * count),
    )(order, *toks, *hids)


def down_grad_kernel(groups, order_ref, *refs):
    acts, ogs, outs, full = refs[:groups], refs[groups : 2 * groups], refs[2 * groups : -1], refs[-1]
    act = jnp.concatenate([a[...] for a in acts], axis=0)
    step = full.shape[1]
    size = full.shape[0] // 4
    for j in range(4):
        columns = slice(j * step, (j + 1) * step)
        og = jnp.concatenate([o[:, columns] for o in ogs], axis=0)
        full[...] = lax.dot_general(act, og, TN, preferred_element_type=F32)
        for k in range(4):
            at = pl.multiple_of(order_ref[k] * size, size)
            outs[k][:, columns] = full[pl.ds(at, size), :].astype(BF16)


def down_grads(order, acts, ogs):
    hid = acts[0].shape[1]
    rows = sum(a.shape[0] for a in acts)
    width = ogs[0].shape[1]
    out = jax.ShapeDtypeStruct((hid // 4, width), BF16)
    return pl.pallas_call(
        functools.partial(down_grad_kernel, len(acts)),
        out_shape=(out,) * 4,
        in_specs=[SMEM] + [VMEM] * (2 * len(acts)),
        out_specs=(VMEM,) * 4,
        scratch_shapes=[pltpu.VMEM((hid, width // 4), F32)],
        compiler_params=MEDIUM,
        cost_estimate=cost(2 * rows * hid * width, tuple(acts) + tuple(ogs)),
    )(order, *acts, *ogs)


PIECE = 256


def pieces(wide_shape, down_shape):
    at = 0
    for number, (rows, columns) in enumerate((wide_shape, down_shape)):
        for j in range(columns // PIECE):
            yield number, slice(at, at + rows), slice(j * PIECE, (j + 1) * PIECE)
            at += rows


def join_kernel(joined, order_ref, wide_own, down_own, *refs):
    came, out_ref = refs[:-1], refs[-1]
    owns = wide_own, down_own
    for number, rows, part in pieces(wide_own.shape, down_own.shape):
        other = came[0][rows, :] if joined else came[number][:, part]
        other = jnp.where(order_ref[4] == 1, other.astype(F32), 0.0)
        out_ref[rows, :] = (owns[number][:, part].astype(F32) + other).astype(BF16)


def join(order, wide_own, down_own, *came):
    out = jax.ShapeDtypeStruct(((wide_own.size + down_own.size) // PIECE, PIECE), BF16)
    return pl.pallas_call(
        functools.partial(join_kernel, len(came) == 1),
        out_shape=out,
        in_specs=[SMEM] + [VMEM] * (2 + len(came)),
        compiler_params=SMALL,
        cost_estimate=cost(wide_own.size, (out,)),
    )(order, wide_own, down_own, *came)


def base_kernel(order_ref, wide_own, down_own, wide_one, down_one, two_ref, wide_out, down_out):
    owns, ones, outs = (wide_own, down_own), (wide_one, down_one), (wide_out, down_out)
    for number, rows, part in pieces(wide_own.shape, down_own.shape):
        came = ones[number][:, part].astype(F32) + two_ref[rows, :].astype(F32)
        came = jnp.where(order_ref[4] == 1, 0.0, came)
        outs[number][:, part] = owns[number][:, part].astype(F32) + came


def base_terms(order, wide_own, down_own, wide_one, down_one, two):
    outs = tuple(jax.ShapeDtypeStruct(a.shape, F32) for a in (wide_own, down_own))
    return pl.pallas_call(
        base_kernel,
        out_shape=outs,
        in_specs=[SMEM] + [VMEM] * 5,
        compiler_params=SMALL,
        cost_estimate=cost(wide_own.size, outs),
    )(order, wide_own, down_own, wide_one, down_one, two)


def finish_kernel(wide_ref, down_ref, up_ref, low_ref, gate_out, up_out, down_out):
    bases, outs = (wide_ref, down_ref), ((gate_out, up_out), (down_out,))
    for number, rows, part in pieces(wide_ref.shape, down_ref.shape):
        came = up_ref[rows, :].astype(F32) + low_ref[rows, :].astype(F32)
        total = bases[number][:, part] + came
        for k, out in enumerate(outs[number]):
            size = out.shape[1]
            a, b = max(part.start, k * size), min(part.stop, (k + 1) * size)
            if a < b:
                out[:, a - k * size : b - k * size] = total[:, a - part.start : b - part.start]


def finish(wide, down, one, two):
    rows, both = wide.shape
    outs = (jax.ShapeDtypeStruct((rows, both // 2), F32),) * 2 + (jax.ShapeDtypeStruct(down.shape, F32),)
    return pl.pallas_call(
        finish_kernel,
        out_shape=outs,
        compiler_params=SMALL,
        cost_estimate=cost(wide.size, outs),
    )(wide, down, one, two)


def after(values, earlier):
    return lax.optimization_barrier((values, earlier))[0]


def pair_sums_kernel(places, *refs):
    for terms, out_ref in zip(places, refs[-2:]):
        each = out_ref.shape[0]
        values = [refs[k][block * each : (block + 1) * each, :].astype(F32) for k, block in terms]
        out_ref[...] = sum(values[1:], values[0]).astype(BF16)


def pair_sums(each, first, second):
    arrays = [a for a, _ in first + second]
    blocks = [block for _, block in first + second]
    numbered = tuple(enumerate(blocks))
    out = jax.ShapeDtypeStruct((each, arrays[0].shape[1]), BF16)
    return pl.pallas_call(
        functools.partial(pair_sums_kernel, (numbered[: len(first)], numbered[len(first) :])),
        out_shape=(out, out),
        in_specs=[VMEM] * len(arrays),
        out_specs=(VMEM, VMEM),
        compiler_params=SMALL,
        cost_estimate=cost(out.size, (out,)),
    )(*arrays)


LINE_ORDER = ((3, 2, 1, 0, 0), (0, 3, 2, 1, 1), (3, 0, 1, 2, 1), (0, 1, 2, 3, 0))


def per_device(tokens, expert_ids, gates, w_gate, w_up, w_down, cotangent):
    width = tokens.shape[1]
    group = lax.axis_size("expert")
    shards = lax.axis_size("dp")
    assert group == 8
    me = lax.axis_index("expert").astype(jnp.int32).reshape(1)
    z = lax.axis_index("dp")
    wg, wu, wd = w_gate[0], w_up[0], w_down[0]

    def flip(array, bit):
        return lax.ppermute(array, "expert", [(i, i ^ bit) for i in range(group)])

    line = shards == 4
    table = jnp.asarray(LINE_ORDER if line else ((0, 1, 2, 3, 0),), jnp.int32)
    order = table[z if line else 0]
    tokens = after(tokens, order)
    cot_0 = cotangent
    tok_0 = packed(tokens, expert_ids, gates)
    tok_x, cot_y = flip(tok_0, NEAR), flip(cot_0, FAR)
    cot_x, tok_y = flip(cot_0, NEAR), flip(tok_0, FAR)
    cot_d, tok_d = flip(cot_y, NEAR), flip(tok_x, FAR)

    toks_a, cots_a = [tok_0, tok_x, tok_y], [cot_0, cot_x, cot_y]
    wide_panel, down_panel = panels(wg, wu, wd)
    cots_a += [flip(c, CORE) for c in [after(cot_0, wide_panel)] + cots_a[1:]]
    toks_a += [flip(t, CORE) for t in toks_a]
    act_a, hid_a, og_a = hidden(me, toks_a, cots_a, wide_panel, down_panel)
    tok_d, cot_d = after((tok_d, cot_d), act_a)
    toks_b, cots_b = [tok_d, flip(tok_d, CORE)], [cot_d, flip(cot_d, CORE)]
    act_b, hid_b, og_b = hidden(me, toks_b, cots_b, wide_panel, down_panel)

    def move(array, pairs):
        return lax.ppermute(array, "dp", pairs) if line else array

    one_pairs = [(0, 1), (1, 0), (2, 3), (3, 2)]
    two_pairs = [(0, 1), (1, 3), (3, 2), (2, 0)]
    up_pairs, down_pairs = [(0, 1), (1, 2)], [(3, 2), (2, 1)]
    toks, hids = toks_a + toks_b, (hid_a, hid_b)
    wide_0 = wide_grads(order, toks, hids, width, 0, 1)
    wide_one = move(wide_0[0], one_pairs)
    act_a = after(act_a, wide_0)
    down = down_grads(order, (act_a, act_b), (og_a, og_b))
    down_one = move(down[0], one_pairs)
    hid_a = after(hid_a, down)
    wide = wide_0 + wide_grads(order, toks, (hid_a, hid_b), width, 1, 3)
    act_a = after(act_a, wide[1])
    acts, hids = (act_a, act_b), (hid_a, hid_b)
    there = tuple((0, i) for i in range(4)), tuple((1, i) for i in range(4))
    sent = rows_out(me, toks_a[3:] + toks_b[1:], acts, hids, 1, wide_panel, down_panel, (), there)
    if line:
        wide_one, down_one = after((wide_one, down_one), sent)
        second = join(order, wide[1], down[1], wide_one, down_one)
        two = move(second, two_pairs)
        sent = after(sent, second)
    sent = [flip(a, CORE) for a in sent]
    here = ((0, 0), (2, 0), (1, 0), (2, 1)), ((3, 0), (4, 0), (5, 0), (5, 1))
    kept = rows_out(me, toks_a[:3] + toks_b[:1], acts, hids, 0, wide_panel, down_panel, sent, here)
    out_0, out_y, out_near, grad_0, grad_x, grad_far = kept
    out_near, grad_far = flip(out_near, NEAR), flip(grad_far, FAR)
    hid_size = wd.shape[0]
    each = tokens.shape[0]
    if line:
        two = after(two, kept)
        last = join(order, wide[2], down[2], two)
        last_up, last_down = move(last, up_pairs), move(last, down_pairs)
        out_near, grad_far = after((out_near, grad_far), last)
    out_y, grad_x = pair_sums(each, [(out_y, 0), (out_near, 1)], [(grad_x, 0), (grad_far, 1)])
    out_yy, grad_xx = flip(out_y, FAR), flip(grad_x, NEAR)
    if line:
        base = base_terms(order, wide[3], down[3], wide_one, down_one, after(two, (out_y, grad_x)))
    mixed, grad_tokens = pair_sums(
        each, [(out_0, 0), (out_near, 0), (out_yy, 0)], [(grad_0, 0), (grad_far, 0), (grad_xx, 0)]
    )
    if line:
        base, mixed, grad_tokens = lax.optimization_barrier((base, mixed, grad_tokens))
        last_up, last_down = after((last_up, last_down), (mixed, grad_tokens))
        grad_gate, grad_up, grad_down = finish(*base, last_up, last_down)
    else:
        wide_all = jnp.concatenate(wide, axis=0)
        grad_wide = lax.psum_scatter(wide_all, "dp", scatter_dimension=0, tiled=True).astype(F32)
        grad_gate, grad_up = grad_wide[:, :hid_size], grad_wide[:, hid_size:]
        grad_down = lax.psum_scatter(jnp.concatenate(down, axis=0), "dp", scatter_dimension=0, tiled=True).astype(F32)
    return (mixed, grad_tokens, grad_gate[None], grad_up[None], grad_down[None])


def solution(mesh):
    return jax.shard_map(
        per_device,
        mesh=mesh,
        in_specs=(
            P(("dp", "expert"), None),
            P(("dp", "expert"), None),
            P(("dp", "expert"), None),
            P("expert", None, None),
            P("expert", None, None),
            P("expert", None, None),
            P(("dp", "expert"), None),
        ),
        out_specs=(
            P(("dp", "expert"), None),
            P(("dp", "expert"), None),
            P("expert", "dp", None),
            P("expert", "dp", None),
            P("expert", "dp", None),
        ),
        check_vma=False,
    )
```

```python
import functools

import jax
import jax.numpy as jnp
from jax import lax
from jax.experimental import pallas as pl
from jax.experimental.pallas import tpu as pltpu
from jax.sharding import PartitionSpec as P

F32 = jnp.float32
BF16 = jnp.bfloat16
LANES = 128
CORE, NEAR, FAR = 1, 2, 4
MEDIUM = pltpu.CompilerParams(vmem_limit_bytes=24 * 1024 * 1024)
SMALL = pltpu.CompilerParams(vmem_limit_bytes=12 * 1024 * 1024)
VMEM = pl.BlockSpec(memory_space=pltpu.VMEM)
SMEM = pl.BlockSpec(memory_space=pltpu.SMEM)
NT = (((1,), (1,)), ((), ()))


def cost(flops, arrays):
    size = sum(a.size * a.dtype.itemsize for a in arrays)
    return pl.CostEstimate(flops=flops // 64, bytes_accessed=size // 64, transcendentals=0)


def own_gate(gate_rows, expert_num):
    lane = lax.broadcasted_iota(jnp.int32, gate_rows.shape, 1)
    kept = jnp.where(lane == expert_num, gate_rows.astype(F32), 0.0)
    return jnp.sum(kept, axis=1, keepdims=True)


def pack_kernel(tok_ref, ids_ref, gates_ref, out_ref):
    rows, width = tok_ref.shape
    out_ref[:, :width] = tok_ref[...]
    lane = lax.broadcasted_iota(jnp.int32, (rows, LANES), 1)
    ids, gates = ids_ref[...], gates_ref[...].astype(F32)
    total = jnp.zeros((rows, LANES), F32)
    for k in range(ids.shape[1]):
        total = total + jnp.where(ids[:, k : k + 1] == lane, gates[:, k : k + 1], 0.0)
    out_ref[:, width:] = total.astype(BF16)


def packed(tokens, ids, gates):
    rows, width = tokens.shape
    return pl.pallas_call(
        pack_kernel,
        out_shape=jax.ShapeDtypeStruct((rows, width + LANES), BF16),
        compiler_params=SMALL,
    )(tokens, ids, gates)


def panels_kernel(wg_ref, wu_ref, wd_ref, wide_ref, down_ref):
    hid = wg_ref.shape[1]
    wide_ref[:, :hid] = wg_ref[...]
    wide_ref[:, hid:] = wu_ref[...]
    down_ref[...] = wd_ref[...]


def panels(wg, wu, wd):
    width, hid = wg.shape
    outs = (jax.ShapeDtypeStruct((width, 2 * hid), BF16), jax.ShapeDtypeStruct(wd.shape, BF16))
    return pl.pallas_call(
        panels_kernel,
        out_shape=outs,
        in_specs=[VMEM] * 3,
        out_specs=(VMEM, VMEM),
        compiler_params=SMALL,
        cost_estimate=cost(width, outs),
    )(wg, wu, wd)


def hidden_kernel(blocks, me_ref, *refs):
    toks, cots = refs[:blocks], refs[blocks : 2 * blocks]
    wide_ref, down_ref, act_ref, hid_ref, og_ref = refs[2 * blocks :]
    each, width = cots[0].shape
    hid = down_ref.shape[0]
    rows = jnp.concatenate([t[:, :width] for t in toks], axis=0)
    pre = jnp.dot(rows, wide_ref[...], preferred_element_type=F32)
    for i in range(blocks):
        gate_col = own_gate(toks[i][:, width:], me_ref[0])
        og_ref[i * each : (i + 1) * each, :] = (gate_col * cots[i][...].astype(F32)).astype(BF16)
    act_grad = lax.dot_general(og_ref[...], down_ref[...], NT, preferred_element_type=F32)
    pre_gate, pre_up = pre[:, :hid], pre[:, hid:]
    s = 1.0 / (1.0 + jnp.exp(-pre_gate))
    act_ref[...] = (pre_gate * s * pre_up).astype(BF16)
    hid_ref[:, :hid] = (act_grad * pre_up * s * (1.0 + pre_gate * (1.0 - s))).astype(BF16)
    hid_ref[:, hid:] = (act_grad * pre_gate * s).astype(BF16)


def hidden(me, toks, cots, wide, down):
    blocks = len(toks)
    rows = blocks * cots[0].shape[0]
    hid, width = down.shape
    outs = tuple(jax.ShapeDtypeStruct((rows, n), BF16) for n in (hid, 2 * hid, width))
    return pl.pallas_call(
        functools.partial(hidden_kernel, blocks),
        out_shape=outs,
        in_specs=[SMEM] + [VMEM] * (2 * blocks + 2),
        out_specs=(VMEM,) * 3,
        compiler_params=MEDIUM,
        cost_estimate=cost(6 * rows * width * hid, (*toks, *cots, wide, down) + outs),
    )(me, *toks, *cots, wide, down)


def rows_kernel(blocks, groups, part, places, more, me_ref, *refs):
    toks, refs = refs[:blocks], refs[blocks:]
    acts, hids, refs = refs[:groups], refs[groups : 2 * groups], refs[2 * groups :]
    wide_ref, down_ref = refs[:2]
    added, outs = refs[2 : 2 + more], refs[2 + more :]
    width = down_ref.shape[1]
    each = toks[0].shape[0]
    gate_col = own_gate(jnp.concatenate([t[:, width:] for t in toks], axis=0), me_ref[0])

    def half(ref):
        size = ref.shape[0] // 2
        return ref[part * size : (part + 1) * size, :]

    def put(values, number, columns):
        for i in range(blocks):
            piece = values[i * each : (i + 1) * each]
            if more:
                other = added[number][i * each : (i + 1) * each, columns]
                piece = (piece.astype(F32) + other.astype(F32)).astype(BF16)
            array, block = places[number][i]
            outs[array][block * each : (block + 1) * each, columns] = piece

    act = jnp.concatenate([half(a) for a in acts], axis=0)
    hidden_grads = jnp.concatenate([half(h) for h in hids], axis=0)
    step = width // 4
    for j in range(4):
        columns = slice(j * step, (j + 1) * step)
        expert_out = jnp.dot(act, down_ref[:, columns], preferred_element_type=F32)
        put((gate_col * expert_out).astype(BF16), 0, columns)
        grad = lax.dot_general(hidden_grads, wide_ref[columns, :], NT, preferred_element_type=F32)
        put(grad.astype(BF16), 1, columns)


def rows_out(me, toks, acts, hids, part, wide, down, added, places):
    blocks, groups = len(toks), len(acts)
    each = toks[0].shape[0]
    hid, width = down.shape
    flat = places[0] + places[1]
    sizes = [sum(array == k for array, _ in flat) for k in range(1 + max(array for array, _ in flat))]
    outs = tuple(jax.ShapeDtypeStruct((n * each, width), BF16) for n in sizes)
    return pl.pallas_call(
        functools.partial(rows_kernel, blocks, groups, part, places, len(added)),
        out_shape=outs,
        in_specs=[SMEM] + [VMEM] * (blocks + 2 * groups + 2 + len(added)),
        out_specs=(VMEM,) * len(outs),
        compiler_params=MEDIUM,
        cost_estimate=cost(6 * blocks * each * width * hid, (wide, down) + outs),
    )(me, *toks, *acts, *hids, wide, down, *added)


TN = (((0,), (0,)), ((), ()))


def wide_grad_kernel(blocks, first, count, order_ref, *refs):
    toks, hids, outs = refs[:blocks], refs[blocks:-count], refs[-count:]
    hidden_grads = jnp.concatenate([h[...] for h in hids], axis=0)
    tile = outs[0].shape[0]
    for k in range(count):
        at = pl.multiple_of(order_ref[first + k] * tile, tile)
        rows = jnp.concatenate([t[:, pl.ds(at, tile)] for t in toks], axis=0)
        outs[k][...] = lax.dot_general(rows, hidden_grads, TN, preferred_element_type=F32).astype(BF16)


def wide_grads(order, toks, hids, width, first, count):
    blocks = len(toks)
    each = toks[0].shape[0]
    both, tile = hids[0].shape[1], width // 4
    out = jax.ShapeDtypeStruct((tile, both), BF16)
    return pl.pallas_call(
        functools.partial(wide_grad_kernel, blocks, first, count),
        out_shape=(out,) * count,
        in_specs=[SMEM] + [VMEM] * (blocks + len(hids)),
        out_specs=(VMEM,) * count,
        compiler_params=MEDIUM,
        cost_estimate=cost(2 * count * blocks * each * both * tile, tuple(hids) + (out,) * count),
    )(order, *toks, *hids)


def down_grad_kernel(groups, order_ref, *refs):
    acts, ogs, outs, full = refs[:groups], refs[groups : 2 * groups], refs[2 * groups : -1], refs[-1]
    act = jnp.concatenate([a[...] for a in acts], axis=0)
    step = full.shape[1]
    size = full.shape[0] // 4
    for j in range(4):
        columns = slice(j * step, (j + 1) * step)
        og = jnp.concatenate([o[:, columns] for o in ogs], axis=0)
        full[...] = lax.dot_general(act, og, TN, preferred_element_type=F32)
        for k in range(4):
            at = pl.multiple_of(order_ref[k] * size, size)
            outs[k][:, columns] = full[pl.ds(at, size), :].astype(BF16)


def down_grads(order, acts, ogs):
    hid = acts[0].shape[1]
    rows = sum(a.shape[0] for a in acts)
    width = ogs[0].shape[1]
    out = jax.ShapeDtypeStruct((hid // 4, width), BF16)
    return pl.pallas_call(
        functools.partial(down_grad_kernel, len(acts)),
        out_shape=(out,) * 4,
        in_specs=[SMEM] + [VMEM] * (2 * len(acts)),
        out_specs=(VMEM,) * 4,
        scratch_shapes=[pltpu.VMEM((hid, width // 4), F32)],
        compiler_params=MEDIUM,
        cost_estimate=cost(2 * rows * hid * width, tuple(acts) + tuple(ogs)),
    )(order, *acts, *ogs)


PIECE = 256


def pieces(wide_shape, down_shape):
    at = 0
    for number, (rows, columns) in enumerate((wide_shape, down_shape)):
        for j in range(columns // PIECE):
            yield number, slice(at, at + rows), slice(j * PIECE, (j + 1) * PIECE)
            at += rows


def join_kernel(joined, order_ref, wide_own, down_own, *refs):
    came, out_ref = refs[:-1], refs[-1]
    owns = wide_own, down_own
    for number, rows, part in pieces(wide_own.shape, down_own.shape):
        other = came[0][rows, :] if joined else came[number][:, part]
        other = jnp.where(order_ref[4] == 1, other.astype(F32), 0.0)
        out_ref[rows, :] = (owns[number][:, part].astype(F32) + other).astype(BF16)


def join(order, wide_own, down_own, *came):
    out = jax.ShapeDtypeStruct(((wide_own.size + down_own.size) // PIECE, PIECE), BF16)
    return pl.pallas_call(
        functools.partial(join_kernel, len(came) == 1),
        out_shape=out,
        in_specs=[SMEM] + [VMEM] * (2 + len(came)),
        compiler_params=SMALL,
        cost_estimate=cost(wide_own.size, (out,)),
    )(order, wide_own, down_own, *came)


def base_kernel(order_ref, wide_own, down_own, wide_one, down_one, two_ref, wide_out, down_out):
    owns, ones, outs = (wide_own, down_own), (wide_one, down_one), (wide_out, down_out)
    for number, rows, part in pieces(wide_own.shape, down_own.shape):
        came = ones[number][:, part].astype(F32) + two_ref[rows, :].astype(F32)
        came = jnp.where(order_ref[4] == 1, 0.0, came)
        outs[number][:, part] = owns[number][:, part].astype(F32) + came


def base_terms(order, wide_own, down_own, wide_one, down_one, two):
    outs = tuple(jax.ShapeDtypeStruct(a.shape, F32) for a in (wide_own, down_own))
    return pl.pallas_call(
        base_kernel,
        out_shape=outs,
        in_specs=[SMEM] + [VMEM] * 5,
        compiler_params=SMALL,
        cost_estimate=cost(wide_own.size, outs),
    )(order, wide_own, down_own, wide_one, down_one, two)


def finish_kernel(wide_ref, down_ref, up_ref, low_ref, gate_out, up_out, down_out):
    bases, outs = (wide_ref, down_ref), ((gate_out, up_out), (down_out,))
    for number, rows, part in pieces(wide_ref.shape, down_ref.shape):
        came = up_ref[rows, :].astype(F32) + low_ref[rows, :].astype(F32)
        total = bases[number][:, part] + came
        for k, out in enumerate(outs[number]):
            size = out.shape[1]
            a, b = max(part.start, k * size), min(part.stop, (k + 1) * size)
            if a < b:
                out[:, a - k * size : b - k * size] = total[:, a - part.start : b - part.start]


def finish(wide, down, one, two):
    rows, both = wide.shape
    outs = (jax.ShapeDtypeStruct((rows, both // 2), F32),) * 2 + (jax.ShapeDtypeStruct(down.shape, F32),)
    return pl.pallas_call(
        finish_kernel,
        out_shape=outs,
        compiler_params=SMALL,
        cost_estimate=cost(wide.size, outs),
    )(wide, down, one, two)


def after(values, earlier):
    return lax.optimization_barrier((values, earlier))[0]


def pair_sums_kernel(places, *refs):
    for terms, out_ref in zip(places, refs[-2:]):
        each = out_ref.shape[0]
        values = [refs[k][block * each : (block + 1) * each, :].astype(F32) for k, block in terms]
        out_ref[...] = sum(values[1:], values[0]).astype(BF16)


def pair_sums(each, first, second):
    arrays = [a for a, _ in first + second]
    blocks = [block for _, block in first + second]
    numbered = tuple(enumerate(blocks))
    out = jax.ShapeDtypeStruct((each, arrays[0].shape[1]), BF16)
    return pl.pallas_call(
        functools.partial(pair_sums_kernel, (numbered[: len(first)], numbered[len(first) :])),
        out_shape=(out, out),
        in_specs=[VMEM] * len(arrays),
        out_specs=(VMEM, VMEM),
        compiler_params=SMALL,
        cost_estimate=cost(out.size, (out,)),
    )(*arrays)


LINE_ORDER = ((3, 2, 1, 0, 0), (0, 3, 2, 1, 1), (3, 0, 1, 2, 1), (0, 1, 2, 3, 0))


def per_device(tokens, expert_ids, gates, w_gate, w_up, w_down, cotangent):
    width = tokens.shape[1]
    group = lax.axis_size("expert")
    shards = lax.axis_size("dp")
    assert group == 8
    me = lax.axis_index("expert").astype(jnp.int32).reshape(1)
    z = lax.axis_index("dp")
    wg, wu, wd = w_gate[0], w_up[0], w_down[0]

    def flip(array, bit):
        return lax.ppermute(array, "expert", [(i, i ^ bit) for i in range(group)])

    line = shards == 4
    table = jnp.asarray(LINE_ORDER if line else ((0, 1, 2, 3, 0),), jnp.int32)
    order = table[z if line else 0]
    tokens = after(tokens, (order, me))
    cot_0 = cotangent
    tok_0 = packed(tokens, expert_ids, gates)
    tok_x, cot_y = flip(tok_0, NEAR), flip(cot_0, FAR)
    cot_x, tok_y = flip(cot_0, NEAR), flip(tok_0, FAR)
    cot_d, tok_d = flip(cot_y, NEAR), flip(tok_x, FAR)

    toks_a, cots_a = [tok_0, tok_x, tok_y], [cot_0, cot_x, cot_y]
    wide_panel, down_panel = panels(wg, wu, wd)
    cots_a += [flip(c, CORE) for c in [after(cot_0, wide_panel)] + cots_a[1:]]
    toks_a += [flip(t, CORE) for t in toks_a]
    act_a, hid_a, og_a = hidden(me, toks_a, cots_a, wide_panel, down_panel)
    tok_d, cot_d = after((tok_d, cot_d), act_a)
    toks_b, cots_b = [tok_d, flip(tok_d, CORE)], [cot_d, flip(cot_d, CORE)]
    act_b, hid_b, og_b = hidden(me, toks_b, cots_b, wide_panel, down_panel)

    def move(array, pairs):
        return lax.ppermute(array, "dp", pairs) if line else array

    one_pairs = [(0, 1), (1, 0), (2, 3), (3, 2)]
    two_pairs = [(0, 1), (1, 3), (3, 2), (2, 0)]
    up_pairs, down_pairs = [(0, 1), (1, 2)], [(3, 2), (2, 1)]
    toks, hids = toks_a + toks_b, (hid_a, hid_b)
    wide_0 = wide_grads(order, toks, hids, width, 0, 1)
    wide_one = move(wide_0[0], one_pairs)
    act_a = after(act_a, wide_0)
    down = down_grads(order, (act_a, act_b), (og_a, og_b))
    down_one = move(down[0], one_pairs)
    hid_a = after(hid_a, down)
    wide = wide_0 + wide_grads(order, toks, (hid_a, hid_b), width, 1, 3)
    act_a = after(act_a, wide[1])
    acts, hids = (act_a, act_b), (hid_a, hid_b)
    there = tuple((0, i) for i in range(4)), tuple((1, i) for i in range(4))
    sent = rows_out(me, toks_a[3:] + toks_b[1:], acts, hids, 1, wide_panel, down_panel, (), there)
    if line:
        wide_one, down_one = after((wide_one, down_one), sent)
        second = join(order, wide[1], down[1], wide_one, down_one)
        two = move(second, two_pairs)
        sent = after(sent, second)
    sent = [flip(a, CORE) for a in sent]
    here = ((0, 0), (2, 0), (1, 0), (2, 1)), ((3, 0), (4, 0), (5, 0), (5, 1))
    kept = rows_out(me, toks_a[:3] + toks_b[:1], acts, hids, 0, wide_panel, down_panel, sent, here)
    out_0, out_y, out_near, grad_0, grad_x, grad_far = kept
    out_near, grad_far = flip(out_near, NEAR), flip(grad_far, FAR)
    hid_size = wd.shape[0]
    each = tokens.shape[0]
    if line:
        two = after(two, kept)
        last = join(order, wide[2], down[2], two)
        last_up, last_down = move(last, up_pairs), move(last, down_pairs)
        out_near, grad_far = after((out_near, grad_far), last)
    out_y, grad_x = pair_sums(each, [(out_y, 0), (out_near, 1)], [(grad_x, 0), (grad_far, 1)])
    out_yy, grad_xx = flip(out_y, FAR), flip(grad_x, NEAR)
    if line:
        base = base_terms(order, wide[3], down[3], wide_one, down_one, after(two, (out_y, grad_x)))
    mixed, grad_tokens = pair_sums(
        each, [(out_0, 0), (out_near, 0), (out_yy, 0)], [(grad_0, 0), (grad_far, 0), (grad_xx, 0)]
    )
    if line:
        base, mixed, grad_tokens = lax.optimization_barrier((base, mixed, grad_tokens))
        last_up, last_down = after((last_up, last_down), (mixed, grad_tokens))
        grad_gate, grad_up, grad_down = finish(*base, last_up, last_down)
    else:
        wide_all = jnp.concatenate(wide, axis=0)
        grad_wide = lax.psum_scatter(wide_all, "dp", scatter_dimension=0, tiled=True).astype(F32)
        grad_gate, grad_up = grad_wide[:, :hid_size], grad_wide[:, hid_size:]
        grad_down = lax.psum_scatter(jnp.concatenate(down, axis=0), "dp", scatter_dimension=0, tiled=True).astype(F32)
    return (mixed, grad_tokens, grad_gate[None], grad_up[None], grad_down[None])


def solution(mesh):
    return jax.shard_map(
        per_device,
        mesh=mesh,
        in_specs=(
            P(("dp", "expert"), None),
            P(("dp", "expert"), None),
            P(("dp", "expert"), None),
            P("expert", None, None),
            P("expert", None, None),
            P("expert", None, None),
            P(("dp", "expert"), None),
        ),
        out_specs=(
            P(("dp", "expert"), None),
            P(("dp", "expert"), None),
            P("expert", "dp", None),
            P("expert", "dp", None),
            P("expert", "dp", None),
        ),
        check_vma=False,
    )
```

```python
import functools

import jax
import jax.numpy as jnp
from jax import lax
from jax.experimental import pallas as pl
from jax.experimental.pallas import tpu as pltpu
from jax.sharding import PartitionSpec as P

F32 = jnp.float32
BF16 = jnp.bfloat16
LANES = 128
CORE, NEAR, FAR = 1, 2, 4
MEDIUM = pltpu.CompilerParams(vmem_limit_bytes=24 * 1024 * 1024)
SMALL = pltpu.CompilerParams(vmem_limit_bytes=12 * 1024 * 1024)
VMEM = pl.BlockSpec(memory_space=pltpu.VMEM)
SMEM = pl.BlockSpec(memory_space=pltpu.SMEM)
NT = (((1,), (1,)), ((), ()))


def cost(flops, arrays):
    size = sum(a.size * a.dtype.itemsize for a in arrays)
    return pl.CostEstimate(flops=flops // 64, bytes_accessed=size // 64, transcendentals=0)


def own_gate(gate_rows, expert_num):
    lane = lax.broadcasted_iota(jnp.int32, gate_rows.shape, 1)
    kept = jnp.where(lane == expert_num, gate_rows.astype(F32), 0.0)
    return jnp.sum(kept, axis=1, keepdims=True)


def pack_kernel(tok_ref, ids_ref, gates_ref, out_ref):
    rows, width = tok_ref.shape
    out_ref[:, :width] = tok_ref[...]
    lane = lax.broadcasted_iota(jnp.int32, (rows, LANES), 1)
    ids, gates = ids_ref[...], gates_ref[...].astype(F32)
    total = jnp.zeros((rows, LANES), F32)
    for k in range(ids.shape[1]):
        total = total + jnp.where(ids[:, k : k + 1] == lane, gates[:, k : k + 1], 0.0)
    out_ref[:, width:] = total.astype(BF16)


def packed(tokens, ids, gates):
    rows, width = tokens.shape
    return pl.pallas_call(
        pack_kernel,
        out_shape=jax.ShapeDtypeStruct((rows, width + LANES), BF16),
        compiler_params=SMALL,
    )(tokens, ids, gates)


def panels_kernel(wg_ref, wu_ref, wd_ref, wide_ref, down_ref):
    hid = wg_ref.shape[1]
    wide_ref[:, :hid] = wg_ref[...]
    wide_ref[:, hid:] = wu_ref[...]
    down_ref[...] = wd_ref[...]


def panels(wg, wu, wd):
    width, hid = wg.shape
    outs = (jax.ShapeDtypeStruct((width, 2 * hid), BF16), jax.ShapeDtypeStruct(wd.shape, BF16))
    return pl.pallas_call(
        panels_kernel,
        out_shape=outs,
        in_specs=[VMEM] * 3,
        out_specs=(VMEM, VMEM),
        compiler_params=SMALL,
        cost_estimate=cost(width, outs),
    )(wg, wu, wd)


def hidden_kernel(blocks, me_ref, *refs):
    toks, cots = refs[:blocks], refs[blocks : 2 * blocks]
    wide_ref, down_ref, act_ref, hid_ref, og_ref = refs[2 * blocks :]
    each, width = cots[0].shape
    hid = down_ref.shape[0]
    rows = jnp.concatenate([t[:, :width] for t in toks], axis=0)
    pre = jnp.dot(rows, wide_ref[...], preferred_element_type=F32)
    for i in range(blocks):
        gate_col = own_gate(toks[i][:, width:], me_ref[0])
        og_ref[i * each : (i + 1) * each, :] = (gate_col * cots[i][...].astype(F32)).astype(BF16)
    act_grad = lax.dot_general(og_ref[...], down_ref[...], NT, preferred_element_type=F32)
    pre_gate, pre_up = pre[:, :hid], pre[:, hid:]
    s = 1.0 / (1.0 + jnp.exp(-pre_gate))
    act_ref[...] = (pre_gate * s * pre_up).astype(BF16)
    hid_ref[:, :hid] = (act_grad * pre_up * s * (1.0 + pre_gate * (1.0 - s))).astype(BF16)
    hid_ref[:, hid:] = (act_grad * pre_gate * s).astype(BF16)


def hidden(me, toks, cots, wide, down):
    blocks = len(toks)
    rows = blocks * cots[0].shape[0]
    hid, width = down.shape
    outs = tuple(jax.ShapeDtypeStruct((rows, n), BF16) for n in (hid, 2 * hid, width))
    return pl.pallas_call(
        functools.partial(hidden_kernel, blocks),
        out_shape=outs,
        in_specs=[SMEM] + [VMEM] * (2 * blocks + 2),
        out_specs=(VMEM,) * 3,
        compiler_params=MEDIUM,
        cost_estimate=cost(6 * rows * width * hid, (*toks, *cots, wide, down) + outs),
    )(me, *toks, *cots, wide, down)


def rows_kernel(blocks, groups, part, places, more, me_ref, *refs):
    toks, refs = refs[:blocks], refs[blocks:]
    acts, hids, refs = refs[:groups], refs[groups : 2 * groups], refs[2 * groups :]
    wide_ref, down_ref = refs[:2]
    added, outs = refs[2 : 2 + more], refs[2 + more :]
    width = down_ref.shape[1]
    each = toks[0].shape[0]
    gate_col = own_gate(jnp.concatenate([t[:, width:] for t in toks], axis=0), me_ref[0])

    def half(ref):
        size = ref.shape[0] // 2
        return ref[part * size : (part + 1) * size, :]

    def put(values, number, columns):
        for i in range(blocks):
            piece = values[i * each : (i + 1) * each]
            if more:
                other = added[number][i * each : (i + 1) * each, columns]
                piece = (piece.astype(F32) + other.astype(F32)).astype(BF16)
            array, block = places[number][i]
            outs[array][block * each : (block + 1) * each, columns] = piece

    act = jnp.concatenate([half(a) for a in acts], axis=0)
    hidden_grads = jnp.concatenate([half(h) for h in hids], axis=0)
    step = width // 4
    for j in range(4):
        columns = slice(j * step, (j + 1) * step)
        expert_out = jnp.dot(act, down_ref[:, columns], preferred_element_type=F32)
        put((gate_col * expert_out).astype(BF16), 0, columns)
        grad = lax.dot_general(hidden_grads, wide_ref[columns, :], NT, preferred_element_type=F32)
        put(grad.astype(BF16), 1, columns)


def rows_out(me, toks, acts, hids, part, wide, down, added, places):
    blocks, groups = len(toks), len(acts)
    each = toks[0].shape[0]
    hid, width = down.shape
    flat = places[0] + places[1]
    sizes = [sum(array == k for array, _ in flat) for k in range(1 + max(array for array, _ in flat))]
    outs = tuple(jax.ShapeDtypeStruct((n * each, width), BF16) for n in sizes)
    return pl.pallas_call(
        functools.partial(rows_kernel, blocks, groups, part, places, len(added)),
        out_shape=outs,
        in_specs=[SMEM] + [VMEM] * (blocks + 2 * groups + 2 + len(added)),
        out_specs=(VMEM,) * len(outs),
        compiler_params=MEDIUM,
        cost_estimate=cost(6 * blocks * each * width * hid, (wide, down) + outs),
    )(me, *toks, *acts, *hids, wide, down, *added)


TN = (((0,), (0,)), ((), ()))


def wide_grad_kernel(blocks, first, count, order_ref, *refs):
    toks, hids, outs = refs[:blocks], refs[blocks:-count], refs[-count:]
    hidden_grads = jnp.concatenate([h[...] for h in hids], axis=0)
    tile = outs[0].shape[0]
    for k in range(count):
        at = pl.multiple_of(order_ref[first + k] * tile, tile)
        rows = jnp.concatenate([t[:, pl.ds(at, tile)] for t in toks], axis=0)
        outs[k][...] = lax.dot_general(rows, hidden_grads, TN, preferred_element_type=F32).astype(BF16)


def wide_grads(order, toks, hids, width, first, count):
    blocks = len(toks)
    each = toks[0].shape[0]
    both, tile = hids[0].shape[1], width // 4
    out = jax.ShapeDtypeStruct((tile, both), BF16)
    return pl.pallas_call(
        functools.partial(wide_grad_kernel, blocks, first, count),
        out_shape=(out,) * count,
        in_specs=[SMEM] + [VMEM] * (blocks + len(hids)),
        out_specs=(VMEM,) * count,
        compiler_params=MEDIUM,
        cost_estimate=cost(2 * count * blocks * each * both * tile, tuple(hids) + (out,) * count),
    )(order, *toks, *hids)


def down_grad_kernel(groups, order_ref, *refs):
    acts, ogs, outs, full = refs[:groups], refs[groups : 2 * groups], refs[2 * groups : -1], refs[-1]
    act = jnp.concatenate([a[...] for a in acts], axis=0)
    step = full.shape[1]
    size = full.shape[0] // 4
    for j in range(4):
        columns = slice(j * step, (j + 1) * step)
        og = jnp.concatenate([o[:, columns] for o in ogs], axis=0)
        full[...] = lax.dot_general(act, og, TN, preferred_element_type=F32)
        for k in range(4):
            at = pl.multiple_of(order_ref[k] * size, size)
            outs[k][:, columns] = full[pl.ds(at, size), :].astype(BF16)


def down_grads(order, acts, ogs):
    hid = acts[0].shape[1]
    rows = sum(a.shape[0] for a in acts)
    width = ogs[0].shape[1]
    out = jax.ShapeDtypeStruct((hid // 4, width), BF16)
    return pl.pallas_call(
        functools.partial(down_grad_kernel, len(acts)),
        out_shape=(out,) * 4,
        in_specs=[SMEM] + [VMEM] * (2 * len(acts)),
        out_specs=(VMEM,) * 4,
        scratch_shapes=[pltpu.VMEM((hid, width // 4), F32)],
        compiler_params=MEDIUM,
        cost_estimate=cost(2 * rows * hid * width, tuple(acts) + tuple(ogs)),
    )(order, *acts, *ogs)


PIECE = 256


def pieces(wide_shape, down_shape):
    at = 0
    for number, (rows, columns) in enumerate((wide_shape, down_shape)):
        for j in range(columns // PIECE):
            yield number, slice(at, at + rows), slice(j * PIECE, (j + 1) * PIECE)
            at += rows


def join_kernel(joined, order_ref, wide_own, down_own, *refs):
    came, out_ref = refs[:-1], refs[-1]
    owns = wide_own, down_own
    for number, rows, part in pieces(wide_own.shape, down_own.shape):
        other = came[0][rows, :] if joined else came[number][:, part]
        other = jnp.where(order_ref[4] == 1, other.astype(F32), 0.0)
        out_ref[rows, :] = (owns[number][:, part].astype(F32) + other).astype(BF16)


def join(order, wide_own, down_own, *came):
    out = jax.ShapeDtypeStruct(((wide_own.size + down_own.size) // PIECE, PIECE), BF16)
    return pl.pallas_call(
        functools.partial(join_kernel, len(came) == 1),
        out_shape=out,
        in_specs=[SMEM] + [VMEM] * (2 + len(came)),
        compiler_params=SMALL,
        cost_estimate=cost(wide_own.size, (out,)),
    )(order, wide_own, down_own, *came)


def base_kernel(order_ref, wide_own, down_own, wide_one, down_one, two_ref, wide_out, down_out):
    owns, ones, outs = (wide_own, down_own), (wide_one, down_one), (wide_out, down_out)
    for number, rows, part in pieces(wide_own.shape, down_own.shape):
        came = ones[number][:, part].astype(F32) + two_ref[rows, :].astype(F32)
        came = jnp.where(order_ref[4] == 1, 0.0, came)
        outs[number][:, part] = owns[number][:, part].astype(F32) + came


def base_terms(order, wide_own, down_own, wide_one, down_one, two):
    outs = tuple(jax.ShapeDtypeStruct(a.shape, F32) for a in (wide_own, down_own))
    return pl.pallas_call(
        base_kernel,
        out_shape=outs,
        in_specs=[SMEM] + [VMEM] * 5,
        compiler_params=SMALL,
        cost_estimate=cost(wide_own.size, outs),
    )(order, wide_own, down_own, wide_one, down_one, two)


def finish_kernel(wide_ref, down_ref, up_ref, low_ref, gate_out, up_out, down_out):
    bases, outs = (wide_ref, down_ref), ((gate_out, up_out), (down_out,))
    for number, rows, part in pieces(wide_ref.shape, down_ref.shape):
        came = up_ref[rows, :].astype(F32) + low_ref[rows, :].astype(F32)
        total = bases[number][:, part] + came
        for k, out in enumerate(outs[number]):
            size = out.shape[1]
            a, b = max(part.start, k * size), min(part.stop, (k + 1) * size)
            if a < b:
                out[:, a - k * size : b - k * size] = total[:, a - part.start : b - part.start]


def finish(wide, down, one, two):
    rows, both = wide.shape
    outs = (jax.ShapeDtypeStruct((rows, both // 2), F32),) * 2 + (jax.ShapeDtypeStruct(down.shape, F32),)
    return pl.pallas_call(
        finish_kernel,
        out_shape=outs,
        compiler_params=SMALL,
        cost_estimate=cost(wide.size, outs),
    )(wide, down, one, two)


def after(values, earlier):
    return lax.optimization_barrier((values, earlier))[0]


def pair_sums_kernel(places, *refs):
    for terms, out_ref in zip(places, refs[-2:]):
        each = out_ref.shape[0]
        values = [refs[k][block * each : (block + 1) * each, :].astype(F32) for k, block in terms]
        out_ref[...] = sum(values[1:], values[0]).astype(BF16)


def pair_sums(each, first, second):
    arrays = [a for a, _ in first + second]
    blocks = [block for _, block in first + second]
    numbered = tuple(enumerate(blocks))
    out = jax.ShapeDtypeStruct((each, arrays[0].shape[1]), BF16)
    return pl.pallas_call(
        functools.partial(pair_sums_kernel, (numbered[: len(first)], numbered[len(first) :])),
        out_shape=(out, out),
        in_specs=[VMEM] * len(arrays),
        out_specs=(VMEM, VMEM),
        compiler_params=SMALL,
        cost_estimate=cost(out.size, (out,)),
    )(*arrays)


LINE_ORDER = ((3, 2, 1, 0, 0), (0, 3, 2, 1, 1), (3, 0, 1, 2, 1), (0, 1, 2, 3, 0))


def per_device(tokens, expert_ids, gates, w_gate, w_up, w_down, cotangent):
    width = tokens.shape[1]
    group = lax.axis_size("expert")
    shards = lax.axis_size("dp")
    assert group == 8
    me = lax.axis_index("expert").astype(jnp.int32).reshape(1)
    z = lax.axis_index("dp")
    wg, wu, wd = w_gate[0], w_up[0], w_down[0]

    def flip(array, bit):
        return lax.ppermute(array, "expert", [(i, i ^ bit) for i in range(group)])

    line = shards == 4
    table = jnp.asarray(LINE_ORDER if line else ((0, 1, 2, 3, 0),), jnp.int32)
    order = table[z if line else 0]
    tokens = after(tokens, (order, me))
    cot_0 = cotangent
    tok_0 = packed(tokens, expert_ids, gates)
    tok_x, cot_y = flip(tok_0, NEAR), flip(cot_0, FAR)
    cot_x, tok_y = flip(cot_0, NEAR), flip(tok_0, FAR)
    cot_d, tok_d = flip(cot_y, NEAR), flip(tok_x, FAR)

    toks_a, cots_a = [tok_0, tok_x, tok_y], [cot_0, cot_x, cot_y]
    wide_panel, down_panel = panels(wg, wu, wd)
    early = [flip(a, CORE) for a in (tok_0, after(cot_0, wide_panel), cot_x, cot_y)]
    late = [flip(a, CORE) for a in after((tok_x, tok_y), early)]
    toks_a += [early[0], *late]
    cots_a += early[1:]
    act_a, hid_a, og_a = hidden(me, toks_a, cots_a, wide_panel, down_panel)
    tok_d, cot_d = after((tok_d, cot_d), act_a)
    toks_b, cots_b = [tok_d, flip(tok_d, CORE)], [cot_d, flip(cot_d, CORE)]
    act_b, hid_b, og_b = hidden(me, toks_b, cots_b, wide_panel, down_panel)

    def move(array, pairs):
        return lax.ppermute(array, "dp", pairs) if line else array

    one_pairs = [(0, 1), (1, 0), (2, 3), (3, 2)]
    two_pairs = [(0, 1), (1, 3), (3, 2), (2, 0)]
    up_pairs, down_pairs = [(0, 1), (1, 2)], [(3, 2), (2, 1)]
    toks, hids = toks_a + toks_b, (hid_a, hid_b)
    wide_0 = wide_grads(order, toks, hids, width, 0, 1)
    wide_one = move(wide_0[0], one_pairs)
    act_a = after(act_a, wide_0)
    down = down_grads(order, (act_a, act_b), (og_a, og_b))
    down_one = move(down[0], one_pairs)
    hid_a = after(hid_a, down)
    wide = wide_0 + wide_grads(order, toks, (hid_a, hid_b), width, 1, 3)
    act_a = after(act_a, wide[1])
    acts, hids = (act_a, act_b), (hid_a, hid_b)
    there = tuple((0, i) for i in range(4)), tuple((1, i) for i in range(4))
    sent = rows_out(me, toks_a[3:] + toks_b[1:], acts, hids, 1, wide_panel, down_panel, (), there)
    if line:
        wide_one, down_one = after((wide_one, down_one), sent)
        second = join(order, wide[1], down[1], wide_one, down_one)
        two = move(second, two_pairs)
        sent = after(sent, second)
    sent = [flip(a, CORE) for a in sent]
    here = ((0, 0), (2, 0), (1, 0), (2, 1)), ((3, 0), (4, 0), (5, 0), (5, 1))
    kept = rows_out(me, toks_a[:3] + toks_b[:1], acts, hids, 0, wide_panel, down_panel, sent, here)
    out_0, out_y, out_near, grad_0, grad_x, grad_far = kept
    out_near, grad_far = flip(out_near, NEAR), flip(grad_far, FAR)
    hid_size = wd.shape[0]
    each = tokens.shape[0]
    if line:
        two = after(two, kept)
        last = join(order, wide[2], down[2], two)
        last_up, last_down = move(last, up_pairs), move(last, down_pairs)
        out_near, grad_far = after((out_near, grad_far), last)
    out_y, grad_x = pair_sums(each, [(out_y, 0), (out_near, 1)], [(grad_x, 0), (grad_far, 1)])
    out_yy, grad_xx = flip(out_y, FAR), flip(grad_x, NEAR)
    if line:
        base = base_terms(order, wide[3], down[3], wide_one, down_one, after(two, (out_y, grad_x)))
    mixed, grad_tokens = pair_sums(
        each, [(out_0, 0), (out_near, 0), (out_yy, 0)], [(grad_0, 0), (grad_far, 0), (grad_xx, 0)]
    )
    if line:
        base, mixed, grad_tokens = lax.optimization_barrier((base, mixed, grad_tokens))
        last_up, last_down = after((last_up, last_down), (mixed, grad_tokens))
        grad_gate, grad_up, grad_down = finish(*base, last_up, last_down)
    else:
        wide_all = jnp.concatenate(wide, axis=0)
        grad_wide = lax.psum_scatter(wide_all, "dp", scatter_dimension=0, tiled=True).astype(F32)
        grad_gate, grad_up = grad_wide[:, :hid_size], grad_wide[:, hid_size:]
        grad_down = lax.psum_scatter(jnp.concatenate(down, axis=0), "dp", scatter_dimension=0, tiled=True).astype(F32)
    return (mixed, grad_tokens, grad_gate[None], grad_up[None], grad_down[None])


def solution(mesh):
    return jax.shard_map(
        per_device,
        mesh=mesh,
        in_specs=(
            P(("dp", "expert"), None),
            P(("dp", "expert"), None),
            P(("dp", "expert"), None),
            P("expert", None, None),
            P("expert", None, None),
            P("expert", None, None),
            P(("dp", "expert"), None),
        ),
        out_specs=(
            P(("dp", "expert"), None),
            P(("dp", "expert"), None),
            P("expert", "dp", None),
            P("expert", "dp", None),
            P("expert", "dp", None),
        ),
        check_vma=False,
    )
```

```python
import functools

import jax
import jax.numpy as jnp
from jax import lax
from jax.experimental import pallas as pl
from jax.experimental.pallas import tpu as pltpu
from jax.sharding import PartitionSpec as P

F32 = jnp.float32
BF16 = jnp.bfloat16
LANES = 128
CORE, NEAR, FAR = 1, 2, 4
MEDIUM = pltpu.CompilerParams(vmem_limit_bytes=24 * 1024 * 1024)
SMALL = pltpu.CompilerParams(vmem_limit_bytes=12 * 1024 * 1024)
VMEM = pl.BlockSpec(memory_space=pltpu.VMEM)
SMEM = pl.BlockSpec(memory_space=pltpu.SMEM)
NT = (((1,), (1,)), ((), ()))


def cost(flops, arrays):
    size = sum(a.size * a.dtype.itemsize for a in arrays)
    return pl.CostEstimate(flops=flops // 64, bytes_accessed=size // 64, transcendentals=0)


def own_gate(gate_rows, expert_num):
    lane = lax.broadcasted_iota(jnp.int32, gate_rows.shape, 1)
    kept = jnp.where(lane == expert_num, gate_rows.astype(F32), 0.0)
    return jnp.sum(kept, axis=1, keepdims=True)


def pack_kernel(tok_ref, ids_ref, gates_ref, out_ref):
    rows, width = tok_ref.shape
    out_ref[:, :width] = tok_ref[...]
    lane = lax.broadcasted_iota(jnp.int32, (rows, LANES), 1)
    ids, gates = ids_ref[...], gates_ref[...].astype(F32)
    total = jnp.zeros((rows, LANES), F32)
    for k in range(ids.shape[1]):
        total = total + jnp.where(ids[:, k : k + 1] == lane, gates[:, k : k + 1], 0.0)
    out_ref[:, width:] = total.astype(BF16)


def packed(tokens, ids, gates):
    rows, width = tokens.shape
    return pl.pallas_call(
        pack_kernel,
        out_shape=jax.ShapeDtypeStruct((rows, width + LANES), BF16),
        compiler_params=SMALL,
    )(tokens, ids, gates)


def panels_kernel(wg_ref, wu_ref, wd_ref, wide_ref, down_ref):
    hid = wg_ref.shape[1]
    wide_ref[:, :hid] = wg_ref[...]
    wide_ref[:, hid:] = wu_ref[...]
    down_ref[...] = wd_ref[...]


def panels(wg, wu, wd):
    width, hid = wg.shape
    outs = (jax.ShapeDtypeStruct((width, 2 * hid), BF16), jax.ShapeDtypeStruct(wd.shape, BF16))
    return pl.pallas_call(
        panels_kernel,
        out_shape=outs,
        in_specs=[VMEM] * 3,
        out_specs=(VMEM, VMEM),
        compiler_params=SMALL,
        cost_estimate=cost(width, outs),
    )(wg, wu, wd)


def hidden_kernel(blocks, me_ref, *refs):
    toks, cots = refs[:blocks], refs[blocks : 2 * blocks]
    wide_ref, down_ref, act_ref, hid_ref, og_ref = refs[2 * blocks :]
    each, width = cots[0].shape
    hid = down_ref.shape[0]
    rows = jnp.concatenate([t[:, :width] for t in toks], axis=0)
    pre = jnp.dot(rows, wide_ref[...], preferred_element_type=F32)
    for i in range(blocks):
        gate_col = own_gate(toks[i][:, width:], me_ref[0])
        og_ref[i * each : (i + 1) * each, :] = (gate_col * cots[i][...].astype(F32)).astype(BF16)
    act_grad = lax.dot_general(og_ref[...], down_ref[...], NT, preferred_element_type=F32)
    pre_gate, pre_up = pre[:, :hid], pre[:, hid:]
    s = 1.0 / (1.0 + jnp.exp(-pre_gate))
    act_ref[...] = (pre_gate * s * pre_up).astype(BF16)
    hid_ref[:, :hid] = (act_grad * pre_up * s * (1.0 + pre_gate * (1.0 - s))).astype(BF16)
    hid_ref[:, hid:] = (act_grad * pre_gate * s).astype(BF16)


def hidden(me, toks, cots, wide, down):
    blocks = len(toks)
    rows = blocks * cots[0].shape[0]
    hid, width = down.shape
    outs = tuple(jax.ShapeDtypeStruct((rows, n), BF16) for n in (hid, 2 * hid, width))
    return pl.pallas_call(
        functools.partial(hidden_kernel, blocks),
        out_shape=outs,
        in_specs=[SMEM] + [VMEM] * (2 * blocks + 2),
        out_specs=(VMEM,) * 3,
        compiler_params=MEDIUM,
        cost_estimate=cost(6 * rows * width * hid, (*toks, *cots, wide, down) + outs),
    )(me, *toks, *cots, wide, down)


def rows_kernel(blocks, groups, part, places, more, me_ref, *refs):
    toks, refs = refs[:blocks], refs[blocks:]
    acts, hids, refs = refs[:groups], refs[groups : 2 * groups], refs[2 * groups :]
    wide_ref, down_ref = refs[:2]
    added, outs = refs[2 : 2 + more], refs[2 + more :]
    width = down_ref.shape[1]
    each = toks[0].shape[0]
    gate_col = own_gate(jnp.concatenate([t[:, width:] for t in toks], axis=0), me_ref[0])

    def joined(refs):
        size = refs[0].shape[0] // 2
        return jnp.concatenate([refs[0][part * size : (part + 1) * size, :]] + [r[...] for r in refs[1:]], axis=0)

    def put(values, number, columns):
        for i in range(blocks):
            piece = values[i * each : (i + 1) * each]
            if more:
                other = added[number][i * each : (i + 1) * each, columns]
                piece = (piece.astype(F32) + other.astype(F32)).astype(BF16)
            array, block = places[number][i]
            outs[array][block * each : (block + 1) * each, columns] = piece

    act, hidden_grads = joined(acts), joined(hids)
    step = width // 4
    for j in range(4):
        columns = slice(j * step, (j + 1) * step)
        expert_out = jnp.dot(act, down_ref[:, columns], preferred_element_type=F32)
        put((gate_col * expert_out).astype(BF16), 0, columns)
        grad = lax.dot_general(hidden_grads, wide_ref[columns, :], NT, preferred_element_type=F32)
        put(grad.astype(BF16), 1, columns)


def rows_out(me, toks, acts, hids, part, wide, down, added, places):
    blocks, groups = len(toks), len(acts)
    each = toks[0].shape[0]
    hid, width = down.shape
    flat = places[0] + places[1]
    sizes = [sum(array == k for array, _ in flat) for k in range(1 + max(array for array, _ in flat))]
    outs = tuple(jax.ShapeDtypeStruct((n * each, width), BF16) for n in sizes)
    return pl.pallas_call(
        functools.partial(rows_kernel, blocks, groups, part, places, len(added)),
        out_shape=outs,
        in_specs=[SMEM] + [VMEM] * (blocks + 2 * groups + 2 + len(added)),
        out_specs=(VMEM,) * len(outs),
        compiler_params=MEDIUM,
        cost_estimate=cost(6 * blocks * each * width * hid, (wide, down) + outs),
    )(me, *toks, *acts, *hids, wide, down, *added)


TN = (((0,), (0,)), ((), ()))


def wide_grad_kernel(blocks, groups, first, count, order_ref, *refs):
    toks, hids, start, outs = refs[:blocks], refs[blocks : blocks + groups], refs[blocks + groups : -count], refs[-count:]
    hidden_grads = jnp.concatenate([h[...] for h in hids], axis=0)
    tile = outs[0].shape[0]
    for k in range(count):
        at = pl.multiple_of(order_ref[first + k] * tile, tile)
        rows = jnp.concatenate([t[:, pl.ds(at, tile)] for t in toks], axis=0)
        total = lax.dot_general(rows, hidden_grads, TN, preferred_element_type=F32)
        if start:
            total = total + start[0][...]
        outs[k][...] = total.astype(outs[k].dtype)


def wide_grads(order, toks, hids, width, first, count, start=(), kind=BF16):
    blocks = len(toks)
    each = toks[0].shape[0]
    both, tile = hids[0].shape[1], width // 4
    out = jax.ShapeDtypeStruct((tile, both), kind)
    return pl.pallas_call(
        functools.partial(wide_grad_kernel, blocks, len(hids), first, count),
        out_shape=(out,) * count,
        in_specs=[SMEM] + [VMEM] * (blocks + len(hids) + len(start)),
        out_specs=(VMEM,) * count,
        compiler_params=MEDIUM,
        cost_estimate=cost(2 * count * blocks * each * both * tile, tuple(hids) + (out,) * count),
    )(order, *toks, *hids, *start)


def down_grad_kernel(groups, order_ref, *refs):
    acts, ogs, outs, full = refs[:groups], refs[groups : 2 * groups], refs[2 * groups : -1], refs[-1]
    act = jnp.concatenate([a[...] for a in acts], axis=0)
    step = full.shape[1]
    size = full.shape[0] // 4
    for j in range(4):
        columns = slice(j * step, (j + 1) * step)
        og = jnp.concatenate([o[:, columns] for o in ogs], axis=0)
        full[...] = lax.dot_general(act, og, TN, preferred_element_type=F32)
        for k in range(4):
            at = pl.multiple_of(order_ref[k] * size, size)
            outs[k][:, columns] = full[pl.ds(at, size), :].astype(BF16)


def down_grads(order, acts, ogs):
    hid = acts[0].shape[1]
    rows = sum(a.shape[0] for a in acts)
    width = ogs[0].shape[1]
    out = jax.ShapeDtypeStruct((hid // 4, width), BF16)
    return pl.pallas_call(
        functools.partial(down_grad_kernel, len(acts)),
        out_shape=(out,) * 4,
        in_specs=[SMEM] + [VMEM] * (2 * len(acts)),
        out_specs=(VMEM,) * 4,
        scratch_shapes=[pltpu.VMEM((hid, width // 4), F32)],
        compiler_params=MEDIUM,
        cost_estimate=cost(2 * rows * hid * width, tuple(acts) + tuple(ogs)),
    )(order, *acts, *ogs)


PIECE = 256


def pieces(wide_shape, down_shape):
    at = 0
    for number, (rows, columns) in enumerate((wide_shape, down_shape)):
        for j in range(columns // PIECE):
            yield number, slice(at, at + rows), slice(j * PIECE, (j + 1) * PIECE)
            at += rows


def join_kernel(order_ref, wide_own, down_own, *refs):
    came, out_ref = refs[:-1], refs[-1]
    owns = wide_own, down_own
    for number, rows, part in pieces(wide_own.shape, down_own.shape):
        own = owns[number][:, part]
        if came:
            other = came[0][rows, :] if len(came) == 1 else came[number][:, part]
            other = jnp.where(order_ref[4] == 1, other.astype(F32), 0.0)
            own = (own.astype(F32) + other).astype(BF16)
        out_ref[rows, :] = own


def join(order, wide_own, down_own, *came):
    out = jax.ShapeDtypeStruct(((wide_own.size + down_own.size) // PIECE, PIECE), BF16)
    return pl.pallas_call(
        join_kernel,
        out_shape=out,
        in_specs=[SMEM] + [VMEM] * (2 + len(came)),
        compiler_params=SMALL,
        cost_estimate=cost(wide_own.size, (out,)),
    )(order, wide_own, down_own, *came)


def base_kernel(order_ref, wide_own, down_own, wide_one, down_one, two_ref, wide_out, down_out):
    owns, ones, outs = (wide_own, down_own), (wide_one, down_one), (wide_out, down_out)
    for number, rows, part in pieces(wide_own.shape, down_own.shape):
        came = ones[number][:, part].astype(F32) + two_ref[rows, :].astype(F32)
        came = jnp.where(order_ref[4] == 1, 0.0, came)
        outs[number][:, part] = owns[number][:, part].astype(F32) + came


def base_terms(order, wide_own, down_own, wide_one, down_one, two):
    outs = tuple(jax.ShapeDtypeStruct(a.shape, F32) for a in (wide_own, down_own))
    return pl.pallas_call(
        base_kernel,
        out_shape=outs,
        in_specs=[SMEM] + [VMEM] * 5,
        compiler_params=SMALL,
        cost_estimate=cost(wide_own.size, outs),
    )(order, wide_own, down_own, wide_one, down_one, two)


def finish_kernel(wide_ref, down_ref, up_ref, low_ref, gate_out, up_out, down_out):
    bases, outs = (wide_ref, down_ref), ((gate_out, up_out), (down_out,))
    for number, rows, part in pieces(wide_ref.shape, down_ref.shape):
        came = up_ref[rows, :].astype(F32) + low_ref[rows, :].astype(F32)
        total = bases[number][:, part] + came
        for k, out in enumerate(outs[number]):
            size = out.shape[1]
            a, b = max(part.start, k * size), min(part.stop, (k + 1) * size)
            if a < b:
                out[:, a - k * size : b - k * size] = total[:, a - part.start : b - part.start]


def finish(wide, down, one, two):
    rows, both = wide.shape
    outs = (jax.ShapeDtypeStruct((rows, both // 2), F32),) * 2 + (jax.ShapeDtypeStruct(down.shape, F32),)
    return pl.pallas_call(
        finish_kernel,
        out_shape=outs,
        compiler_params=SMALL,
        cost_estimate=cost(wide.size, outs),
    )(wide, down, one, two)


def after(values, earlier):
    return lax.optimization_barrier((values, earlier))[0]


def pair_sums_kernel(places, *refs):
    for terms, out_ref in zip(places, refs[-2:]):
        each = out_ref.shape[0]
        values = [refs[k][block * each : (block + 1) * each, :].astype(F32) for k, block in terms]
        out_ref[...] = sum(values[1:], values[0]).astype(BF16)


def pair_sums(each, first, second):
    arrays = [a for a, _ in first + second]
    blocks = [block for _, block in first + second]
    numbered = tuple(enumerate(blocks))
    out = jax.ShapeDtypeStruct((each, arrays[0].shape[1]), BF16)
    return pl.pallas_call(
        functools.partial(pair_sums_kernel, (numbered[: len(first)], numbered[len(first) :])),
        out_shape=(out, out),
        in_specs=[VMEM] * len(arrays),
        out_specs=(VMEM, VMEM),
        compiler_params=SMALL,
        cost_estimate=cost(out.size, (out,)),
    )(*arrays)


LINE_ORDER = ((3, 2, 1, 0, 0), (0, 3, 2, 1, 1), (3, 0, 1, 2, 1), (0, 1, 2, 3, 0))


def per_device(tokens, expert_ids, gates, w_gate, w_up, w_down, cotangent):
    width = tokens.shape[1]
    group = lax.axis_size("expert")
    shards = lax.axis_size("dp")
    assert group == 8
    me = lax.axis_index("expert").astype(jnp.int32).reshape(1)
    z = lax.axis_index("dp")
    wg, wu, wd = w_gate[0], w_up[0], w_down[0]

    def flip(array, bit):
        return lax.ppermute(array, "expert", [(i, i ^ bit) for i in range(group)])

    line = shards == 4
    table = jnp.asarray(LINE_ORDER if line else ((0, 1, 2, 3, 0),), jnp.int32)
    order = table[z if line else 0]
    tokens = after(tokens, (order, me))
    cot_0 = cotangent
    tok_0 = packed(tokens, expert_ids, gates)
    tok_x, cot_y = flip(tok_0, NEAR), flip(cot_0, FAR)
    cot_x, tok_y = flip(cot_0, NEAR), flip(tok_0, FAR)
    cot_d, tok_d = flip(cot_y, NEAR), flip(tok_x, FAR)

    toks_a, cots_a = [tok_0, tok_x, tok_y], [cot_0, cot_x, cot_y]
    wide_panel, down_panel = panels(wg, wu, wd)
    cots_a += [flip(c, CORE) for c in [after(cot_0, wide_panel)] + cots_a[1:]]
    toks_a += [flip(t, CORE) for t in toks_a]
    act_a, hid_a, og_a = hidden(me, toks_a, cots_a, wide_panel, down_panel)
    tok_d, cot_d = after((tok_d, cot_d), act_a)
    tok_e, cot_e = flip(tok_d, CORE), flip(cot_d, CORE)
    act_d, hid_d, og_d = hidden(me, [tok_d], [cot_d], wide_panel, down_panel)
    toks = toks_a + [tok_d]
    (wide_part,) = wide_grads(order, toks, (hid_a, hid_d), width, 0, 1, kind=F32)
    tok_e, cot_e = after((tok_e, cot_e), wide_part)
    act_e, hid_e, og_e = hidden(me, [tok_e], [cot_e], wide_panel, down_panel)

    def move(array, pairs):
        return lax.ppermute(array, "dp", pairs) if line else array

    one_pairs = [(0, 1), (1, 0), (2, 3), (3, 2)]
    two_pairs = [(0, 1), (1, 3), (3, 2), (2, 0)]
    end_pairs, mid_pairs = [(0, 1), (3, 2)], [(1, 2), (2, 1)]
    toks = toks + [tok_e]
    wide_0 = wide_grads(order, [tok_e], (hid_e,), width, 0, 1, start=(wide_part,))
    wide_one = move(wide_0[0], one_pairs)
    act_a = after(act_a, wide_0)
    down = down_grads(order, (act_a, act_d, act_e), (og_a, og_d, og_e))
    down_one = move(down[0], one_pairs)
    hid_a = after(hid_a, down)
    wide = wide_0 + wide_grads(order, toks, (hid_a, hid_d, hid_e), width, 1, 3)
    act_a = after(act_a, wide[1])
    there = tuple((0, i) for i in range(4)), tuple((1, i) for i in range(4))
    sent = rows_out(me, toks_a[3:] + [tok_e], (act_a, act_e), (hid_a, hid_e), 1, wide_panel, down_panel, (), there)
    if line:
        wide_one, down_one = after((wide_one, down_one), sent)
        second = join(order, wide[1], down[1], wide_one, down_one)
        two = move(second, two_pairs)
        sent = after(sent, second)
    sent = [flip(a, CORE) for a in sent]
    here = ((0, 0), (2, 0), (1, 0), (2, 1)), ((3, 0), (4, 0), (5, 0), (5, 1))
    kept = rows_out(me, toks_a[:3] + [tok_d], (act_a, act_d), (hid_a, hid_d), 0, wide_panel, down_panel, sent, here)
    out_0, out_y, out_near, grad_0, grad_x, grad_far = kept
    out_near, grad_far = flip(out_near, NEAR), flip(grad_far, FAR)
    hid_size = wd.shape[0]
    each = tokens.shape[0]
    if line:
        own_last = join(order, *after((wide[2], down[2]), kept))
        two = after(two, own_last)
        last = join(order, wide[2], down[2], two)
        last_end, last_mid = move(own_last, end_pairs), move(last, mid_pairs)
        out_near, grad_far = after((out_near, grad_far), last)
    out_y, grad_x = pair_sums(each, [(out_y, 0), (out_near, 1)], [(grad_x, 0), (grad_far, 1)])
    out_yy, grad_xx = flip(out_y, FAR), flip(grad_x, NEAR)
    if line:
        base = base_terms(order, wide[3], down[3], wide_one, down_one, after(two, (out_y, grad_x)))
    mixed, grad_tokens = pair_sums(
        each, [(out_0, 0), (out_near, 0), (out_yy, 0)], [(grad_0, 0), (grad_far, 0), (grad_xx, 0)]
    )
    if line:
        base, mixed, grad_tokens = lax.optimization_barrier((base, mixed, grad_tokens))
        last_end, last_mid = after((last_end, last_mid), (mixed, grad_tokens))
        grad_gate, grad_up, grad_down = finish(*base, last_end, last_mid)
    else:
        wide_all = jnp.concatenate(wide, axis=0)
        grad_wide = lax.psum_scatter(wide_all, "dp", scatter_dimension=0, tiled=True).astype(F32)
        grad_gate, grad_up = grad_wide[:, :hid_size], grad_wide[:, hid_size:]
        grad_down = lax.psum_scatter(jnp.concatenate(down, axis=0), "dp", scatter_dimension=0, tiled=True).astype(F32)
    return (mixed, grad_tokens, grad_gate[None], grad_up[None], grad_down[None])


def solution(mesh):
    return jax.shard_map(
        per_device,
        mesh=mesh,
        in_specs=(
            P(("dp", "expert"), None),
            P(("dp", "expert"), None),
            P(("dp", "expert"), None),
            P("expert", None, None),
            P("expert", None, None),
            P("expert", None, None),
            P(("dp", "expert"), None),
        ),
        out_specs=(
            P(("dp", "expert"), None),
            P(("dp", "expert"), None),
            P("expert", "dp", None),
            P("expert", "dp", None),
            P("expert", "dp", None),
        ),
        check_vma=False,
    )
```

```python
import functools

import jax
import jax.numpy as jnp
from jax import lax
from jax.experimental import pallas as pl
from jax.experimental.pallas import tpu as pltpu
from jax.sharding import PartitionSpec as P

F32 = jnp.float32
BF16 = jnp.bfloat16
LANES = 128
CORE, NEAR, FAR = 1, 2, 4
MEDIUM = pltpu.CompilerParams(vmem_limit_bytes=24 * 1024 * 1024)
SMALL = pltpu.CompilerParams(vmem_limit_bytes=12 * 1024 * 1024)
VMEM = pl.BlockSpec(memory_space=pltpu.VMEM)
SMEM = pl.BlockSpec(memory_space=pltpu.SMEM)
NT = (((1,), (1,)), ((), ()))


def cost(flops, arrays):
    size = sum(a.size * a.dtype.itemsize for a in arrays)
    return pl.CostEstimate(flops=flops // 64, bytes_accessed=size // 64, transcendentals=0)


def own_gate(gate_rows, expert_num):
    lane = lax.broadcasted_iota(jnp.int32, gate_rows.shape, 1)
    kept = jnp.where(lane == expert_num, gate_rows.astype(F32), 0.0)
    return jnp.sum(kept, axis=1, keepdims=True)


def pack_kernel(tok_ref, ids_ref, gates_ref, out_ref):
    rows, width = tok_ref.shape
    out_ref[:, :width] = tok_ref[...]
    lane = lax.broadcasted_iota(jnp.int32, (rows, LANES), 1)
    ids, gates = ids_ref[...], gates_ref[...].astype(F32)
    total = jnp.zeros((rows, LANES), F32)
    for k in range(ids.shape[1]):
        total = total + jnp.where(ids[:, k : k + 1] == lane, gates[:, k : k + 1], 0.0)
    out_ref[:, width:] = total.astype(BF16)


def packed(tokens, ids, gates):
    rows, width = tokens.shape
    return pl.pallas_call(
        pack_kernel,
        out_shape=jax.ShapeDtypeStruct((rows, width + LANES), BF16),
        compiler_params=SMALL,
    )(tokens, ids, gates)


def panels_kernel(wg_ref, wu_ref, wd_ref, wide_ref, down_ref):
    hid = wg_ref.shape[1]
    wide_ref[:, :hid] = wg_ref[...]
    wide_ref[:, hid:] = wu_ref[...]
    down_ref[...] = wd_ref[...]


def panels(wg, wu, wd):
    width, hid = wg.shape
    outs = (jax.ShapeDtypeStruct((width, 2 * hid), BF16), jax.ShapeDtypeStruct(wd.shape, BF16))
    return pl.pallas_call(
        panels_kernel,
        out_shape=outs,
        in_specs=[VMEM] * 3,
        out_specs=(VMEM, VMEM),
        compiler_params=SMALL,
        cost_estimate=cost(width, outs),
    )(wg, wu, wd)


def hidden_kernel(blocks, me_ref, *refs):
    toks, cots = refs[:blocks], refs[blocks : 2 * blocks]
    wide_ref, down_ref, act_ref, hid_ref, og_ref = refs[2 * blocks :]
    each, width = cots[0].shape
    hid = down_ref.shape[0]
    rows = jnp.concatenate([t[:, :width] for t in toks], axis=0)
    pre = jnp.dot(rows, wide_ref[...], preferred_element_type=F32)
    for i in range(blocks):
        gate_col = own_gate(toks[i][:, width:], me_ref[0])
        og_ref[i * each : (i + 1) * each, :] = (gate_col * cots[i][...].astype(F32)).astype(BF16)
    act_grad = lax.dot_general(og_ref[...], down_ref[...], NT, preferred_element_type=F32)
    pre_gate, pre_up = pre[:, :hid], pre[:, hid:]
    s = 1.0 / (1.0 + jnp.exp(-pre_gate))
    act_ref[...] = (pre_gate * s * pre_up).astype(BF16)
    hid_ref[:, :hid] = (act_grad * pre_up * s * (1.0 + pre_gate * (1.0 - s))).astype(BF16)
    hid_ref[:, hid:] = (act_grad * pre_gate * s).astype(BF16)


def hidden(me, toks, cots, wide, down):
    blocks = len(toks)
    rows = blocks * cots[0].shape[0]
    hid, width = down.shape
    outs = tuple(jax.ShapeDtypeStruct((rows, n), BF16) for n in (hid, 2 * hid, width))
    return pl.pallas_call(
        functools.partial(hidden_kernel, blocks),
        out_shape=outs,
        in_specs=[SMEM] + [VMEM] * (2 * blocks + 2),
        out_specs=(VMEM,) * 3,
        compiler_params=MEDIUM,
        cost_estimate=cost(6 * rows * width * hid, (*toks, *cots, wide, down) + outs),
    )(me, *toks, *cots, wide, down)


def rows_kernel(blocks, groups, part, places, more, me_ref, *refs):
    toks, refs = refs[:blocks], refs[blocks:]
    acts, hids, refs = refs[:groups], refs[groups : 2 * groups], refs[2 * groups :]
    wide_ref, down_ref = refs[:2]
    added, outs = refs[2 : 2 + more], refs[2 + more :]
    width = down_ref.shape[1]
    each = toks[0].shape[0]
    gate_col = own_gate(jnp.concatenate([t[:, width:] for t in toks], axis=0), me_ref[0])

    def joined(refs):
        size = refs[0].shape[0] // 2
        return jnp.concatenate([refs[0][part * size : (part + 1) * size, :]] + [r[...] for r in refs[1:]], axis=0)

    def put(values, number, columns):
        for i in range(blocks):
            piece = values[i * each : (i + 1) * each]
            if more:
                other = added[number][i * each : (i + 1) * each, columns]
                piece = (piece.astype(F32) + other.astype(F32)).astype(BF16)
            array, block = places[number][i]
            outs[array][block * each : (block + 1) * each, columns] = piece

    act, hidden_grads = joined(acts), joined(hids)
    step = width // 4
    for j in range(4):
        columns = slice(j * step, (j + 1) * step)
        expert_out = jnp.dot(act, down_ref[:, columns], preferred_element_type=F32)
        put((gate_col * expert_out).astype(BF16), 0, columns)
        grad = lax.dot_general(hidden_grads, wide_ref[columns, :], NT, preferred_element_type=F32)
        put(grad.astype(BF16), 1, columns)


def rows_out(me, toks, acts, hids, part, wide, down, added, places):
    blocks, groups = len(toks), len(acts)
    each = toks[0].shape[0]
    hid, width = down.shape
    flat = places[0] + places[1]
    sizes = [sum(array == k for array, _ in flat) for k in range(1 + max(array for array, _ in flat))]
    outs = tuple(jax.ShapeDtypeStruct((n * each, width), BF16) for n in sizes)
    return pl.pallas_call(
        functools.partial(rows_kernel, blocks, groups, part, places, len(added)),
        out_shape=outs,
        in_specs=[SMEM] + [VMEM] * (blocks + 2 * groups + 2 + len(added)),
        out_specs=(VMEM,) * len(outs),
        compiler_params=MEDIUM,
        cost_estimate=cost(6 * blocks * each * width * hid, (wide, down) + outs),
    )(me, *toks, *acts, *hids, wide, down, *added)


TN = (((0,), (0,)), ((), ()))


def wide_grad_kernel(blocks, groups, first, count, order_ref, *refs):
    toks, hids, start, outs = refs[:blocks], refs[blocks : blocks + groups], refs[blocks + groups : -count], refs[-count:]
    hidden_grads = jnp.concatenate([h[...] for h in hids], axis=0)
    tile = outs[0].shape[0]
    for k in range(count):
        at = pl.multiple_of(order_ref[first + k] * tile, tile)
        rows = jnp.concatenate([t[:, pl.ds(at, tile)] for t in toks], axis=0)
        total = lax.dot_general(rows, hidden_grads, TN, preferred_element_type=F32)
        if start:
            total = total + start[0][...]
        outs[k][...] = total.astype(outs[k].dtype)


def wide_grads(order, toks, hids, width, first, count, start=(), kind=BF16):
    blocks = len(toks)
    each = toks[0].shape[0]
    both, tile = hids[0].shape[1], width // 4
    out = jax.ShapeDtypeStruct((tile, both), kind)
    return pl.pallas_call(
        functools.partial(wide_grad_kernel, blocks, len(hids), first, count),
        out_shape=(out,) * count,
        in_specs=[SMEM] + [VMEM] * (blocks + len(hids) + len(start)),
        out_specs=(VMEM,) * count,
        compiler_params=MEDIUM,
        cost_estimate=cost(2 * count * blocks * each * both * tile, tuple(hids) + (out,) * count),
    )(order, *toks, *hids, *start)


def down_grad_kernel(groups, order_ref, *refs):
    acts, ogs, outs, full = refs[:groups], refs[groups : 2 * groups], refs[2 * groups : -1], refs[-1]
    act = jnp.concatenate([a[...] for a in acts], axis=0)
    step = full.shape[1]
    size = full.shape[0] // 4
    for j in range(4):
        columns = slice(j * step, (j + 1) * step)
        og = jnp.concatenate([o[:, columns] for o in ogs], axis=0)
        full[...] = lax.dot_general(act, og, TN, preferred_element_type=F32)
        for k in range(4):
            at = pl.multiple_of(order_ref[k] * size, size)
            outs[k][:, columns] = full[pl.ds(at, size), :].astype(BF16)


def down_grads(order, acts, ogs):
    hid = acts[0].shape[1]
    rows = sum(a.shape[0] for a in acts)
    width = ogs[0].shape[1]
    out = jax.ShapeDtypeStruct((hid // 4, width), BF16)
    return pl.pallas_call(
        functools.partial(down_grad_kernel, len(acts)),
        out_shape=(out,) * 4,
        in_specs=[SMEM] + [VMEM] * (2 * len(acts)),
        out_specs=(VMEM,) * 4,
        scratch_shapes=[pltpu.VMEM((hid, width // 4), F32)],
        compiler_params=MEDIUM,
        cost_estimate=cost(2 * rows * hid * width, tuple(acts) + tuple(ogs)),
    )(order, *acts, *ogs)


PIECE = 256


def pieces(wide_shape, down_shape):
    at = 0
    for number, (rows, columns) in enumerate((wide_shape, down_shape)):
        for j in range(columns // PIECE):
            yield number, slice(at, at + rows), slice(j * PIECE, (j + 1) * PIECE)
            at += rows


def join_kernel(order_ref, wide_own, down_own, *refs):
    came, out_ref = refs[:-1], refs[-1]
    owns = wide_own, down_own
    for number, rows, part in pieces(wide_own.shape, down_own.shape):
        own = owns[number][:, part]
        if came:
            other = came[0][rows, :] if len(came) == 1 else came[number][:, part]
            other = jnp.where(order_ref[4] == 1, other.astype(F32), 0.0)
            own = (own.astype(F32) + other).astype(BF16)
        out_ref[rows, :] = own


def join(order, wide_own, down_own, *came):
    out = jax.ShapeDtypeStruct(((wide_own.size + down_own.size) // PIECE, PIECE), BF16)
    return pl.pallas_call(
        join_kernel,
        out_shape=out,
        in_specs=[SMEM] + [VMEM] * (2 + len(came)),
        compiler_params=SMALL,
        cost_estimate=cost(wide_own.size, (out,)),
    )(order, wide_own, down_own, *came)


def base_kernel(order_ref, wide_own, down_own, wide_one, down_one, two_ref, wide_out, down_out):
    owns, ones, outs = (wide_own, down_own), (wide_one, down_one), (wide_out, down_out)
    for number, rows, part in pieces(wide_own.shape, down_own.shape):
        came = ones[number][:, part].astype(F32) + two_ref[rows, :].astype(F32)
        came = jnp.where(order_ref[4] == 1, 0.0, came)
        outs[number][:, part] = owns[number][:, part].astype(F32) + came


def base_terms(order, wide_own, down_own, wide_one, down_one, two):
    outs = tuple(jax.ShapeDtypeStruct(a.shape, F32) for a in (wide_own, down_own))
    return pl.pallas_call(
        base_kernel,
        out_shape=outs,
        in_specs=[SMEM] + [VMEM] * 5,
        compiler_params=SMALL,
        cost_estimate=cost(wide_own.size, outs),
    )(order, wide_own, down_own, wide_one, down_one, two)


def finish_kernel(wide_ref, down_ref, up_ref, low_ref, gate_out, up_out, down_out):
    bases, outs = (wide_ref, down_ref), ((gate_out, up_out), (down_out,))
    for number, rows, part in pieces(wide_ref.shape, down_ref.shape):
        came = up_ref[rows, :].astype(F32) + low_ref[rows, :].astype(F32)
        total = bases[number][:, part] + came
        for k, out in enumerate(outs[number]):
            size = out.shape[1]
            a, b = max(part.start, k * size), min(part.stop, (k + 1) * size)
            if a < b:
                out[:, a - k * size : b - k * size] = total[:, a - part.start : b - part.start]


def finish(wide, down, one, two):
    rows, both = wide.shape
    outs = (jax.ShapeDtypeStruct((rows, both // 2), F32),) * 2 + (jax.ShapeDtypeStruct(down.shape, F32),)
    return pl.pallas_call(
        finish_kernel,
        out_shape=outs,
        compiler_params=SMALL,
        cost_estimate=cost(wide.size, outs),
    )(wide, down, one, two)


def after(values, earlier):
    return lax.optimization_barrier((values, earlier))[0]


def pair_sums_kernel(places, *refs):
    for terms, out_ref in zip(places, refs[-2:]):
        each = out_ref.shape[0]
        values = [refs[k][block * each : (block + 1) * each, :].astype(F32) for k, block in terms]
        out_ref[...] = sum(values[1:], values[0]).astype(BF16)


def pair_sums(each, first, second):
    arrays = [a for a, _ in first + second]
    blocks = [block for _, block in first + second]
    numbered = tuple(enumerate(blocks))
    out = jax.ShapeDtypeStruct((each, arrays[0].shape[1]), BF16)
    return pl.pallas_call(
        functools.partial(pair_sums_kernel, (numbered[: len(first)], numbered[len(first) :])),
        out_shape=(out, out),
        in_specs=[VMEM] * len(arrays),
        out_specs=(VMEM, VMEM),
        compiler_params=SMALL,
        cost_estimate=cost(out.size, (out,)),
    )(*arrays)


LINE_ORDER = ((3, 2, 1, 0, 0), (0, 3, 2, 1, 1), (3, 0, 1, 2, 1), (0, 1, 2, 3, 0))


def per_device(tokens, expert_ids, gates, w_gate, w_up, w_down, cotangent):
    width = tokens.shape[1]
    group = lax.axis_size("expert")
    shards = lax.axis_size("dp")
    assert group == 8
    me = lax.axis_index("expert").astype(jnp.int32).reshape(1)
    z = lax.axis_index("dp")
    wg, wu, wd = w_gate[0], w_up[0], w_down[0]

    def flip(array, bit):
        return lax.ppermute(array, "expert", [(i, i ^ bit) for i in range(group)])

    line = shards == 4
    table = jnp.asarray(LINE_ORDER if line else ((0, 1, 2, 3, 0),), jnp.int32)
    order = table[z if line else 0]
    tokens = after(tokens, (order, me))
    cot_0 = cotangent
    tok_0 = packed(tokens, expert_ids, gates)
    tok_x, cot_y = flip(tok_0, NEAR), flip(cot_0, FAR)
    cot_x, tok_y = flip(cot_0, NEAR), flip(tok_0, FAR)
    cot_d, tok_d = flip(cot_y, NEAR), flip(tok_x, FAR)

    toks_a, cots_a = [tok_0, tok_x, tok_y], [cot_0, cot_x, cot_y]
    wide_panel, down_panel = panels(wg, wu, wd)
    cots_a += [flip(c, CORE) for c in [after(cot_0, wide_panel)] + cots_a[1:]]
    toks_a += [flip(t, CORE) for t in toks_a]
    act_a, hid_a, og_a = hidden(me, toks_a, cots_a, wide_panel, down_panel)
    (wide_part,) = wide_grads(order, toks_a, (hid_a,), width, 0, 1, kind=F32)
    tok_d, cot_d = after((tok_d, cot_d), wide_part)
    tok_e, cot_e = flip(tok_d, CORE), flip(cot_d, CORE)
    act_d, hid_d, og_d = hidden(me, [tok_d], [cot_d], wide_panel, down_panel)
    tok_e, cot_e = after((tok_e, cot_e), hid_d)
    act_e, hid_e, og_e = hidden(me, [tok_e], [cot_e], wide_panel, down_panel)

    def move(array, pairs):
        return lax.ppermute(array, "dp", pairs) if line else array

    one_pairs = [(0, 1), (1, 0), (2, 3), (3, 2)]
    two_pairs = [(0, 1), (1, 3), (3, 2), (2, 0)]
    end_pairs, mid_pairs = [(0, 1), (3, 2)], [(1, 2), (2, 1)]
    toks = toks_a + [tok_d, tok_e]
    wide_0 = wide_grads(order, [tok_d, tok_e], (hid_d, hid_e), width, 0, 1, start=(wide_part,))
    wide_one = move(wide_0[0], one_pairs)
    act_a = after(act_a, wide_0)
    down = down_grads(order, (act_a, act_d, act_e), (og_a, og_d, og_e))
    down_one = move(down[0], one_pairs)
    hid_a = after(hid_a, down)
    wide = wide_0 + wide_grads(order, toks, (hid_a, hid_d, hid_e), width, 1, 3)
    act_a = after(act_a, wide[1])
    there = tuple((0, i) for i in range(4)), tuple((1, i) for i in range(4))
    sent = rows_out(me, toks_a[3:] + [tok_e], (act_a, act_e), (hid_a, hid_e), 1, wide_panel, down_panel, (), there)
    if line:
        wide_one, down_one = after((wide_one, down_one), sent)
        second = join(order, wide[1], down[1], wide_one, down_one)
        two = move(second, two_pairs)
        sent = after(sent, second)
    sent = [flip(a, CORE) for a in sent]
    here = ((0, 0), (2, 0), (1, 0), (2, 1)), ((3, 0), (4, 0), (5, 0), (5, 1))
    kept = rows_out(me, toks_a[:3] + [tok_d], (act_a, act_d), (hid_a, hid_d), 0, wide_panel, down_panel, sent, here)
    out_0, out_y, out_near, grad_0, grad_x, grad_far = kept
    out_near, grad_far = flip(out_near, NEAR), flip(grad_far, FAR)
    hid_size = wd.shape[0]
    each = tokens.shape[0]
    if line:
        own_last = join(order, *after((wide[2], down[2]), kept))
        two = after(two, own_last)
        last = join(order, wide[2], down[2], two)
        last_mid, last_end = move(last, mid_pairs), move(own_last, end_pairs)
        out_near, grad_far = after((out_near, grad_far), last)
    out_y, grad_x = pair_sums(each, [(out_y, 0), (out_near, 1)], [(grad_x, 0), (grad_far, 1)])
    out_yy, grad_xx = flip(out_y, FAR), flip(grad_x, NEAR)
    if line:
        base = base_terms(order, wide[3], down[3], wide_one, down_one, after(two, (out_y, grad_x)))
    mixed, grad_tokens = pair_sums(
        each, [(out_0, 0), (out_near, 0), (out_yy, 0)], [(grad_0, 0), (grad_far, 0), (grad_xx, 0)]
    )
    if line:
        base, mixed, grad_tokens = lax.optimization_barrier((base, mixed, grad_tokens))
        last_end = after(last_end, (mixed, grad_tokens))
        last_mid = after(last_mid, last_end)
        grad_gate, grad_up, grad_down = finish(*base, last_mid, last_end)
    else:
        wide_all = jnp.concatenate(wide, axis=0)
        grad_wide = lax.psum_scatter(wide_all, "dp", scatter_dimension=0, tiled=True).astype(F32)
        grad_gate, grad_up = grad_wide[:, :hid_size], grad_wide[:, hid_size:]
        grad_down = lax.psum_scatter(jnp.concatenate(down, axis=0), "dp", scatter_dimension=0, tiled=True).astype(F32)
    return (mixed, grad_tokens, grad_gate[None], grad_up[None], grad_down[None])


def solution(mesh):
    return jax.shard_map(
        per_device,
        mesh=mesh,
        in_specs=(
            P(("dp", "expert"), None),
            P(("dp", "expert"), None),
            P(("dp", "expert"), None),
            P("expert", None, None),
            P("expert", None, None),
            P("expert", None, None),
            P(("dp", "expert"), None),
        ),
        out_specs=(
            P(("dp", "expert"), None),
            P(("dp", "expert"), None),
            P("expert", "dp", None),
            P("expert", "dp", None),
            P("expert", "dp", None),
        ),
        check_vma=False,
    )
```

```python
import functools

import jax
import jax.numpy as jnp
from jax import lax
from jax.experimental import pallas as pl
from jax.experimental.pallas import tpu as pltpu
from jax.sharding import PartitionSpec as P

F32 = jnp.float32
BF16 = jnp.bfloat16
LANES = 128
CORE, NEAR, FAR = 1, 2, 4
MEDIUM = pltpu.CompilerParams(vmem_limit_bytes=24 * 1024 * 1024)
SMALL = pltpu.CompilerParams(vmem_limit_bytes=12 * 1024 * 1024)
VMEM = pl.BlockSpec(memory_space=pltpu.VMEM)
SMEM = pl.BlockSpec(memory_space=pltpu.SMEM)
NT = (((1,), (1,)), ((), ()))


def cost(flops, arrays):
    size = sum(a.size * a.dtype.itemsize for a in arrays)
    return pl.CostEstimate(flops=flops // 64, bytes_accessed=size // 64, transcendentals=0)


def own_gate(gate_rows, expert_num):
    lane = lax.broadcasted_iota(jnp.int32, gate_rows.shape, 1)
    kept = jnp.where(lane == expert_num, gate_rows.astype(F32), 0.0)
    return jnp.sum(kept, axis=1, keepdims=True)


def pack_kernel(tok_ref, ids_ref, gates_ref, out_ref):
    rows, width = tok_ref.shape
    out_ref[:, :width] = tok_ref[...]
    lane = lax.broadcasted_iota(jnp.int32, (rows, LANES), 1)
    ids, gates = ids_ref[...], gates_ref[...].astype(F32)
    total = jnp.zeros((rows, LANES), F32)
    for k in range(ids.shape[1]):
        total = total + jnp.where(ids[:, k : k + 1] == lane, gates[:, k : k + 1], 0.0)
    out_ref[:, width:] = total.astype(BF16)


def packed(tokens, ids, gates):
    rows, width = tokens.shape
    return pl.pallas_call(
        pack_kernel,
        out_shape=jax.ShapeDtypeStruct((rows, width + LANES), BF16),
        compiler_params=SMALL,
    )(tokens, ids, gates)


def panels_kernel(wg_ref, wu_ref, wd_ref, wide_ref, down_ref):
    hid = wg_ref.shape[1]
    wide_ref[:, :hid] = wg_ref[...]
    wide_ref[:, hid:] = wu_ref[...]
    down_ref[...] = wd_ref[...]


def panels(wg, wu, wd):
    width, hid = wg.shape
    outs = (jax.ShapeDtypeStruct((width, 2 * hid), BF16), jax.ShapeDtypeStruct(wd.shape, BF16))
    return pl.pallas_call(
        panels_kernel,
        out_shape=outs,
        in_specs=[VMEM] * 3,
        out_specs=(VMEM, VMEM),
        compiler_params=SMALL,
        cost_estimate=cost(width, outs),
    )(wg, wu, wd)


def hidden_kernel(blocks, me_ref, *refs):
    toks, cots = refs[:blocks], refs[blocks : 2 * blocks]
    wide_ref, down_ref, act_ref, hid_ref, og_ref = refs[2 * blocks :]
    each, width = cots[0].shape
    hid = down_ref.shape[0]
    rows = jnp.concatenate([t[:, :width] for t in toks], axis=0)
    pre = jnp.dot(rows, wide_ref[...], preferred_element_type=F32)
    for i in range(blocks):
        gate_col = own_gate(toks[i][:, width:], me_ref[0])
        og_ref[i * each : (i + 1) * each, :] = (gate_col * cots[i][...].astype(F32)).astype(BF16)
    act_grad = lax.dot_general(og_ref[...], down_ref[...], NT, preferred_element_type=F32)
    pre_gate, pre_up = pre[:, :hid], pre[:, hid:]
    s = 1.0 / (1.0 + jnp.exp(-pre_gate))
    act_ref[...] = (pre_gate * s * pre_up).astype(BF16)
    hid_ref[:, :hid] = (act_grad * pre_up * s * (1.0 + pre_gate * (1.0 - s))).astype(BF16)
    hid_ref[:, hid:] = (act_grad * pre_gate * s).astype(BF16)


def hidden(me, toks, cots, wide, down):
    blocks = len(toks)
    rows = blocks * cots[0].shape[0]
    hid, width = down.shape
    outs = tuple(jax.ShapeDtypeStruct((rows, n), BF16) for n in (hid, 2 * hid, width))
    return pl.pallas_call(
        functools.partial(hidden_kernel, blocks),
        out_shape=outs,
        in_specs=[SMEM] + [VMEM] * (2 * blocks + 2),
        out_specs=(VMEM,) * 3,
        compiler_params=MEDIUM,
        cost_estimate=cost(6 * rows * width * hid, (*toks, *cots, wide, down) + outs),
    )(me, *toks, *cots, wide, down)


def rows_kernel(blocks, groups, part, places, more, me_ref, *refs):
    toks, refs = refs[:blocks], refs[blocks:]
    acts, hids, refs = refs[:groups], refs[groups : 2 * groups], refs[2 * groups :]
    wide_ref, down_ref = refs[:2]
    added, outs = refs[2 : 2 + more], refs[2 + more :]
    width = down_ref.shape[1]
    each = toks[0].shape[0]
    gate_col = own_gate(jnp.concatenate([t[:, width:] for t in toks], axis=0), me_ref[0])

    def joined(refs):
        size = refs[0].shape[0] // 2
        return jnp.concatenate([refs[0][part * size : (part + 1) * size, :]] + [r[...] for r in refs[1:]], axis=0)

    def put(values, number, columns):
        for i in range(blocks):
            piece = values[i * each : (i + 1) * each]
            if more:
                other = added[number][i * each : (i + 1) * each, columns]
                piece = (piece.astype(F32) + other.astype(F32)).astype(BF16)
            array, block = places[number][i]
            outs[array][block * each : (block + 1) * each, columns] = piece

    act, hidden_grads = joined(acts), joined(hids)
    step = width // 4
    for j in range(4):
        columns = slice(j * step, (j + 1) * step)
        expert_out = jnp.dot(act, down_ref[:, columns], preferred_element_type=F32)
        put((gate_col * expert_out).astype(BF16), 0, columns)
        grad = lax.dot_general(hidden_grads, wide_ref[columns, :], NT, preferred_element_type=F32)
        put(grad.astype(BF16), 1, columns)


def rows_out(me, toks, acts, hids, part, wide, down, added, places):
    blocks, groups = len(toks), len(acts)
    each = toks[0].shape[0]
    hid, width = down.shape
    flat = places[0] + places[1]
    sizes = [sum(array == k for array, _ in flat) for k in range(1 + max(array for array, _ in flat))]
    outs = tuple(jax.ShapeDtypeStruct((n * each, width), BF16) for n in sizes)
    return pl.pallas_call(
        functools.partial(rows_kernel, blocks, groups, part, places, len(added)),
        out_shape=outs,
        in_specs=[SMEM] + [VMEM] * (blocks + 2 * groups + 2 + len(added)),
        out_specs=(VMEM,) * len(outs),
        compiler_params=MEDIUM,
        cost_estimate=cost(6 * blocks * each * width * hid, (wide, down) + outs),
    )(me, *toks, *acts, *hids, wide, down, *added)


TN = (((0,), (0,)), ((), ()))


def wide_grad_kernel(blocks, groups, first, count, order_ref, *refs):
    toks, hids, start, outs = refs[:blocks], refs[blocks : blocks + groups], refs[blocks + groups : -count], refs[-count:]
    hidden_grads = jnp.concatenate([h[...] for h in hids], axis=0)
    tile = outs[0].shape[0]
    for k in range(count):
        at = pl.multiple_of(order_ref[first + k] * tile, tile)
        rows = jnp.concatenate([t[:, pl.ds(at, tile)] for t in toks], axis=0)
        total = lax.dot_general(rows, hidden_grads, TN, preferred_element_type=F32)
        if start:
            total = total + start[0][...]
        outs[k][...] = total.astype(outs[k].dtype)


def wide_grads(order, toks, hids, width, first, count, start=(), kind=BF16):
    blocks = len(toks)
    each = toks[0].shape[0]
    both, tile = hids[0].shape[1], width // 4
    out = jax.ShapeDtypeStruct((tile, both), kind)
    return pl.pallas_call(
        functools.partial(wide_grad_kernel, blocks, len(hids), first, count),
        out_shape=(out,) * count,
        in_specs=[SMEM] + [VMEM] * (blocks + len(hids) + len(start)),
        out_specs=(VMEM,) * count,
        compiler_params=MEDIUM,
        cost_estimate=cost(2 * count * blocks * each * both * tile, tuple(hids) + (out,) * count),
    )(order, *toks, *hids, *start)


def down_grad_kernel(groups, order_ref, *refs):
    acts, ogs, outs, full = refs[:groups], refs[groups : 2 * groups], refs[2 * groups : -1], refs[-1]
    act = jnp.concatenate([a[...] for a in acts], axis=0)
    step = full.shape[1]
    size = full.shape[0] // 4
    for j in range(4):
        columns = slice(j * step, (j + 1) * step)
        og = jnp.concatenate([o[:, columns] for o in ogs], axis=0)
        full[...] = lax.dot_general(act, og, TN, preferred_element_type=F32)
        for k in range(4):
            at = pl.multiple_of(order_ref[k] * size, size)
            outs[k][:, columns] = full[pl.ds(at, size), :].astype(BF16)


def down_grads(order, acts, ogs):
    hid = acts[0].shape[1]
    rows = sum(a.shape[0] for a in acts)
    width = ogs[0].shape[1]
    out = jax.ShapeDtypeStruct((hid // 4, width), BF16)
    return pl.pallas_call(
        functools.partial(down_grad_kernel, len(acts)),
        out_shape=(out,) * 4,
        in_specs=[SMEM] + [VMEM] * (2 * len(acts)),
        out_specs=(VMEM,) * 4,
        scratch_shapes=[pltpu.VMEM((hid, width // 4), F32)],
        compiler_params=MEDIUM,
        cost_estimate=cost(2 * rows * hid * width, tuple(acts) + tuple(ogs)),
    )(order, *acts, *ogs)


PIECE = 256


def pieces(wide_shape, down_shape):
    at = 0
    for number, (rows, columns) in enumerate((wide_shape, down_shape)):
        for j in range(columns // PIECE):
            yield number, slice(at, at + rows), slice(j * PIECE, (j + 1) * PIECE)
            at += rows


def join_kernel(order_ref, wide_own, down_own, *refs):
    came, out_ref = refs[:-1], refs[-1]
    owns = wide_own, down_own
    parts = list(pieces(wide_own.shape, down_own.shape))

    def own_terms():
        for number, rows, part in parts:
            out_ref[rows, :] = owns[number][:, part]

    def with_arrivals():
        for number, rows, part in parts:
            other = came[0][rows, :] if len(came) == 1 else came[number][:, part]
            out_ref[rows, :] = owns[number][:, part] + other

    if came:
        pl.when(order_ref[4] == 0)(own_terms)
        pl.when(order_ref[4] == 1)(with_arrivals)
    else:
        own_terms()


def join(order, wide_own, down_own, *came):
    out = jax.ShapeDtypeStruct(((wide_own.size + down_own.size) // PIECE, PIECE), BF16)
    return pl.pallas_call(
        join_kernel,
        out_shape=out,
        in_specs=[SMEM] + [VMEM] * (2 + len(came)),
        compiler_params=SMALL,
        cost_estimate=cost(wide_own.size, (out,)),
    )(order, wide_own, down_own, *came)


def base_kernel(order_ref, wide_own, down_own, wide_one, down_one, two_ref, wide_out, down_out):
    owns, ones, outs = (wide_own, down_own), (wide_one, down_one), (wide_out, down_out)
    for number, rows, part in pieces(wide_own.shape, down_own.shape):
        came = ones[number][:, part].astype(F32) + two_ref[rows, :].astype(F32)
        came = jnp.where(order_ref[4] == 1, 0.0, came)
        outs[number][:, part] = owns[number][:, part].astype(F32) + came


def base_terms(order, wide_own, down_own, wide_one, down_one, two):
    outs = tuple(jax.ShapeDtypeStruct(a.shape, F32) for a in (wide_own, down_own))
    return pl.pallas_call(
        base_kernel,
        out_shape=outs,
        in_specs=[SMEM] + [VMEM] * 5,
        compiler_params=SMALL,
        cost_estimate=cost(wide_own.size, outs),
    )(order, wide_own, down_own, wide_one, down_one, two)


def finish_kernel(wide_ref, down_ref, up_ref, low_ref, gate_out, up_out, down_out):
    bases, outs = (wide_ref, down_ref), ((gate_out, up_out), (down_out,))
    for number, rows, part in pieces(wide_ref.shape, down_ref.shape):
        came = up_ref[rows, :].astype(F32) + low_ref[rows, :].astype(F32)
        total = bases[number][:, part] + came
        for k, out in enumerate(outs[number]):
            size = out.shape[1]
            a, b = max(part.start, k * size), min(part.stop, (k + 1) * size)
            if a < b:
                out[:, a - k * size : b - k * size] = total[:, a - part.start : b - part.start]


def finish(wide, down, one, two):
    rows, both = wide.shape
    outs = (jax.ShapeDtypeStruct((rows, both // 2), F32),) * 2 + (jax.ShapeDtypeStruct(down.shape, F32),)
    return pl.pallas_call(
        finish_kernel,
        out_shape=outs,
        compiler_params=SMALL,
        cost_estimate=cost(wide.size, outs),
    )(wide, down, one, two)


def after(values, earlier):
    return lax.optimization_barrier((values, earlier))[0]


def pair_sums_kernel(places, *refs):
    for terms, out_ref in zip(places, refs[-2:]):
        each = out_ref.shape[0]
        values = [refs[k][block * each : (block + 1) * each, :].astype(F32) for k, block in terms]
        out_ref[...] = sum(values[1:], values[0]).astype(BF16)


def pair_sums(each, first, second):
    arrays = [a for a, _ in first + second]
    blocks = [block for _, block in first + second]
    numbered = tuple(enumerate(blocks))
    out = jax.ShapeDtypeStruct((each, arrays[0].shape[1]), BF16)
    return pl.pallas_call(
        functools.partial(pair_sums_kernel, (numbered[: len(first)], numbered[len(first) :])),
        out_shape=(out, out),
        in_specs=[VMEM] * len(arrays),
        out_specs=(VMEM, VMEM),
        compiler_params=SMALL,
        cost_estimate=cost(out.size, (out,)),
    )(*arrays)


LINE_ORDER = ((3, 2, 1, 0, 0), (0, 3, 2, 1, 1), (3, 0, 1, 2, 1), (0, 1, 2, 3, 0))


def per_device(tokens, expert_ids, gates, w_gate, w_up, w_down, cotangent):
    width = tokens.shape[1]
    group = lax.axis_size("expert")
    shards = lax.axis_size("dp")
    assert group == 8
    me = lax.axis_index("expert").astype(jnp.int32).reshape(1)
    z = lax.axis_index("dp")
    wg, wu, wd = w_gate[0], w_up[0], w_down[0]

    def flip(array, bit):
        return lax.ppermute(array, "expert", [(i, i ^ bit) for i in range(group)])

    line = shards == 4
    table = jnp.asarray(LINE_ORDER if line else ((0, 1, 2, 3, 0),), jnp.int32)
    order = table[z if line else 0]
    tokens = after(tokens, (order, me))
    cot_0 = cotangent
    tok_0 = packed(tokens, expert_ids, gates)
    tok_x, cot_y = flip(tok_0, NEAR), flip(cot_0, FAR)
    cot_x, tok_y = flip(cot_0, NEAR), flip(tok_0, FAR)
    cot_d, tok_d = flip(cot_y, NEAR), flip(tok_x, FAR)

    toks_a, cots_a = [tok_0, tok_x, tok_y], [cot_0, cot_x, cot_y]
    wide_panel, down_panel = panels(wg, wu, wd)
    cots_a += [flip(c, CORE) for c in [after(cot_0, wide_panel)] + cots_a[1:]]
    toks_a += [flip(t, CORE) for t in toks_a]
    act_a, hid_a, og_a = hidden(me, toks_a, cots_a, wide_panel, down_panel)
    (wide_part,) = wide_grads(order, toks_a, (hid_a,), width, 0, 1, kind=F32)
    tok_d, cot_d = after((tok_d, cot_d), wide_part)
    tok_e, cot_e = flip(tok_d, CORE), flip(cot_d, CORE)
    act_d, hid_d, og_d = hidden(me, [tok_d], [cot_d], wide_panel, down_panel)
    tok_e, cot_e = after((tok_e, cot_e), hid_d)
    act_e, hid_e, og_e = hidden(me, [tok_e], [cot_e], wide_panel, down_panel)

    def move(array, pairs):
        return lax.ppermute(array, "dp", pairs) if line else array

    one_pairs = [(0, 1), (1, 0), (2, 3), (3, 2)]
    two_pairs = [(0, 1), (1, 3), (3, 2), (2, 0)]
    end_pairs, mid_pairs = [(0, 1), (3, 2)], [(1, 2), (2, 1)]
    toks = toks_a + [tok_d, tok_e]
    wide_0 = wide_grads(order, [tok_d, tok_e], (hid_d, hid_e), width, 0, 1, start=(wide_part,))
    wide_one = move(wide_0[0], one_pairs)
    act_a = after(act_a, wide_0)
    down = down_grads(order, (act_a, act_d, act_e), (og_a, og_d, og_e))
    down_one = move(down[0], one_pairs)
    hid_a = after(hid_a, down)
    wide = wide_0 + wide_grads(order, toks, (hid_a, hid_d, hid_e), width, 1, 3)
    act_a = after(act_a, wide[1])
    there = tuple((0, i) for i in range(4)), tuple((1, i) for i in range(4))
    sent = rows_out(me, toks_a[3:] + [tok_e], (act_a, act_e), (hid_a, hid_e), 1, wide_panel, down_panel, (), there)
    if line:
        wide_one, down_one = after((wide_one, down_one), sent)
        second = join(order, wide[1], down[1], wide_one, down_one)
        two = move(second, two_pairs)
        sent = after(sent, second)
    sent = [flip(a, CORE) for a in sent]
    here = ((0, 0), (2, 0), (1, 0), (2, 1)), ((3, 0), (4, 0), (5, 0), (5, 1))
    kept = rows_out(me, toks_a[:3] + [tok_d], (act_a, act_d), (hid_a, hid_d), 0, wide_panel, down_panel, sent, here)
    out_0, out_y, out_near, grad_0, grad_x, grad_far = kept
    out_near, grad_far = flip(out_near, NEAR), flip(grad_far, FAR)
    hid_size = wd.shape[0]
    each = tokens.shape[0]
    if line:
        own_last = join(order, *after((wide[2], down[2]), kept))
        two = after(two, own_last)
        last = join(order, wide[2], down[2], two)
        last_mid, last_end = move(last, mid_pairs), move(own_last, end_pairs)
        out_near, grad_far = after((out_near, grad_far), last)
    out_y, grad_x = pair_sums(each, [(out_y, 0), (out_near, 1)], [(grad_x, 0), (grad_far, 1)])
    out_yy, grad_xx = flip(out_y, FAR), flip(grad_x, NEAR)
    if line:
        base = base_terms(order, wide[3], down[3], wide_one, down_one, after(two, (out_y, grad_x)))
    mixed, grad_tokens = pair_sums(
        each, [(out_0, 0), (out_near, 0), (out_yy, 0)], [(grad_0, 0), (grad_far, 0), (grad_xx, 0)]
    )
    if line:
        base, mixed, grad_tokens = lax.optimization_barrier((base, mixed, grad_tokens))
        last_end = after(last_end, (mixed, grad_tokens))
        last_mid = after(last_mid, last_end)
        grad_gate, grad_up, grad_down = finish(*base, last_mid, last_end)
    else:
        wide_all = jnp.concatenate(wide, axis=0)
        grad_wide = lax.psum_scatter(wide_all, "dp", scatter_dimension=0, tiled=True).astype(F32)
        grad_gate, grad_up = grad_wide[:, :hid_size], grad_wide[:, hid_size:]
        grad_down = lax.psum_scatter(jnp.concatenate(down, axis=0), "dp", scatter_dimension=0, tiled=True).astype(F32)
    return (mixed, grad_tokens, grad_gate[None], grad_up[None], grad_down[None])


def solution(mesh):
    return jax.shard_map(
        per_device,
        mesh=mesh,
        in_specs=(
            P(("dp", "expert"), None),
            P(("dp", "expert"), None),
            P(("dp", "expert"), None),
            P("expert", None, None),
            P("expert", None, None),
            P("expert", None, None),
            P(("dp", "expert"), None),
        ),
        out_specs=(
            P(("dp", "expert"), None),
            P(("dp", "expert"), None),
            P("expert", "dp", None),
            P("expert", "dp", None),
            P("expert", "dp", None),
        ),
        check_vma=False,
    )
```

```python
import functools

import jax
import jax.numpy as jnp
from jax import lax
from jax.experimental import pallas as pl
from jax.experimental.pallas import tpu as pltpu
from jax.sharding import PartitionSpec as P

F32 = jnp.float32
BF16 = jnp.bfloat16
LANES = 128
CORE, NEAR, FAR = 1, 2, 4
MEDIUM = pltpu.CompilerParams(vmem_limit_bytes=24 * 1024 * 1024)
SMALL = pltpu.CompilerParams(vmem_limit_bytes=12 * 1024 * 1024)
VMEM = pl.BlockSpec(memory_space=pltpu.VMEM)
SMEM = pl.BlockSpec(memory_space=pltpu.SMEM)
NT = (((1,), (1,)), ((), ()))


def cost(flops, arrays):
    size = sum(a.size * a.dtype.itemsize for a in arrays)
    return pl.CostEstimate(flops=flops // 64, bytes_accessed=size // 64, transcendentals=0)


def own_gate(gate_rows, expert_num):
    lane = lax.broadcasted_iota(jnp.int32, gate_rows.shape, 1)
    kept = jnp.where(lane == expert_num, gate_rows.astype(F32), 0.0)
    return jnp.sum(kept, axis=1, keepdims=True)


def pack_kernel(tok_ref, ids_ref, gates_ref, out_ref):
    rows, width = tok_ref.shape
    out_ref[:, :width] = tok_ref[...]
    lane = lax.broadcasted_iota(jnp.int32, (rows, LANES), 1)
    ids, gates = ids_ref[...], gates_ref[...].astype(F32)
    total = jnp.zeros((rows, LANES), F32)
    for k in range(ids.shape[1]):
        total = total + jnp.where(ids[:, k : k + 1] == lane, gates[:, k : k + 1], 0.0)
    out_ref[:, width:] = total.astype(BF16)


def packed(tokens, ids, gates):
    rows, width = tokens.shape
    return pl.pallas_call(
        pack_kernel,
        out_shape=jax.ShapeDtypeStruct((rows, width + LANES), BF16),
        compiler_params=SMALL,
    )(tokens, ids, gates)


def panels_kernel(wg_ref, wu_ref, wd_ref, wide_ref, down_ref):
    hid = wg_ref.shape[1]
    wide_ref[:, :hid] = wg_ref[...]
    wide_ref[:, hid:] = wu_ref[...]
    down_ref[...] = wd_ref[...]


def panels(wg, wu, wd):
    width, hid = wg.shape
    outs = (jax.ShapeDtypeStruct((width, 2 * hid), BF16), jax.ShapeDtypeStruct(wd.shape, BF16))
    return pl.pallas_call(
        panels_kernel,
        out_shape=outs,
        in_specs=[VMEM] * 3,
        out_specs=(VMEM, VMEM),
        compiler_params=SMALL,
        cost_estimate=cost(width, outs),
    )(wg, wu, wd)


def hidden_kernel(blocks, me_ref, *refs):
    toks, cots = refs[:blocks], refs[blocks : 2 * blocks]
    wide_ref, down_ref, act_ref, hid_ref, og_ref = refs[2 * blocks :]
    each, width = cots[0].shape
    hid = down_ref.shape[0]
    rows = jnp.concatenate([t[:, :width] for t in toks], axis=0)
    pre = jnp.dot(rows, wide_ref[...], preferred_element_type=F32)
    for i in range(blocks):
        gate_col = own_gate(toks[i][:, width:], me_ref[0])
        og_ref[i * each : (i + 1) * each, :] = (gate_col * cots[i][...].astype(F32)).astype(BF16)
    act_grad = lax.dot_general(og_ref[...], down_ref[...], NT, preferred_element_type=F32)
    pre_gate, pre_up = pre[:, :hid], pre[:, hid:]
    s = 1.0 / (1.0 + jnp.exp(-pre_gate))
    act_ref[...] = (pre_gate * s * pre_up).astype(BF16)
    hid_ref[:, :hid] = (act_grad * pre_up * s * (1.0 + pre_gate * (1.0 - s))).astype(BF16)
    hid_ref[:, hid:] = (act_grad * pre_gate * s).astype(BF16)


def hidden(me, toks, cots, wide, down):
    blocks = len(toks)
    rows = blocks * cots[0].shape[0]
    hid, width = down.shape
    outs = tuple(jax.ShapeDtypeStruct((rows, n), BF16) for n in (hid, 2 * hid, width))
    return pl.pallas_call(
        functools.partial(hidden_kernel, blocks),
        out_shape=outs,
        in_specs=[SMEM] + [VMEM] * (2 * blocks + 2),
        out_specs=(VMEM,) * 3,
        compiler_params=MEDIUM,
        cost_estimate=cost(6 * rows * width * hid, (*toks, *cots, wide, down) + outs),
    )(me, *toks, *cots, wide, down)


def rows_kernel(blocks, groups, part, places, more, me_ref, *refs):
    toks, refs = refs[:blocks], refs[blocks:]
    acts, hids, refs = refs[:groups], refs[groups : 2 * groups], refs[2 * groups :]
    wide_ref, down_ref = refs[:2]
    added, outs = refs[2 : 2 + more], refs[2 + more :]
    width = down_ref.shape[1]
    each = toks[0].shape[0]
    gate_col = own_gate(jnp.concatenate([t[:, width:] for t in toks], axis=0), me_ref[0])

    def joined(refs):
        size = refs[0].shape[0] // 2
        return jnp.concatenate([refs[0][part * size : (part + 1) * size, :]] + [r[...] for r in refs[1:]], axis=0)

    def put(values, number, columns):
        for i in range(blocks):
            piece = values[i * each : (i + 1) * each]
            if more:
                other = added[number][i * each : (i + 1) * each, columns]
                piece = (piece.astype(F32) + other.astype(F32)).astype(BF16)
            array, block = places[number][i]
            outs[array][block * each : (block + 1) * each, columns] = piece

    act, hidden_grads = joined(acts), joined(hids)
    step = width // 4
    for j in range(4):
        columns = slice(j * step, (j + 1) * step)
        expert_out = jnp.dot(act, down_ref[:, columns], preferred_element_type=F32)
        put((gate_col * expert_out).astype(BF16), 0, columns)
        grad = lax.dot_general(hidden_grads, wide_ref[columns, :], NT, preferred_element_type=F32)
        put(grad.astype(BF16), 1, columns)


def rows_out(me, toks, acts, hids, part, wide, down, added, places):
    blocks, groups = len(toks), len(acts)
    each = toks[0].shape[0]
    hid, width = down.shape
    flat = places[0] + places[1]
    sizes = [sum(array == k for array, _ in flat) for k in range(1 + max(array for array, _ in flat))]
    outs = tuple(jax.ShapeDtypeStruct((n * each, width), BF16) for n in sizes)
    return pl.pallas_call(
        functools.partial(rows_kernel, blocks, groups, part, places, len(added)),
        out_shape=outs,
        in_specs=[SMEM] + [VMEM] * (blocks + 2 * groups + 2 + len(added)),
        out_specs=(VMEM,) * len(outs),
        compiler_params=MEDIUM,
        cost_estimate=cost(6 * blocks * each * width * hid, (wide, down) + outs),
    )(me, *toks, *acts, *hids, wide, down, *added)


TN = (((0,), (0,)), ((), ()))


def wide_grad_kernel(blocks, groups, first, count, order_ref, *refs):
    toks, hids, start, outs = refs[:blocks], refs[blocks : blocks + groups], refs[blocks + groups : -count], refs[-count:]
    hidden_grads = jnp.concatenate([h[...] for h in hids], axis=0)
    tile = outs[0].shape[0]
    for k in range(count):
        at = pl.multiple_of(order_ref[first + k] * tile, tile)
        rows = jnp.concatenate([t[:, pl.ds(at, tile)] for t in toks], axis=0)
        total = lax.dot_general(rows, hidden_grads, TN, preferred_element_type=F32)
        if start:
            total = total + start[0][...]
        outs[k][...] = total.astype(outs[k].dtype)


def wide_grads(order, toks, hids, width, first, count, start=(), kind=BF16):
    blocks = len(toks)
    each = toks[0].shape[0]
    both, tile = hids[0].shape[1], width // 4
    out = jax.ShapeDtypeStruct((tile, both), kind)
    return pl.pallas_call(
        functools.partial(wide_grad_kernel, blocks, len(hids), first, count),
        out_shape=(out,) * count,
        in_specs=[SMEM] + [VMEM] * (blocks + len(hids) + len(start)),
        out_specs=(VMEM,) * count,
        compiler_params=MEDIUM,
        cost_estimate=cost(2 * count * blocks * each * both * tile, tuple(hids) + (out,) * count),
    )(order, *toks, *hids, *start)


def down_grad_kernel(groups, order_ref, *refs):
    acts, ogs, outs, full = refs[:groups], refs[groups : 2 * groups], refs[2 * groups : -1], refs[-1]
    act = jnp.concatenate([a[...] for a in acts], axis=0)
    step = full.shape[1]
    size = full.shape[0] // 4
    for j in range(4):
        columns = slice(j * step, (j + 1) * step)
        og = jnp.concatenate([o[:, columns] for o in ogs], axis=0)
        full[...] = lax.dot_general(act, og, TN, preferred_element_type=F32)
        for k in range(4):
            at = pl.multiple_of(order_ref[k] * size, size)
            outs[k][:, columns] = full[pl.ds(at, size), :].astype(BF16)


def down_grads(order, acts, ogs):
    hid = acts[0].shape[1]
    rows = sum(a.shape[0] for a in acts)
    width = ogs[0].shape[1]
    out = jax.ShapeDtypeStruct((hid // 4, width), BF16)
    return pl.pallas_call(
        functools.partial(down_grad_kernel, len(acts)),
        out_shape=(out,) * 4,
        in_specs=[SMEM] + [VMEM] * (2 * len(acts)),
        out_specs=(VMEM,) * 4,
        scratch_shapes=[pltpu.VMEM((hid, width // 4), F32)],
        compiler_params=MEDIUM,
        cost_estimate=cost(2 * rows * hid * width, tuple(acts) + tuple(ogs)),
    )(order, *acts, *ogs)


PIECE = 256


def pieces(wide_shape, down_shape):
    at = 0
    for number, (rows, columns) in enumerate((wide_shape, down_shape)):
        for j in range(columns // PIECE):
            yield number, slice(at, at + rows), slice(j * PIECE, (j + 1) * PIECE)
            at += rows


def join_kernel(order_ref, wide_own, down_own, *refs):
    came, out_ref = refs[:-1], refs[-1]
    owns = wide_own, down_own
    parts = list(pieces(wide_own.shape, down_own.shape))

    def own_terms():
        for number, rows, part in parts:
            out_ref[rows, :] = owns[number][:, part]

    def with_arrivals():
        for number, rows, part in parts:
            other = came[0][rows, :] if len(came) == 1 else came[number][:, part]
            out_ref[rows, :] = owns[number][:, part] + other

    if came:
        pl.when(order_ref[4] == 0)(own_terms)
        pl.when(order_ref[4] == 1)(with_arrivals)
    else:
        own_terms()


def join(order, wide_own, down_own, *came):
    out = jax.ShapeDtypeStruct(((wide_own.size + down_own.size) // PIECE, PIECE), BF16)
    return pl.pallas_call(
        join_kernel,
        out_shape=out,
        in_specs=[SMEM] + [VMEM] * (2 + len(came)),
        compiler_params=SMALL,
        cost_estimate=cost(wide_own.size, (out,)),
    )(order, wide_own, down_own, *came)


def base_kernel(order_ref, wide_own, down_own, wide_one, down_one, two_ref, wide_out, down_out):
    owns, ones, outs = (wide_own, down_own), (wide_one, down_one), (wide_out, down_out)
    for number, rows, part in pieces(wide_own.shape, down_own.shape):
        came = ones[number][:, part].astype(F32) + two_ref[rows, :].astype(F32)
        came = jnp.where(order_ref[4] == 1, 0.0, came)
        outs[number][:, part] = owns[number][:, part].astype(F32) + came


def base_terms(order, wide_own, down_own, wide_one, down_one, two):
    outs = tuple(jax.ShapeDtypeStruct(a.shape, F32) for a in (wide_own, down_own))
    return pl.pallas_call(
        base_kernel,
        out_shape=outs,
        in_specs=[SMEM] + [VMEM] * 5,
        compiler_params=SMALL,
        cost_estimate=cost(wide_own.size, outs),
    )(order, wide_own, down_own, wide_one, down_one, two)


FINISH_STEPS = 4


def finish_kernel(wide_ref, down_ref, up_ref, low_ref, gate_hbm, up_hbm, down_hbm, gate, up, down, sems):
    parts = list(pieces(wide_ref.shape, down_ref.shape))
    copies = []

    def send(source, target):
        made = pltpu.make_async_copy(source, target, sems.at[len(copies)])
        made.start()
        copies.append(made)

    size = wide_ref.shape[0] // FINISH_STEPS
    hid = gate.shape[1]
    for step in range(FINISH_STEPS):
        here = slice(step * size, (step + 1) * size)
        for number, rows, part in parts:
            if number == 1:
                continue
            there = slice(rows.start + here.start, rows.start + here.stop)
            came = up_ref[there, :].astype(F32) + low_ref[there, :].astype(F32)
            total = wide_ref[here, part] + came
            for k, out in enumerate((gate, up)):
                first, last = max(part.start, k * hid), min(part.stop, (k + 1) * hid)
                if first < last:
                    out[here, first - k * hid : last - k * hid] = total[:, first - part.start : last - part.start]
        send(gate.at[pl.ds(step * size, size), :], gate_hbm.at[pl.ds(step * size, size), :])
        send(up.at[pl.ds(step * size, size), :], up_hbm.at[pl.ds(step * size, size), :])
    for number, rows, part in parts:
        if number == 1:
            came = up_ref[rows, :].astype(F32) + low_ref[rows, :].astype(F32)
            down[:, part] = down_ref[:, part] + came
    send(down, down_hbm)
    for made in copies:
        made.wait()


def finish(wide, down, one, two):
    rows, both = wide.shape
    shapes = ((rows, both // 2), (rows, both // 2), down.shape)
    outs = tuple(jax.ShapeDtypeStruct(s, F32) for s in shapes)
    return pl.pallas_call(
        finish_kernel,
        out_shape=outs,
        in_specs=[VMEM] * 4,
        out_specs=(pl.BlockSpec(memory_space=pl.ANY),) * 3,
        scratch_shapes=[pltpu.VMEM(s, F32) for s in shapes] + [pltpu.SemaphoreType.DMA((2 * FINISH_STEPS + 1,))],
        compiler_params=SMALL,
        cost_estimate=cost(wide.size, outs),
    )(wide, down, one, two)


def after(values, earlier):
    return lax.optimization_barrier((values, earlier))[0]


def pair_sums_kernel(places, *refs):
    for terms, out_ref in zip(places, refs[-2:]):
        each = out_ref.shape[0]
        values = [refs[k][block * each : (block + 1) * each, :].astype(F32) for k, block in terms]
        out_ref[...] = sum(values[1:], values[0]).astype(BF16)


def pair_sums(each, first, second):
    arrays = [a for a, _ in first + second]
    blocks = [block for _, block in first + second]
    numbered = tuple(enumerate(blocks))
    out = jax.ShapeDtypeStruct((each, arrays[0].shape[1]), BF16)
    return pl.pallas_call(
        functools.partial(pair_sums_kernel, (numbered[: len(first)], numbered[len(first) :])),
        out_shape=(out, out),
        in_specs=[VMEM] * len(arrays),
        out_specs=(VMEM, VMEM),
        compiler_params=SMALL,
        cost_estimate=cost(out.size, (out,)),
    )(*arrays)


LINE_ORDER = ((3, 2, 1, 0, 0), (0, 3, 2, 1, 1), (3, 0, 1, 2, 1), (0, 1, 2, 3, 0))


def per_device(tokens, expert_ids, gates, w_gate, w_up, w_down, cotangent):
    width = tokens.shape[1]
    group = lax.axis_size("expert")
    shards = lax.axis_size("dp")
    assert group == 8
    me = lax.axis_index("expert").astype(jnp.int32).reshape(1)
    z = lax.axis_index("dp")
    wg, wu, wd = w_gate[0], w_up[0], w_down[0]

    def flip(array, bit):
        return lax.ppermute(array, "expert", [(i, i ^ bit) for i in range(group)])

    line = shards == 4
    table = jnp.asarray(LINE_ORDER if line else ((0, 1, 2, 3, 0),), jnp.int32)
    order = table[z if line else 0]
    tokens = after(tokens, (order, me))
    cot_0 = cotangent
    tok_0 = packed(tokens, expert_ids, gates)
    tok_x, cot_y = flip(tok_0, NEAR), flip(cot_0, FAR)
    cot_x, tok_y = flip(cot_0, NEAR), flip(tok_0, FAR)
    cot_d, tok_d = flip(cot_y, NEAR), flip(tok_x, FAR)

    toks_a, cots_a = [tok_0, tok_x, tok_y], [cot_0, cot_x, cot_y]
    wide_panel, down_panel = panels(wg, wu, wd)
    cots_a += [flip(c, CORE) for c in [after(cot_0, wide_panel)] + cots_a[1:]]
    toks_a += [flip(t, CORE) for t in toks_a]
    act_a, hid_a, og_a = hidden(me, toks_a, cots_a, wide_panel, down_panel)
    (wide_part,) = wide_grads(order, toks_a, (hid_a,), width, 0, 1, kind=F32)
    tok_d, cot_d = after((tok_d, cot_d), wide_part)
    tok_e, cot_e = flip(tok_d, CORE), flip(cot_d, CORE)
    act_d, hid_d, og_d = hidden(me, [tok_d], [cot_d], wide_panel, down_panel)
    tok_e, cot_e = after((tok_e, cot_e), hid_d)
    act_e, hid_e, og_e = hidden(me, [tok_e], [cot_e], wide_panel, down_panel)

    def move(array, pairs):
        return lax.ppermute(array, "dp", pairs) if line else array

    one_pairs = [(0, 1), (1, 0), (2, 3), (3, 2)]
    two_pairs = [(0, 1), (1, 3), (3, 2), (2, 0)]
    end_pairs, mid_pairs = [(0, 1), (3, 2)], [(1, 2), (2, 1)]
    toks = toks_a + [tok_d, tok_e]
    wide_0 = wide_grads(order, [tok_d, tok_e], (hid_d, hid_e), width, 0, 1, start=(wide_part,))
    wide_one = move(wide_0[0], one_pairs)
    act_a = after(act_a, wide_0)
    down = down_grads(order, (act_a, act_d, act_e), (og_a, og_d, og_e))
    down_one = move(down[0], one_pairs)
    hid_a = after(hid_a, down)
    wide = wide_0 + wide_grads(order, toks, (hid_a, hid_d, hid_e), width, 1, 3)
    act_a = after(act_a, wide[1])
    there = tuple((0, i) for i in range(4)), tuple((1, i) for i in range(4))
    sent = rows_out(me, toks_a[3:] + [tok_e], (act_a, act_e), (hid_a, hid_e), 1, wide_panel, down_panel, (), there)
    if line:
        wide_one, down_one = after((wide_one, down_one), sent)
        second = join(order, wide[1], down[1], wide_one, down_one)
        two = move(second, two_pairs)
        sent = after(sent, second)
    sent = [flip(a, CORE) for a in sent]
    here = ((0, 0), (2, 0), (1, 0), (2, 1)), ((3, 0), (4, 0), (5, 0), (5, 1))
    kept = rows_out(me, toks_a[:3] + [tok_d], (act_a, act_d), (hid_a, hid_d), 0, wide_panel, down_panel, sent, here)
    out_0, out_y, out_near, grad_0, grad_x, grad_far = kept
    out_near, grad_far = flip(out_near, NEAR), flip(grad_far, FAR)
    hid_size = wd.shape[0]
    each = tokens.shape[0]
    if line:
        own_last = join(order, *after((wide[2], down[2]), kept))
        two = after(two, own_last)
        last = join(order, wide[2], down[2], two)
        last_mid, last_end = move(last, mid_pairs), move(own_last, end_pairs)
        out_near, grad_far = after((out_near, grad_far), last)
    out_y, grad_x = pair_sums(each, [(out_y, 0), (out_near, 1)], [(grad_x, 0), (grad_far, 1)])
    out_yy, grad_xx = flip(out_y, FAR), flip(grad_x, NEAR)
    if line:
        base = base_terms(order, wide[3], down[3], wide_one, down_one, after(two, (out_y, grad_x)))
    mixed, grad_tokens = pair_sums(
        each, [(out_0, 0), (out_near, 0), (out_yy, 0)], [(grad_0, 0), (grad_far, 0), (grad_xx, 0)]
    )
    if line:
        base, mixed, grad_tokens = lax.optimization_barrier((base, mixed, grad_tokens))
        last_end = after(last_end, (mixed, grad_tokens))
        last_mid = after(last_mid, last_end)
        grad_gate, grad_up, grad_down = finish(*base, last_mid, last_end)
    else:
        wide_all = jnp.concatenate(wide, axis=0)
        grad_wide = lax.psum_scatter(wide_all, "dp", scatter_dimension=0, tiled=True).astype(F32)
        grad_gate, grad_up = grad_wide[:, :hid_size], grad_wide[:, hid_size:]
        grad_down = lax.psum_scatter(jnp.concatenate(down, axis=0), "dp", scatter_dimension=0, tiled=True).astype(F32)
    return (mixed, grad_tokens, grad_gate[None], grad_up[None], grad_down[None])


def solution(mesh):
    return jax.shard_map(
        per_device,
        mesh=mesh,
        in_specs=(
            P(("dp", "expert"), None),
            P(("dp", "expert"), None),
            P(("dp", "expert"), None),
            P("expert", None, None),
            P("expert", None, None),
            P("expert", None, None),
            P(("dp", "expert"), None),
        ),
        out_specs=(
            P(("dp", "expert"), None),
            P(("dp", "expert"), None),
            P("expert", "dp", None),
            P("expert", "dp", None),
            P("expert", "dp", None),
        ),
        check_vma=False,
    )
```
